32 devices in a mesh: span: 8 (over z, x), ctx: 4 (over y, core).
Axes of the slice: x: 2, y: 2, z: 4, core: 2. Of those that a mesh axis runs over, the one named last changes fastest.
Arguments:
- queries: bfloat16 [4096, 3072], P(('span', 'ctx')), may hold values from -64 to 64
- keys: bfloat16 [4096, 512], P(('span', 'ctx')), may hold values from -16 to 16
- values: bfloat16 [4096, 512], P(('span', 'ctx')), may hold values from -6 to 6
- temps: float32 [8, 24], replicated, may hold values from 0.5 to 2
- levels: int32 [8], replicated, may hold values from 0 to 7
- ctx_list: int32 [8, 4], replicated, may hold values from -1 to 6, as said below
- counts: int32 [8], replicated, may hold values from 256 to 512
Outputs:
- attended: bfloat16 [4096, 3072], P(('span', 'ctx'))
The draws below stay inside these ranges and needn't reach their ends.
Inputs may be any that keep to these rules, and one draw needn't show every extreme that they name: `ctx_list`: slot 0 of span c's list is c - 1 (-1 for span 0). Slot 1, when used, is span 0. The other slots hold distinct spans below c - 1, used slots first, then -1. The list of span 8 - 1 has no -1.
All inputs are finite; a program needn't handle non-finite values.
Results may differ from the reference program's by a relative error of at most 0.0041.
Values may be sent and summed in bfloat16 or wider, within the bound.
No kernel may reach another device: no remote copies, remote signals or barrier semaphores. Data moves between devices by JAX's collectives and lax.ppermute only.
A program may use at most 128 MiB of HBM per device.

```python
import math
import jax
import jax.numpy as jnp
from jax import lax

HQ = 24
KVH = 4
HD = 128
CTXN = 4
LEVELS = 8
SPANS = 8
TOK_SPAN = 512
ROWS = 4096


def base_keys(key):
    raw = jax.random.normal(jax.random.fold_in(key, 11), (ROWS, KVH * HD), jnp.float32)
    return jnp.clip(raw, -6.0, 6.0)


def draw_keys(key, part):
    keys_now = base_keys(key)
    return keys_now.astype(jnp.bfloat16)


def draw_queries(key, part):
    raw = jax.random.normal(jax.random.fold_in(key, 12), (ROWS, HQ * HD), jnp.float32)
    queries_now = jnp.clip(raw, -6.0, 6.0)
    return queries_now.astype(jnp.bfloat16)


def draw_ctx_list(key, part):
    span_ids = jnp.arange(SPANS, dtype=jnp.int32)
    columns = jnp.arange(SPANS, dtype=jnp.int32)
    noise = jax.random.randint(jax.random.fold_in(key, 21), (SPANS, SPANS), 0, 1 << 16)
    boosted = noise + jnp.where(columns == 0, 1 << 17, 0)[None, :]
    scores = boosted * SPANS + columns[None, :]
    allowed = columns[None, :] < span_ids[:, None] - 1
    scores = jnp.where(allowed, scores, -1)
    picked, unused = lax.top_k(scores, CTXN - 1)
    taken = jax.random.randint(jax.random.fold_in(key, 22), (SPANS,), 0, CTXN)
    taken = jnp.where(span_ids == SPANS - 1, CTXN - 1, taken)
    slots = jnp.arange(CTXN - 1, dtype=jnp.int32)
    valid = (picked >= 0) & (slots[None, :] < taken[:, None])
    others = jnp.where(valid, picked % SPANS, -1)
    first = jnp.where(span_ids >= 1, span_ids - 1, -1)
    return jnp.concatenate([first[:, None], others], axis=1).astype(jnp.int32)


def draw_counts(key, part):
    drawn = jax.random.randint(jax.random.fold_in(key, 31), (SPANS,), TOK_SPAN // 2, TOK_SPAN + 1)
    span_ids = jnp.arange(SPANS, dtype=jnp.int32)
    drawn = jnp.where(span_ids == 0, TOK_SPAN, drawn)
    drawn = jnp.where(span_ids == 1, TOK_SPAN // 2, drawn)
    return drawn.astype(jnp.int32)


def set_ends(values, own_key, least, high):
    longest = values.shape.index(max(values.shape))
    spots = []
    for shift in (0, 1):
        where = [jax.random.randint(jax.random.fold_in(own_key, axis), (), 0, length) for axis, length in enumerate(values.shape)]
        where[longest] = (where[longest] + shift) % values.shape[longest]
        spots.append(tuple(where))
    return values.at[spots[0]].set(least).at[spots[1]].set(high)


def level_of(stream_key, shape, split, least, largest):
    def one(axis_at, parts):
        steps = jax.random.uniform(jax.random.fold_in(jax.random.fold_in(stream_key, 6), axis_at), (parts,), jnp.float32, least / len(split), largest / len(split))
        return jnp.repeat(jnp.exp(steps), shape[axis_at] // parts).reshape((-1,) + (1,) * (len(shape) - axis_at - 1))

    gain = one(*split[0])
    for cut in split[1:]:
        gain = gain * one(*cut)
    return gain


def bell_draw(stream_key, extent, width, limit, cuts=(), kind=jnp.bfloat16):
    values = jax.random.normal(stream_key, extent, jnp.float32) * width
    if len(cuts) > 0:
        values = level_of(stream_key, extent, cuts, -0.22, 0.18) * values
    return jnp.clip(values, min=-limit, max=limit).astype(kind)


def setup_inputs(seed: int = 0) -> dict:
    streams_of = jax.random.split(jax.random.key(seed), 8)
    queries = draw_queries(jax.random.fold_in(streams_of[7], 71), 0)
    keys = draw_keys(jax.random.fold_in(streams_of[7], 71), 0)
    values = bell_draw(streams_of[2], (ROWS, KVH * HD), 1.0, 6.0, ((0, 32),))
    temps = jnp.clip(jnp.exp(jax.random.uniform(streams_of[3], (LEVELS, HQ), jnp.float32, math.log(0.5), math.log(2.0))), 0.5, 2.0)
    levels = set_ends(jax.random.randint(streams_of[4], (SPANS,), 0, LEVELS), jax.random.fold_in(streams_of[4], 1), 0, LEVELS - 1).astype(jnp.int32)
    ctx_list = draw_ctx_list(jax.random.fold_in(streams_of[7], 71), 0)
    counts = draw_counts(jax.random.fold_in(streams_of[7], 71), 0)
    return {"queries": queries, "keys": keys, "values": values, "temps": temps, "levels": levels, "ctx_list": ctx_list, "counts": counts}


def reference(queries, keys, values, temps, levels, ctx_list, counts):
    group_size = HQ // KVH
    key_rows = keys.reshape(SPANS, TOK_SPAN, KVH * HD)
    value_rows = values.reshape(SPANS, TOK_SPAN, KVH * HD)
    query_rows = queries.reshape(SPANS, TOK_SPAN, HQ, HD)
    positions = jnp.arange(TOK_SPAN, dtype=jnp.int32)

    def one_span(span_id):
        span_ids = jnp.concatenate([span_id[None], ctx_list[span_id]]).astype(jnp.int32)
        safe_ids = jnp.maximum(span_ids, 0)
        mask = (span_ids[:, None] >= 0) & (positions[None, :] < counts[safe_ids][:, None])
        mask = mask.reshape(-1)
        all_keys = key_rows[safe_ids].reshape(-1, KVH * HD).astype(jnp.float32)
        all_values = value_rows[safe_ids].reshape(-1, KVH * HD).astype(jnp.float32)
        query_here = query_rows[span_id].astype(jnp.float32)
        scale = temps[levels[span_id]] / math.sqrt(HD)
        pieces = []
        for kv_head in range(KVH):
            lower = kv_head * group_size
            query_group = query_here[:, lower:lower + group_size]
            key_group = all_keys[:, kv_head * HD:(kv_head + 1) * HD]
            value_group = all_values[:, kv_head * HD:(kv_head + 1) * HD]
            scores = jnp.einsum('tgd,kd->gtk', query_group, key_group) * scale[lower:lower + group_size][:, None, None]
            scores = jnp.where(mask[None, None, :], scores, -1e+30)
            highest = lax.optimization_barrier(jnp.max(scores, axis=-1, keepdims=True))
            weights = jnp.where(mask[None, None, :], jnp.exp(scores - highest), 0.0)
            totals = lax.optimization_barrier(jnp.sum(weights, axis=-1))
            rounded = lax.optimization_barrier(weights.astype(jnp.bfloat16)).astype(jnp.float32)
            summed = jnp.einsum('gtk,kd->tgd', rounded, value_group)
            pieces.append(summed / jnp.transpose(totals)[:, :, None])
        joined = jnp.concatenate(pieces, axis=1)
        return joined.reshape(TOK_SPAN, HQ * HD).astype(jnp.bfloat16)
    result = lax.map(one_span, jnp.arange(SPANS, dtype=jnp.int32))
    return result.reshape(ROWS, HQ * HD)
```

```python
import functools
import math

import jax
import jax.numpy as jnp
from jax import lax
from jax.experimental import pallas as pl
from jax.experimental.pallas import tpu as pltpu
from jax.sharding import PartitionSpec as P

HQ = 24
KVH = 4
HD = 128
GROUP = HQ // KVH
LOW = -1e30


def attend_kernel(slots, pieces, valid_ref, first_ref, scale_ref, q_ref, *refs):
    kv_refs, out_ref = refs[:-1], refs[-1]
    rows = q_ref.shape[0]
    piece_rows = kv_refs[0].shape[0]
    row_ids = lax.broadcasted_iota(jnp.int32, (piece_rows, HD), 0)
    in_own = first_ref[0] == 0
    for g in range(KVH):
        keys_at = slice(g * HD, (g + 1) * HD)
        values_at = slice((KVH + g) * HD, (KVH + g + 1) * HD)
        heads = [g * GROUP + i for i in range(GROUP)]
        q = jnp.concatenate([q_ref[:, h * HD : (h + 1) * HD] for h in heads], axis=0)
        scale = jnp.concatenate([jnp.full((rows, 1), scale_ref[h], jnp.float32) for h in heads], axis=0)
        spare = jnp.where(
            in_own,
            kv_refs[0][0:1, keys_at].astype(jnp.float32),
            kv_refs[2][0:1, keys_at].astype(jnp.float32),
        )
        top = None
        for j in range(slots):
            ks, vs = [], []
            for i in range(pieces):
                at = j * pieces + i
                keep = row_ids < valid_ref[at]
                k = kv_refs[at][:, keys_at].astype(jnp.float32)
                v = kv_refs[at][:, values_at].astype(jnp.float32)
                ks.append(jnp.where(keep, k, spare).astype(jnp.bfloat16))
                ones = jnp.where(keep, 1.0, 0.0).astype(jnp.bfloat16)
                vs.append(jnp.concatenate([jnp.where(keep, v, 0.0).astype(jnp.bfloat16), ones], axis=1))
            k = jnp.concatenate(ks, axis=0)
            v = jnp.concatenate(vs, axis=0)
            s = lax.dot_general(q, k, (((1,), (1,)), ((), ())), preferred_element_type=jnp.float32)
            s = s * scale
            slot_top = jnp.max(s, axis=1, keepdims=True)
            if top is None:
                top = slot_top
                weight = jnp.exp2(s - top).astype(jnp.bfloat16)
                sums = jnp.dot(weight, v, preferred_element_type=jnp.float32)
            else:
                new_top = jnp.maximum(top, slot_top)
                weight = jnp.exp2(s - new_top).astype(jnp.bfloat16)
                sums = sums * jnp.exp2(top - new_top) + jnp.dot(weight, v, preferred_element_type=jnp.float32)
                top = new_top
        result = (sums[:, :HD] / sums[:, HD:]).astype(jnp.bfloat16)
        for i, h in enumerate(heads):
            out_ref[:, h * HD : (h + 1) * HD] = result[i * rows : (i + 1) * rows]


def attend(q, kv, valid, first, scale, slots, pieces):
    keys = slots * pieces * kv[0].shape[0]
    smem = pl.BlockSpec(memory_space=pltpu.SMEM)
    vmem = pl.BlockSpec(memory_space=pltpu.VMEM)
    return pl.pallas_call(
        functools.partial(attend_kernel, slots, pieces),
        out_shape=jax.ShapeDtypeStruct(q.shape, jnp.bfloat16),
        in_specs=[smem] * 3 + [vmem] * (1 + len(kv)),
        out_specs=vmem,
        compiler_params=pltpu.CompilerParams(vmem_limit_bytes=48 << 20),
        cost_estimate=pl.CostEstimate(
            flops=4 * q.shape[0] * keys * HQ * HD,
            bytes_accessed=4 * q.size + 2 * len(kv) * kv[0].size,
            transcendentals=q.shape[0] * HQ * keys,
        ),
    )(valid, first, scale, q, *kv)


def per_device(spans, ctx, queries, keys, values, temps, levels, ctx_list, counts):
    me = lax.axis_index("span")
    tok = lax.axis_index("ctx")
    rows = keys.shape[0]
    kv = jnp.concatenate([keys, values], axis=1)
    up = [(s, s + 2) for s in range(spans - 2)]
    across = [(s, s ^ 1) for s in range(spans)]
    other_chip = [(t, t ^ 2) for t in range(ctx)]
    other_core = [(t, t ^ 1) for t in range(ctx)]

    wanted = lax.dynamic_index_in_dim(ctx_list, me, 0, keepdims=False)
    straight, crossed = [kv], [lax.ppermute(kv, "span", across)]
    for step in range(1, spans // 2):
        straight.append(lax.ppermute(straight[-1], "span", up))
        crossed.append(lax.ppermute(straight[-1], "span", across))

    def pick(source):
        same = ((source ^ me) & 1) == 0
        back = jnp.where(same, me, me ^ 1) - source
        at = jnp.clip(back // 2, 0, spans // 2 - 1) + jnp.where(same, 0, spans // 2)
        return select(at, straight + crossed)

    def select(at, slabs):
        result = slabs[0]
        for i in range(1, len(slabs)):
            result = jnp.where(at == i, slabs[i], result)
        return result

    def spread(slab):
        far = lax.ppermute(slab, "ctx", other_chip)
        near = lax.ppermute(slab, "ctx", other_core)
        both = lax.ppermute(far, "ctx", other_core)
        return [slab, near, far, both]

    pieces = spread(kv)
    for j in range(wanted.shape[0]):
        pieces += spread(pick(jnp.maximum(wanted[j], 0)))

    ids = jnp.concatenate([me[None], wanted])
    lengths = jnp.where(ids >= 0, counts[jnp.maximum(ids, 0)], 0)
    starts = rows * (tok ^ jnp.arange(ctx, dtype=jnp.int32))
    valid = jnp.clip(lengths[:, None] - starts[None, :], 0, rows).reshape(-1).astype(jnp.int32)
    scale = temps[levels[me]] * (math.log2(math.e) / math.sqrt(HD))
    first = (tok & 2).reshape(1).astype(jnp.int32)
    return attend(queries, pieces, valid, first, scale, ids.shape[0], ctx)


def solution(mesh):
    return jax.shard_map(
        functools.partial(per_device, mesh.shape["span"], mesh.shape["ctx"]),
        mesh=mesh,
        in_specs=(
            P(("span", "ctx"), None),
            P(("span", "ctx"), None),
            P(("span", "ctx"), None),
            P(),
            P(),
            P(),
            P(),
        ),
        out_specs=P(("span", "ctx"), None),
        check_vma=False,
    )
```

```python
import functools
import math

import jax
import jax.numpy as jnp
from jax import lax
from jax.experimental import pallas as pl
from jax.experimental.pallas import tpu as pltpu
from jax.sharding import PartitionSpec as P

HQ = 24
KVH = 4
HD = 128
GROUP = HQ // KVH
WIDE = GROUP * HD
SCALE = math.log2(math.e) / math.sqrt(HD)
SMEM = pl.BlockSpec(memory_space=pltpu.SMEM)
VMEM = pl.BlockSpec(memory_space=pltpu.VMEM)
PARAMS = pltpu.CompilerParams(vmem_limit_bytes=48 << 20)


def head_of(where_ref):
    return 2 * (where_ref[0] & 1) + (where_ref[1] >> 1)


def span_of(where_ref):
    return (where_ref[0] & -2) + (where_ref[1] & 1)


def cut_kernel(where_ref, *refs):
    sources, pieces = refs[: len(refs) - KVH], refs[len(refs) - KVH :]
    for j, piece in enumerate(pieces):
        head = where_ref[1] ^ j
        at = 0
        for source in sources:
            width = source.shape[1] // KVH
            piece[:, at : at + width] = source[:, pl.ds(pl.multiple_of(head * width, HD), width)]
            at += width


def cut(where, *sources):
    rows = sources[0].shape[0]
    width = sum(source.shape[1] for source in sources) // KVH
    return pl.pallas_call(
        cut_kernel,
        out_shape=[jax.ShapeDtypeStruct((rows, width), jnp.bfloat16)] * KVH,
        in_specs=[SMEM] + [VMEM] * len(sources),
        out_specs=[VMEM] * KVH,
        compiler_params=PARAMS,
    )(where, *sources)


def slab_kernel(where_ref, counts_ref, *refs):
    pieces, key_ref, value_ref = refs[:-2], refs[-2], refs[-1]
    rows = pieces[0].shape[0]
    head = head_of(where_ref)
    count = counts_ref[span_of(where_ref)]
    for j, piece in enumerate(pieces):
        at = pl.ds(pl.multiple_of((head ^ j) * rows, rows), rows)
        key_ref[at, :] = piece[:, :HD]
        value_ref[at, :] = piece[:, HD:]
    spare = key_ref[0:16, :][0:1].astype(jnp.float32)
    for block in range(2, len(pieces)):
        at = slice(block * rows, (block + 1) * rows)
        keep = lax.broadcasted_iota(jnp.int32, (rows, HD), 0) + block * rows < count
        key_ref[at, :] = jnp.where(keep, key_ref[at, :].astype(jnp.float32), spare).astype(jnp.bfloat16)
        value_ref[at, :] = jnp.where(keep, value_ref[at, :].astype(jnp.float32), 0.0).astype(jnp.bfloat16)


def slab_of(where, counts, pieces):
    tokens = len(pieces) * pieces[0].shape[0]
    return pl.pallas_call(
        slab_kernel,
        out_shape=[jax.ShapeDtypeStruct((tokens, HD), jnp.bfloat16)] * 2,
        in_specs=[SMEM] * 2 + [VMEM] * len(pieces),
        out_specs=[VMEM] * 2,
        compiler_params=PARAMS,
    )(where, counts, *pieces)


def join_kernel(where_ref, *refs):
    pieces, out_ref = refs[:-1], refs[-1]
    for j, piece in enumerate(pieces):
        head = where_ref[1] ^ j
        out_ref[:, pl.ds(pl.multiple_of(head * WIDE, HD), WIDE)] = piece[...]


def join(where, pieces):
    return pl.pallas_call(
        join_kernel,
        out_shape=jax.ShapeDtypeStruct((pieces[0].shape[0], HQ * HD), jnp.bfloat16),
        in_specs=[SMEM] + [VMEM] * len(pieces),
        out_specs=VMEM,
        compiler_params=PARAMS,
    )(where, *pieces)


def attend_kernel(backs, first, final, blocks, where_ref, levels_ref, temps_ref, list_ref, counts_ref, q_ref, *refs):
    refs = list(refs)
    if not first:
        sums_in, stats_in = refs.pop(0), refs.pop(0)
    slabs = [(refs.pop(0), refs.pop(0)) for _ in backs]
    if final:
        out_ref = refs.pop(0)
    else:
        sums_out, stats_out = refs.pop(0), refs.pop(0)
    sums_ref, top_ref = refs
    rows = q_ref.shape[1]
    head = head_of(where_ref)
    span = span_of(where_ref)
    level = levels_ref[span]
    factors = [temps_ref[level, head * GROUP + i] * SCALE for i in range(GROUP)]

    def visit(key_ref, value_ref, count, width, fresh):
        ones = (lax.broadcasted_iota(jnp.int32, (width, HD), 0) < count).astype(jnp.float32).astype(jnp.bfloat16)
        keys = key_ref[:width, :]
        values = jnp.concatenate([value_ref[:width, :], ones], axis=1)
        for b in range(blocks):
            q = jnp.concatenate([q_ref[b, :, i * HD : (i + 1) * HD] for i in range(GROUP)], axis=0)
            scale = jnp.concatenate([jnp.full((rows, 1), f, jnp.float32) for f in factors], axis=0)
            s = lax.dot_general(q, keys, (((1,), (1,)), ((), ())), preferred_element_type=jnp.float32)
            s = s * scale
            top = jnp.max(s, axis=1, keepdims=True)
            if not fresh:
                old_top = top_ref[b, :, 0:1]
                top = jnp.maximum(top, old_top)
            weight = jnp.exp2(s - top).astype(jnp.bfloat16)
            sums = jnp.dot(weight, values, preferred_element_type=jnp.float32)
            if not fresh:
                sums = sums + sums_ref[b] * jnp.exp2(old_top - top)
            sums_ref[b] = sums
            top_ref[b] = jnp.broadcast_to(top, (GROUP * rows, HD))

    def visit_any(slab, count, fresh):
        tokens = slab[0].shape[0]
        rung = tokens // 4
        widths = [2 * rung, 3 * rung, 4 * rung]
        for low, width in zip([0] + widths, widths):
            pl.when((count > low) & (count <= width))(functools.partial(visit, *slab, count, width, fresh))

    def wanted(ident):
        found = list_ref[span, 0] == ident
        for j in range(1, list_ref.shape[1]):
            found = found | (list_ref[span, j] == ident)
        return jnp.where(found & (ident >= 0), counts_ref[jnp.maximum(ident, 0)], 0)

    if not first:
        for b in range(blocks):
            sums_ref[b, :, :HD] = sums_in[b]
            sums_ref[b, :, HD:] = jnp.broadcast_to(stats_in[b, :, HD // 2 : HD // 2 + 1], (GROUP * rows, HD))
            top_ref[b] = jnp.broadcast_to(stats_in[b, :, 0:1], (GROUP * rows, HD))
    for slab, (parity, back) in zip(slabs, backs):
        if parity == 0 and back == 0:
            visit_any(slab, counts_ref[span], True)
        else:
            visit_any(slab, wanted((span ^ parity) - 2 * back), False)
    lane = lax.broadcasted_iota(jnp.int32, (GROUP * rows, HD), 1)
    for b in range(blocks):
        if final:
            result = (sums_ref[b, :, :HD] / sums_ref[b, :, HD:]).astype(jnp.bfloat16)
            for i in range(GROUP):
                out_ref[b, :, i * HD : (i + 1) * HD] = result[i * rows : (i + 1) * rows]
        else:
            sums_out[b] = sums_ref[b, :, :HD]
            stats_out[b] = jnp.where(lane < HD // 2, top_ref[b], sums_ref[b, :, HD:])


def attend(scalars, q, state, slabs, backs, final, begin, count):
    blocks = 2
    steps = count // blocks
    parts, rows, _ = q.shape
    tall = GROUP * rows
    at = begin // blocks
    state_spec = pl.BlockSpec((blocks, tall, HD), lambda i: (i + at, 0, 0))
    q_spec = pl.BlockSpec((blocks, rows, WIDE), lambda i: (i + at, 0, 0))
    whole = [pl.BlockSpec(k.shape, lambda i: (0, 0)) for k, _ in slabs for _ in range(2)]
    if final:
        out_shape = jax.ShapeDtypeStruct((count, rows, WIDE), jnp.bfloat16)
        out_specs = pl.BlockSpec((blocks, rows, WIDE), lambda i: (i, 0, 0))
    else:
        out_shape = [jax.ShapeDtypeStruct((parts, tall, HD), jnp.float32)] * 2
        out_specs = [state_spec] * 2
    keys = sum(k.shape[0] for k, _ in slabs)
    return pl.pallas_call(
        functools.partial(attend_kernel, backs, state is None, final, blocks),
        grid=(steps,),
        out_shape=out_shape,
        in_specs=[SMEM] * 5 + [q_spec] + ([] if state is None else [state_spec] * 2) + whole,
        out_specs=out_specs,
        scratch_shapes=[
            pltpu.VMEM((blocks, tall, 2 * HD), jnp.float32),
            pltpu.VMEM((blocks, tall, HD), jnp.float32),
        ],
        compiler_params=PARAMS,
        cost_estimate=pl.CostEstimate(
            flops=4 * count * tall * keys * HD,
            bytes_accessed=2 * q.size + 4 * keys * HD,
            transcendentals=count * tall * keys,
        ),
    )(*scalars, q, *(state or ()), *[a for slab in slabs for a in slab])


def per_device(spans, ctx, queries, keys, values, temps, levels, ctx_list, counts):
    where = jnp.stack([lax.axis_index("span"), lax.axis_index("ctx")]).astype(jnp.int32)
    scalars = (where, levels, temps, ctx_list, counts)
    out_of = []
    for j in range(KVH):
        pairs = []
        for s in range(spans):
            for t in range(ctx):
                chip = t ^ j
                target = ((s & -2) + (chip >> 1), 2 * (chip & 1) + (s & 1))
                pairs.append((s * ctx + t, target[0] * ctx + target[1]))
        out_of.append(pairs)
    back_of = [[(b, a) for a, b in pairs] for pairs in out_of]
    plane = ("span", "ctx")
    up = [(s, s + 2) for s in range(spans - 2)]
    other_core = [(t, t ^ 1) for t in range(ctx)]

    kv_pieces = [lax.ppermute(p, plane, pairs) for p, pairs in zip(cut(where, keys, values), out_of)]
    own = slab_of(where, counts, kv_pieces)
    q_pieces = [lax.ppermute(p, plane, pairs) for p, pairs in zip(cut(where, queries), out_of)]
    q = jnp.stack(q_pieces)

    slabs = {(0, 0): tuple(own)}
    for k in range(spans // 2):
        if k:
            slabs[0, k] = tuple(lax.ppermute(a, "span", up) for a in slabs[0, k - 1])
        slabs[1, k] = tuple(lax.ppermute(a, "ctx", other_core) for a in slabs[0, k])

    last = spans // 2 - 1
    stages = [[(0, 0), (0, 1), (1, 0)]] + [[(0, k), (1, k - 1)] for k in range(2, last)]
    stages.append([(0, last), (1, last - 1), (1, last)])
    state = None
    for stage in stages[:-1]:
        state = attend(scalars, q, state, [slabs[b] for b in stage], stage, False, 0, KVH)
    result = []
    for begin in range(0, KVH, 2):
        part = attend(scalars, q, state, [slabs[b] for b in stages[-1]], stages[-1], True, begin, 2)
        for i in range(2):
            result.append(lax.ppermute(part[i], plane, back_of[begin + i]))
    return join(where, result)


def solution(mesh):
    return jax.shard_map(
        functools.partial(per_device, mesh.shape["span"], mesh.shape["ctx"]),
        mesh=mesh,
        in_specs=(
            P(("span", "ctx"), None),
            P(("span", "ctx"), None),
            P(("span", "ctx"), None),
            P(),
            P(),
            P(),
            P(),
        ),
        out_specs=P(("span", "ctx"), None),
        check_vma=False,
    )
```

```python
import functools
import math

import jax
import jax.numpy as jnp
from jax import lax
from jax.experimental import pallas as pl
from jax.experimental.pallas import tpu as pltpu
from jax.sharding import PartitionSpec as P

HQ = 24
KVH = 4
HD = 128
GROUP = HQ // KVH
WIDE = GROUP * HD
SCALE = math.log2(math.e) / math.sqrt(HD)
SMEM = pl.BlockSpec(memory_space=pltpu.SMEM)
ANY = pl.BlockSpec(memory_space=pl.ANY)
PARAMS = pltpu.CompilerParams(vmem_limit_bytes=40 << 20)


def plan_kernel(ready, where_ref, list_ref, counts_ref, pick_ref, count_ref):
    span = where_ref[0]
    slots = []
    for j in range(list_ref.shape[1]):
        ident = list_ref[span, j]
        other = (ident ^ span) & 1
        back = ((span ^ other) - ident) >> 1
        slots.append([ident, 2 * back + other, back + 1 + other, ident < 0])
    count_ref[0] = counts_ref[span]
    for lane, turn in enumerate(ready):
        free = jnp.bool_(True)
        pick = jnp.int32(0)
        count = jnp.int32(0)
        for slot in slots:
            ident, number, at, done = slot
            take = free & (at <= turn) & jnp.logical_not(done)
            pick = jnp.where(take, number, pick)
            count = jnp.where(take, counts_ref[jnp.maximum(ident, 0)], count)
            slot[3] = done | take
            free = free & jnp.logical_not(take)
        pick_ref[lane] = pick
        count_ref[lane + 1] = count


def plan(where, ctx_list, counts, ready):
    return pl.pallas_call(
        functools.partial(plan_kernel, ready),
        out_shape=[
            jax.ShapeDtypeStruct((len(ready),), jnp.int32),
            jax.ShapeDtypeStruct((len(ready) + 1,), jnp.int32),
        ],
        in_specs=[SMEM] * 3,
        out_specs=[SMEM] * 2,
    )(where, ctx_list, counts)


def pick_kernel(lane, numbers, pick_ref, *refs):
    slabs, out_ref, sem = refs[:-2], refs[-2], refs[-1]
    wanted = pick_ref[lane]
    known = functools.reduce(jnp.logical_or, [wanted == n for n in numbers[1:]], jnp.bool_(False))
    for i, (number, slab) in enumerate(zip(numbers, slabs)):

        @pl.when(jnp.logical_not(known) if i == 0 else wanted == number)
        def _():
            copy = pltpu.make_async_copy(slab, out_ref, sem)
            copy.start()
            copy.wait()


def pick_slab(picks, lane, slabs):
    numbers = sorted(slabs)
    return pl.pallas_call(
        functools.partial(pick_kernel, lane, numbers),
        out_shape=jax.ShapeDtypeStruct(slabs[numbers[0]].shape, jnp.bfloat16),
        in_specs=[SMEM] + [ANY] * len(numbers),
        out_specs=ANY,
        scratch_shapes=[pltpu.SemaphoreType.DMA],
    )(picks, *[slabs[n] for n in numbers])


def attend_kernel(lanes, first, final, where_ref, levels_ref, temps_ref, count_ref, q_ref, *refs):
    refs = list(refs)
    state_in = None if first else (refs.pop(0), refs.pop(0))
    pieces = [[(refs.pop(0), refs.pop(0)) for _ in range(KVH)] for _ in lanes]
    outs = [refs.pop(0)] if final else [refs.pop(0), refs.pop(0)]
    sums_ref, top_ref = refs
    rows = q_ref.shape[0]
    tall = GROUP * rows
    tok = where_ref[1]
    level = levels_ref[where_ref[0]]
    head = pl.program_id(0) * GROUP
    factors = [temps_ref[level, head + i] * SCALE for i in range(GROUP)]
    row_ids = lax.broadcasted_iota(jnp.int32, (rows, HD), 0)

    def visit(lane, count, fresh):
        lane = pieces[lane]
        low = tok < 2
        spare = jnp.where(low, lane[0][0][0:16].astype(jnp.float32), lane[2][0][0:16].astype(jnp.float32))[0:1]
        ks, vs = [], []
        for i, (k_ref, v_ref) in enumerate(lane):
            keep = row_ids < count - rows * (tok ^ i)
            ks.append(jnp.where(keep, k_ref[...].astype(jnp.float32), spare).astype(jnp.bfloat16))
            v = jnp.where(keep, v_ref[...].astype(jnp.float32), 0.0).astype(jnp.bfloat16)
            vs.append(jnp.concatenate([v, jnp.where(keep, 1.0, 0.0).astype(jnp.bfloat16)], axis=1))
        k = jnp.concatenate(ks, axis=0)
        v = jnp.concatenate(vs, axis=0)
        q = jnp.concatenate([q_ref[:, i * HD : (i + 1) * HD] for i in range(GROUP)], axis=0)
        scale = jnp.concatenate([jnp.full((rows, 1), f, jnp.float32) for f in factors], axis=0)
        s = lax.dot_general(q, k, (((1,), (1,)), ((), ())), preferred_element_type=jnp.float32)
        s = s * scale
        top = jnp.max(s, axis=1, keepdims=True)
        if not fresh:
            old_top = top_ref[:, 0:1]
            top = jnp.maximum(top, old_top)
        weight = jnp.exp2(s - top).astype(jnp.bfloat16)
        sums = jnp.dot(weight, v, preferred_element_type=jnp.float32)
        if not fresh:
            sums = sums + sums_ref[...] * jnp.exp2(old_top - top)
        sums_ref[...] = sums
        top_ref[...] = jnp.broadcast_to(top, (tall, HD))

    if not first:
        sums_in, stats_in = state_in
        sums_ref[:, :HD] = sums_in[0]
        sums_ref[:, HD:] = jnp.broadcast_to(stats_in[0, :, HD // 2 : HD // 2 + 1], (tall, HD))
        top_ref[...] = jnp.broadcast_to(stats_in[0, :, 0:1], (tall, HD))
    for i, lane in enumerate(lanes):
        count = count_ref[lane]
        if lane == 0:
            visit(i, count, True)
        else:
            pl.when(count > 0)(functools.partial(visit, i, count, False))
    if final:
        result = (sums_ref[:, :HD] / sums_ref[:, HD:]).astype(jnp.bfloat16)
        for i in range(GROUP):
            outs[0][:, i * HD : (i + 1) * HD] = result[i * rows : (i + 1) * rows]
    else:
        lane_ids = lax.broadcasted_iota(jnp.int32, (tall, HD), 1)
        outs[0][0] = sums_ref[:, :HD]
        outs[1][0] = jnp.where(lane_ids < HD // 2, top_ref[...], sums_ref[:, HD:])


def attend(scalars, q, state, pieces, lanes, final):
    rows = q.shape[0]
    tall = GROUP * rows
    state_spec = pl.BlockSpec((1, tall, HD), lambda g: (g, 0, 0))
    q_spec = pl.BlockSpec((rows, WIDE), lambda g: (0, g))
    piece_specs = [pl.BlockSpec((rows, HD), lambda g: (0, g)), pl.BlockSpec((rows, HD), lambda g: (0, g + KVH))]
    flat = [p for lane in lanes for p in pieces[lane]]
    if final:
        out_shape = jax.ShapeDtypeStruct(q.shape, jnp.bfloat16)
        out_specs = q_spec
    else:
        out_shape = [jax.ShapeDtypeStruct((KVH, tall, HD), jnp.float32)] * 2
        out_specs = [state_spec] * 2
    keys = len(flat) * rows
    return pl.pallas_call(
        functools.partial(attend_kernel, lanes, state is None, final),
        grid=(KVH,),
        out_shape=out_shape,
        in_specs=[SMEM] * 4 + [q_spec] + ([] if state is None else [state_spec] * 2) + piece_specs * len(flat),
        out_specs=out_specs,
        scratch_shapes=[pltpu.VMEM((tall, 2 * HD), jnp.float32), pltpu.VMEM((tall, HD), jnp.float32)],
        compiler_params=PARAMS,
        cost_estimate=pl.CostEstimate(
            flops=4 * KVH * tall * keys * HD,
            bytes_accessed=2 * q.size + 4 * keys * KVH * HD,
            transcendentals=KVH * tall * keys,
        ),
    )(*scalars, q, *(state or ()), *[p for piece in flat for p in (piece, piece)])


def per_device(spans, ctx, queries, keys, values, temps, levels, ctx_list, counts):
    where = jnp.stack([lax.axis_index("span"), lax.axis_index("ctx")]).astype(jnp.int32)
    turns = spans // 2
    ready = list(range(2, turns + 1)) + [turns, turns + 1]
    picks, lane_counts = plan(where, ctx_list, counts, ready)
    kv = jnp.concatenate([keys, values], axis=1)
    up = [(s, (s + 2) % spans) for s in range(spans)]
    across = [(s, s ^ 1) for s in range(spans)]
    other_chip = [(t, t ^ 2) for t in range(ctx)]
    other_core = [(t, t ^ 1) for t in range(ctx)]

    def near(slab):
        return lax.ppermute(slab, "ctx", other_core)

    slabs = {0: kv}
    lanes = []
    for turn in range(1, turns + 2):
        held = dict(slabs)
        if turn < turns:
            slabs[2 * turn] = lax.ppermute(held[2 * turn - 2], "span", up)
        if turn <= turns:
            slabs[2 * turn - 1] = lax.ppermute(held[2 * turn - 2], "span", across)
        for lane in lanes:
            if len(lane) == 3:
                lane.append(near(lane[2]))
        if turn == 1:
            leave = [kv]
        else:
            leave = [pick_slab(picks, i, held) for i, at in enumerate(ready) if at == turn]
        for slab in leave:
            lanes.append([slab, near(slab), lax.ppermute(slab, "ctx", other_chip)])
        if turn <= turns:
            slabs, lanes = lax.optimization_barrier((slabs, lanes))
    for lane in lanes:
        if len(lane) == 3:
            lane.append(near(lane[2]))

    scalars = (where, levels, temps, lane_counts)
    total = len(lanes)
    stages = [list(range(total - 3)), [total - 3, total - 2], [total - 1]]
    state = None
    for stage in stages[:-1]:
        state = attend(scalars, queries, state, lanes, stage, False)
    return attend(scalars, queries, state, lanes, stages[-1], True)


def solution(mesh):
    return jax.shard_map(
        functools.partial(per_device, mesh.shape["span"], mesh.shape["ctx"]),
        mesh=mesh,
        in_specs=(
            P(("span", "ctx"), None),
            P(("span", "ctx"), None),
            P(("span", "ctx"), None),
            P(),
            P(),
            P(),
            P(),
        ),
        out_specs=P(("span", "ctx"), None),
        check_vma=False,
    )
```

```python
import functools
import math

import jax
import jax.numpy as jnp
from jax import lax
from jax.experimental import pallas as pl
from jax.experimental.pallas import tpu as pltpu
from jax.sharding import PartitionSpec as P

HQ = 24
KVH = 4
HD = 128
GROUP = HQ // KVH
WIDE = GROUP * HD
LOW = -1e30
SCALE = math.log2(math.e) / math.sqrt(HD)
SMEM = pl.BlockSpec(memory_space=pltpu.SMEM)
VMEM = pl.BlockSpec(memory_space=pltpu.VMEM)
PARAMS = pltpu.CompilerParams(vmem_limit_bytes=32 << 20)


def attend_kernel(backs, first, final, where_ref, levels_ref, temps_ref, list_ref, counts_ref, q_ref, *refs):
    refs = list(refs)
    state_in = None if first else (refs.pop(0), refs.pop(0))
    slabs = [(refs.pop(0), refs.pop(0)) for _ in backs]
    if final:
        out_ref, key_ref, value_ref, sums_ref, top_ref = refs
    else:
        sums_ref, top_ref, key_ref, value_ref = refs
    base = where_ref[0] & -2
    core = where_ref[1] & 1
    head = 2 * (where_ref[0] & 1) + (where_ref[1] >> 1)
    rows = q_ref.shape[0] // 4
    tall = GROUP * rows
    half = slabs[0][0].shape[0] // 2
    part = half // 4

    if first:
        sums_ref[...] = jnp.zeros_like(sums_ref)
        top_ref[...] = jnp.full_like(top_ref, LOW)
    elif final:
        sums_ref[...] = state_in[0][...]
        top_ref[...] = state_in[1][...]

    def wanted(span, ident):
        found = span == ident
        for j in range(list_ref.shape[1]):
            found = found | (list_ref[span, j] == ident)
        return found & (ident >= 0)

    index = lax.broadcasted_iota(jnp.int32, (half, HD), 0)
    for slab, back in zip(slabs, backs):
        for x in range(2):
            count = counts_ref[jnp.maximum(base + x - 2 * back, 0)]
            mine = slab[0]
            spare = mine[x * half : x * half + 16, :HD].astype(jnp.float32)[0:1]
            for side, ref in enumerate(slab):
                token = (index // part) * (2 * part) + (core ^ side) * part + index % part
                keep = token < count
                at = slice(x * half, (x + 1) * half)
                to = slice(side * half, (side + 1) * half)
                keys = jnp.where(keep, ref[at, :HD].astype(jnp.float32), spare)
                values = jnp.where(keep, ref[at, HD:].astype(jnp.float32), 0.0)
                key_ref[x, to, :] = keys.astype(jnp.bfloat16)
                value_ref[x, to, :HD] = values.astype(jnp.bfloat16)
                value_ref[x, to, HD:] = jnp.where(keep, 1.0, 0.0).astype(jnp.bfloat16)

        @pl.loop(0, 4)
        def _(turn):
            side = turn >> 1
            x = turn & 1
            span = base + side

            @pl.when(wanted(span, base + x - 2 * back))
            def _():
                level = levels_ref[span]
                keys = key_ref[x]
                values = value_ref[x]
                scale = jnp.concatenate(
                    [jnp.full((rows, 1), temps_ref[level, head * GROUP + i] * SCALE, jnp.float32) for i in range(GROUP)],
                    axis=0,
                )
                for b in range(2):
                    block = 2 * side + b
                    q_rows = q_ref[pl.ds(pl.multiple_of(block * rows, rows), rows), :]
                    q = jnp.concatenate([q_rows[:, i * HD : (i + 1) * HD] for i in range(GROUP)], axis=0)
                    s = lax.dot_general(q, keys, (((1,), (1,)), ((), ())), preferred_element_type=jnp.float32)
                    s = s * scale
                    old_top = top_ref[block, :, 0:1]
                    top = jnp.maximum(jnp.max(s, axis=1, keepdims=True), old_top)
                    weight = jnp.exp2(s - top).astype(jnp.bfloat16)
                    sums = jnp.dot(weight, values, preferred_element_type=jnp.float32)
                    sums_ref[block] = sums + sums_ref[block] * jnp.exp2(old_top - top)
                    top_ref[block] = jnp.broadcast_to(top, (tall, HD))

    if final:
        for block in range(4):
            result = (sums_ref[block, :, :HD] / sums_ref[block, :, HD:]).astype(jnp.bfloat16)
            for i in range(GROUP):
                out_ref[block * rows : (block + 1) * rows, i * HD : (i + 1) * HD] = result[i * rows : (i + 1) * rows]


def attend(scalars, q, state, slabs, backs, final):
    tall = GROUP * q.shape[0] // 4
    tokens = slabs[0][0].shape[0]
    shapes = [(4, tall, 2 * HD), (4, tall, HD)]
    scratch = [pltpu.VMEM((2, tokens, HD), jnp.bfloat16), pltpu.VMEM((2, tokens, 2 * HD), jnp.bfloat16)]
    aliases = {}
    if final:
        out_shape = jax.ShapeDtypeStruct(q.shape, jnp.bfloat16)
        out_specs = VMEM
        scratch += [pltpu.VMEM(shape, jnp.float32) for shape in shapes]
    else:
        out_shape = [jax.ShapeDtypeStruct(shape, jnp.float32) for shape in shapes]
        out_specs = [VMEM] * 2
        if state is not None:
            aliases = {6: 0, 7: 1}
    work = len(backs) * 4 * tall * tokens
    return pl.pallas_call(
        functools.partial(attend_kernel, backs, state is None, final),
        out_shape=out_shape,
        in_specs=[SMEM] * 5 + [VMEM] * (1 + (0 if state is None else 2) + 2 * len(backs)),
        out_specs=out_specs,
        scratch_shapes=scratch,
        input_output_aliases=aliases,
        compiler_params=PARAMS,
        cost_estimate=pl.CostEstimate(flops=4 * work * HD, bytes_accessed=2 * q.size, transcendentals=work),
    )(*scalars, q, *(state or ()), *[a for slab in slabs for a in slab])


def per_device(spans, ctx, queries, keys, values, temps, levels, ctx_list, counts):
    where = jnp.stack([lax.axis_index("span"), lax.axis_index("ctx")]).astype(jnp.int32)
    scalars = (where, levels, temps, ctx_list, counts)
    planes = [list(range(p * ctx, (p + 2) * ctx)) for p in range(0, spans, 2)]
    up = [(s, (s + 2) % spans) for s in range(spans)]
    other_core = [(t, t ^ 1) for t in range(ctx)]
    rows = keys.shape[0]

    def exchange(a):
        return lax.all_to_all(a, ("span", "ctx"), 0, 0, axis_index_groups=planes, tiled=True)

    def by_head(a):
        width = a.shape[1] // KVH
        a = jnp.transpose(a.reshape(2, rows // 2, KVH, width), (2, 0, 1, 3))
        return a.reshape(KVH * rows, width)

    slab = exchange(jnp.concatenate([by_head(keys), by_head(values)], axis=1))
    q = exchange(by_head(queries))
    slabs = []
    for back in range(spans // 2):
        if back:
            slab = lax.ppermute(slab, "span", up)
        slabs.append((slab, lax.ppermute(slab, "ctx", other_core)))

    stages = [[0, 1]] + [[back] for back in range(2, spans // 2)]
    state = None
    for stage in stages:
        state = attend(scalars, q, state, [slabs[back] for back in stage], stage, stage is stages[-1])
    out = exchange(state).reshape(KVH, 2, rows // 2, WIDE)
    return jnp.transpose(out, (1, 2, 0, 3)).reshape(rows, HQ * HD)


def solution(mesh):
    return jax.shard_map(
        functools.partial(per_device, mesh.shape["span"], mesh.shape["ctx"]),
        mesh=mesh,
        in_specs=(
            P(("span", "ctx"), None),
            P(("span", "ctx"), None),
            P(("span", "ctx"), None),
            P(),
            P(),
            P(),
            P(),
        ),
        out_specs=P(("span", "ctx"), None),
        check_vma=False,
    )
```

```python
import functools
import math

import jax
import jax.numpy as jnp
from jax import lax
from jax.experimental import pallas as pl
from jax.experimental.pallas import tpu as pltpu
from jax.sharding import PartitionSpec as P

HQ = 24
KVH = 4
HD = 128
GROUP = HQ // KVH
WIDE = GROUP * HD
LOW = -1e30
SCALE = math.log2(math.e) / math.sqrt(HD)
SMEM = pl.BlockSpec(memory_space=pltpu.SMEM)
VMEM = pl.BlockSpec(memory_space=pltpu.VMEM)
PARAMS = pltpu.CompilerParams(vmem_limit_bytes=32 << 20)


def attend_kernel(backs, blocks, first, final, where_ref, levels_ref, temps_ref, list_ref, counts_ref, q_ref, *refs):
    refs = list(refs)
    if not first:
        del refs[:2]
    slabs = [(refs.pop(0), refs.pop(0)) for _ in backs]
    out_ref = refs.pop(0) if final else None
    sums_ref, top_ref, key_ref, value_ref = refs
    base = where_ref[0] & -2
    core = where_ref[1] & 1
    head = 2 * (where_ref[0] & 1) + (where_ref[1] >> 1)
    span_rows = q_ref.shape[0] // 2
    piece = span_rows // 4
    part = piece // 2
    half = slabs[0][0].shape[0] // 2
    group = GROUP // 2
    chains = [(block, g) for block in blocks for g in range(2)]

    if first:
        sums_ref[...] = jnp.zeros_like(sums_ref)
        top_ref[...] = jnp.full_like(top_ref, LOW)

    def wanted(span, ident):
        found = span == ident
        for j in range(list_ref.shape[1]):
            found = found | (list_ref[span, j] == ident)
        return found & (ident >= 0)

    index = lax.broadcasted_iota(jnp.int32, (half, HD), 0)
    for slab, back in zip(slabs, backs):
        for x in range(2):
            count = counts_ref[jnp.maximum(base + x - 2 * back, 0)]
            spare = slab[0][x * half : x * half + 16, :HD].astype(jnp.float32)[0:1]
            for side, ref in enumerate(slab):
                token = (index // piece) * (2 * piece) + (core ^ side) * piece + index % piece
                keep = token < count
                at = slice(x * half, (x + 1) * half)
                to = slice(side * half, (side + 1) * half)
                keys = jnp.where(keep, ref[at, :HD].astype(jnp.float32), spare)
                values = jnp.where(keep, ref[at, HD:].astype(jnp.float32), 0.0)
                key_ref[x, :, to] = jnp.transpose(keys).astype(jnp.bfloat16)
                value_ref[x, to, :HD] = values.astype(jnp.bfloat16)
                value_ref[x, to, HD:] = jnp.where(keep, 1.0, 0.0).astype(jnp.bfloat16)

        @pl.loop(0, 4)
        def _(turn):
            side = turn >> 1
            x = turn & 1
            span = base + side

            @pl.when(wanted(span, base + x - 2 * back))
            def _():
                level = levels_ref[span]
                keys = key_ref[x]
                values = value_ref[x]

                def scores(block, g):
                    rows = []
                    for i in range(group):
                        lanes = slice((g * group + i) * HD, (g * group + i + 1) * HD)
                        for t in range(4):
                            at = pl.multiple_of(side * span_rows + t * piece + block * part, part)
                            rows.append(q_ref[pl.ds(at, part), lanes])
                    return jnp.dot(jnp.concatenate(rows, axis=0), keys, preferred_element_type=jnp.float32)

                ready = scores(*chains[0])
                for n, (block, g) in enumerate(chains):
                    s = ready
                    if n + 1 < len(chains):
                        ready = scores(*chains[n + 1])
                    step = s.shape[0] // group
                    s = jnp.concatenate(
                        [
                            s[i * step : (i + 1) * step] * (temps_ref[level, head * GROUP + g * group + i] * SCALE)
                            for i in range(group)
                        ],
                        axis=0,
                    )
                    chain = 2 * block + g
                    old_top = top_ref[side, chain]
                    top = jnp.maximum(old_top, jnp.max(s, axis=1, keepdims=True))
                    weight = jnp.concatenate(
                        [jnp.exp2(s[:, at : at + HD] - top).astype(jnp.bfloat16) for at in range(0, s.shape[1], HD)],
                        axis=1,
                    )
                    sums = jnp.dot(weight, values, preferred_element_type=jnp.float32)
                    shrink = jnp.exp2(old_top - top)
                    sums_ref[side, chain] = sums + sums_ref[side, chain] * jnp.concatenate([shrink, shrink], axis=1)
                    top_ref[side, chain] = top

    if final:
        for side in range(2):
            for block, g in chains:
                sums = sums_ref[side, 2 * block + g]
                result = (sums[:, :HD] / sums[:, HD:]).astype(jnp.bfloat16)
                for i in range(group):
                    lanes = slice((g * group + i) * HD, (g * group + i + 1) * HD)
                    for t in range(4):
                        to = (4 * side + t) * part
                        at = (4 * i + t) * part
                        out_ref[to : to + part, lanes] = result[at : at + part]


def attend(scalars, q, state, slabs, backs, blocks, final):
    tall = GROUP * q.shape[0] // 8
    tokens = slabs[0][0].shape[0]
    out_shape = [
        jax.ShapeDtypeStruct((2, 4, tall, 2 * HD), jnp.float32),
        jax.ShapeDtypeStruct((2, 4, tall, HD), jnp.float32),
    ]
    if final:
        out_shape = [jax.ShapeDtypeStruct((q.shape[0] // 2, q.shape[1]), jnp.bfloat16)] + out_shape
    work = len(backs) * len(blocks) * 4 * tall * tokens
    return pl.pallas_call(
        functools.partial(attend_kernel, backs, blocks, state is None, final),
        out_shape=out_shape,
        in_specs=[SMEM] * 5 + [VMEM] * (1 + (0 if state is None else 2) + 2 * len(backs)),
        out_specs=[VMEM] * len(out_shape),
        scratch_shapes=[pltpu.VMEM((2, HD, tokens), jnp.bfloat16), pltpu.VMEM((2, tokens, 2 * HD), jnp.bfloat16)],
        input_output_aliases={} if state is None else {6: final + 0, 7: final + 1},
        compiler_params=PARAMS,
        cost_estimate=pl.CostEstimate(flops=4 * work * HD, bytes_accessed=2 * q.size, transcendentals=work),
    )(*scalars, q, *(state or ()), *[a for slab in slabs for a in slab])


def per_device(spans, ctx, queries, keys, values, temps, levels, ctx_list, counts):
    where = jnp.stack([lax.axis_index("span"), lax.axis_index("ctx")]).astype(jnp.int32)
    scalars = (where, levels, temps, ctx_list, counts)
    planes = [list(range(p * ctx, (p + 2) * ctx)) for p in range(0, spans, 2)]
    other_core = [(t, t ^ 1) for t in range(ctx)]
    rows = keys.shape[0]
    last = spans // 2 - 1

    def exchange(a):
        return lax.all_to_all(a, ("span", "ctx"), 0, 0, axis_index_groups=planes, tiled=True)

    def by_head(a):
        width = a.shape[1] // KVH
        a = jnp.transpose(a.reshape(2, rows // 2, KVH, width), (2, 0, 1, 3))
        return a.reshape(KVH * rows, width)

    def up(a, steps):
        return lax.ppermute(a, "span", [(s, (s + 2 * steps) % spans) for s in range(spans)])

    def near(a):
        return lax.ppermute(a, "ctx", other_core)

    own = exchange(jnp.concatenate([by_head(keys), by_head(values)], axis=1))
    slabs = {0: own, 1: up(own, 1), last: up(own, last)}
    q = exchange(by_head(queries))
    others = {back: near(slab) for back, slab in slabs.items()}
    slabs, others = lax.optimization_barrier((slabs, others))
    stage = sorted(slabs)
    state = None
    for back in range(2, last + 1):
        state = attend(scalars, q, state, [(slabs[b], others[b]) for b in stage], stage, (0, 1), False)
        if back < last:
            slabs[back] = up(slabs[back - 1], 1)
            slabs[back], state = lax.optimization_barrier((slabs[back], state))
            others[back] = near(slabs[back])
            stage = [back]
        if back >= last - 1:
            break
    result = []
    for block in range(2):
        out, *state = attend(scalars, q, state, [(slabs[b], others[b]) for b in stage], stage, (block,), True)
        result.append(exchange(out).reshape(KVH, 2, 1, rows // 4, WIDE))
    out = jnp.concatenate(result, axis=2)
    return jnp.transpose(out, (1, 2, 3, 0, 4)).reshape(rows, HQ * HD)


def solution(mesh):
    return jax.shard_map(
        functools.partial(per_device, mesh.shape["span"], mesh.shape["ctx"]),
        mesh=mesh,
        in_specs=(
            P(("span", "ctx"), None),
            P(("span", "ctx"), None),
            P(("span", "ctx"), None),
            P(),
            P(),
            P(),
            P(),
        ),
        out_specs=P(("span", "ctx"), None),
        check_vma=False,
    )
```

```python
import functools
import math

import jax
import jax.numpy as jnp
from jax import lax
from jax.experimental import pallas as pl
from jax.experimental.pallas import tpu as pltpu
from jax.sharding import PartitionSpec as P

HQ = 24
KVH = 4
HD = 128
GROUP = HQ // KVH
WIDE = GROUP * HD
PEERS = 8
LOW = -1e30
SCALE = math.log2(math.e) / math.sqrt(HD)
SMEM = pl.BlockSpec(memory_space=pltpu.SMEM)
VMEM = pl.BlockSpec(memory_space=pltpu.VMEM)
ANY = pl.BlockSpec(memory_space=pl.ANY)
SMALL = pltpu.CompilerParams(vmem_limit_bytes=6 << 20)
LARGE = pltpu.CompilerParams(vmem_limit_bytes=16 << 20)


def place():
    span, tok = lax.axis_index("span"), lax.axis_index("ctx")
    return span & -2, 4 * (span & 1) + tok


def begin_kernel(planes, levels_ref, temps_ref, list_ref, counts_ref, keys_ref, values_ref, *refs):
    kv_ref, table_ref, factor_ref, source, target, sems = refs
    loads = [
        pltpu.make_async_copy(ref, source.at[i], sems.at[i]) for i, ref in enumerate((keys_ref, values_ref))
    ]
    for load in loads:
        load.start()
    base, number = place()
    head = number >> 1
    for side in range(2):
        level = levels_ref[base + side]
        for i in range(GROUP):
            factor_ref[side * GROUP + i] = temps_ref[level, head * GROUP + i] * SCALE

        @pl.loop(0, 2 * planes)
        def _(slab):
            ident = base + (slab & 1) - 2 * (slab >> 1)
            found = base + side == ident
            for j in range(list_ref.shape[1]):
                found = found | (list_ref[base + side, j] == ident)
            count = jnp.where(found & (ident >= 0), counts_ref[jnp.maximum(ident, 0)], 0)
            table_ref[2 * slab + side] = count

    for load in loads:
        load.wait()
    part = source.shape[1] // 2
    for peer in range(PEERS):
        rows = slice((peer & 1) * part, (peer & 1) * part + part)
        lanes = slice((peer >> 1) * HD, (peer >> 1) * HD + HD)
        to = slice(peer * part, (peer + 1) * part)
        target[to, :HD] = source[0, rows, lanes]
        target[to, HD:] = source[1, rows, lanes]
    store = pltpu.make_async_copy(target, kv_ref, sems.at[0])
    store.start()
    store.wait()


def begin(planes, levels, temps, ctx_list, counts, keys, values):
    rows = keys.shape[0]
    shape = (PEERS * rows // 2, 2 * HD)
    return pl.pallas_call(
        functools.partial(begin_kernel, planes),
        out_shape=[
            jax.ShapeDtypeStruct(shape, jnp.bfloat16),
            jax.ShapeDtypeStruct((4 * planes,), jnp.int32),
            jax.ShapeDtypeStruct((2 * GROUP,), jnp.float32),
        ],
        in_specs=[SMEM] * 4 + [ANY] * 2,
        out_specs=[ANY, SMEM, SMEM],
        scratch_shapes=[
            pltpu.VMEM((2, *keys.shape), jnp.bfloat16),
            pltpu.VMEM(shape, jnp.bfloat16),
            pltpu.SemaphoreType.DMA((2,)),
        ],
        compiler_params=SMALL,
    )(levels, temps, ctx_list, counts, keys, values)


def cut_kernel(q_ref, *pieces):
    number = place()[1]
    part = q_ref.shape[0] // 2
    for j, piece in enumerate(pieces):
        peer = number ^ j
        rows = pl.ds(pl.multiple_of((peer & 1) * part, part), part)
        lanes = pl.ds(pl.multiple_of((peer >> 1) * WIDE, HD), WIDE)
        piece[...] = q_ref[rows, lanes]


def cut(q):
    return pl.pallas_call(
        cut_kernel,
        out_shape=[jax.ShapeDtypeStruct((q.shape[0] // 2, WIDE), jnp.bfloat16)] * PEERS,
        in_specs=[VMEM],
        out_specs=[VMEM] * PEERS,
        compiler_params=SMALL,
    )(q)


def join_kernel(*refs):
    pieces, out_ref, sems = refs[:PEERS], refs[PEERS], refs[PEERS + 1]
    number = place()[1]
    part = out_ref.shape[0] // 2
    copies = []
    for j, piece in enumerate(pieces):
        peer = number ^ j
        rows = pl.ds(pl.multiple_of((peer & 1) * part, part), part)
        lanes = pl.ds(pl.multiple_of((peer >> 1) * WIDE, HD), WIDE)
        copies.append(pltpu.make_async_copy(piece, out_ref.at[rows, lanes], sems.at[j]))
        copies[-1].start()
    for copy in copies:
        copy.wait()


def join(pieces):
    return pl.pallas_call(
        join_kernel,
        out_shape=jax.ShapeDtypeStruct((2 * pieces[0].shape[0], HQ * HD), jnp.bfloat16),
        in_specs=[VMEM] * PEERS,
        out_specs=ANY,
        scratch_shapes=[pltpu.SemaphoreType.DMA((PEERS,))],
        compiler_params=SMALL,
    )(*pieces)


def attend_kernel(backs, first, final, table_ref, factor_ref, *refs):
    refs = list(refs)
    if first:
        q_pieces = [refs.pop(0) for _ in range(PEERS)]
    else:
        q_ref = refs.pop(0)
        del refs[:2]
    slabs = [(refs.pop(0), refs.pop(0)) for _ in backs]
    out_refs = [refs.pop(0) for _ in range(PEERS)] if final else None
    sums_ref, top_ref = refs.pop(0), refs.pop(0)
    number = place()[1]
    core = number & 1
    if first:
        q_ref = refs.pop(0)
        for j, piece in enumerate(q_pieces):
            q_ref[number ^ j] = piece[...]
        sums_ref[...] = jnp.zeros_like(sums_ref)
        top_ref[...] = jnp.full_like(top_ref, LOW)
    key_ref, value_ref = refs[:2]
    piece = q_ref.shape[1]
    half = slabs[0][0].shape[0] // 2
    group = GROUP // 2
    chains = [(block, g) for block in range(2) for g in range(2)]

    index = lax.broadcasted_iota(jnp.int32, (half, HD), 0)
    for slab, back in zip(slabs, backs):
        for x in range(2):
            count = jnp.maximum(table_ref[4 * back + 2 * x], table_ref[4 * back + 2 * x + 1])
            spare = slab[0][x * half : x * half + 16, :HD].astype(jnp.float32)[0:1]
            for side, ref in enumerate(slab):
                token = (index // piece) * (2 * piece) + (core ^ side) * piece + index % piece
                keep = token < count
                at = slice(x * half, (x + 1) * half)
                to = slice(side * half, (side + 1) * half)
                keys = jnp.where(keep, ref[at, :HD].astype(jnp.float32), spare)
                values = jnp.where(keep, ref[at, HD:].astype(jnp.float32), 0.0)
                key_ref[x, :, to] = jnp.transpose(keys).astype(jnp.bfloat16)
                value_ref[x, to, :HD] = values.astype(jnp.bfloat16)
                value_ref[x, to, HD:] = jnp.where(keep, 1.0, 0.0).astype(jnp.bfloat16)

        @pl.loop(0, 4)
        def _(turn):
            x = turn >> 1
            side = turn & 1

            @pl.when(table_ref[4 * back + turn] > 0)
            def _():
                keys = key_ref[x]
                values = value_ref[x]

                def scores(block, g):
                    rows = []
                    for i in range(group):
                        lanes = slice((g * group + i) * HD, (g * group + i + 1) * HD)
                        for t in range(2):
                            rows.append(q_ref[4 * side + 2 * block + t, :, lanes])
                    return jnp.dot(jnp.concatenate(rows, axis=0), keys, preferred_element_type=jnp.float32)

                ready = scores(*chains[0])
                for n, (block, g) in enumerate(chains):
                    s = ready
                    if n + 1 < len(chains):
                        ready = scores(*chains[n + 1])
                    step = s.shape[0] // group
                    s = jnp.concatenate(
                        [
                            s[i * step : (i + 1) * step] * factor_ref[side * GROUP + g * group + i]
                            for i in range(group)
                        ],
                        axis=0,
                    )
                    chain = 2 * block + g
                    old_top = top_ref[side, chain]
                    top = jnp.maximum(old_top, jnp.max(s, axis=1, keepdims=True))
                    weight = jnp.concatenate(
                        [jnp.exp2(s[:, at : at + HD] - top).astype(jnp.bfloat16) for at in range(0, s.shape[1], HD)],
                        axis=1,
                    )
                    sums = jnp.dot(weight, values, preferred_element_type=jnp.float32)
                    shrink = jnp.exp2(old_top - top)
                    sums_ref[side, chain] = sums + sums_ref[side, chain] * jnp.concatenate([shrink, shrink], axis=1)
                    top_ref[side, chain] = top

    if final:
        done_ref = refs[2]
        for side in range(2):
            for block, g in chains:
                sums = sums_ref[side, 2 * block + g]
                result = (sums[:, :HD] / sums[:, HD:]).astype(jnp.bfloat16)
                for i in range(group):
                    lanes = slice((g * group + i) * HD, (g * group + i + 1) * HD)
                    for t in range(2):
                        at = (2 * i + t) * piece
                        done_ref[4 * side + 2 * block + t, :, lanes] = result[at : at + piece]
        for j, out_ref in enumerate(out_refs):
            out_ref[...] = done_ref[number ^ j]


def attend(tables, q, state, slabs, backs, final):
    first = state is None
    piece = q[0].shape[-2]
    tall = GROUP * piece
    tokens = slabs[0][0].shape[0]
    q_shape = (PEERS, piece, WIDE)
    out_shape = [
        jax.ShapeDtypeStruct((2, 4, tall, 2 * HD), jnp.float32),
        jax.ShapeDtypeStruct((2, 4, tall, HD), jnp.float32),
    ]
    scratch = [pltpu.VMEM((2, HD, tokens), jnp.bfloat16), pltpu.VMEM((2, tokens, 2 * HD), jnp.bfloat16)]
    if final:
        out_shape = [jax.ShapeDtypeStruct(q_shape[1:], jnp.bfloat16)] * PEERS + out_shape
        scratch.append(pltpu.VMEM(q_shape, jnp.bfloat16))
    if first:
        out_shape.append(jax.ShapeDtypeStruct(q_shape, jnp.bfloat16))
    work = len(backs) * PEERS * tall * tokens
    inputs = [*q, *(state or ()), *[a for slab in slabs for a in slab]]
    aliases = {} if first else {3: PEERS * final, 4: PEERS * final + 1}
    return pl.pallas_call(
        functools.partial(attend_kernel, backs, first, final),
        out_shape=out_shape,
        in_specs=[SMEM] * 2 + [VMEM] * len(inputs),
        out_specs=[VMEM] * len(out_shape),
        scratch_shapes=scratch,
        input_output_aliases=aliases,
        compiler_params=LARGE,
        cost_estimate=pl.CostEstimate(flops=2 * work * HD, bytes_accessed=4 * PEERS * piece * WIDE, transcendentals=work // 2),
    )(*tables, *inputs)


def per_device(spans, ctx, queries, keys, values, temps, levels, ctx_list, counts):
    planes = [list(range(p * ctx, (p + 2) * ctx)) for p in range(0, spans, 2)]
    other_core = [(t, t ^ 1) for t in range(ctx)]
    last = spans // 2 - 1

    def swap(pieces):
        moved = [pieces[0]]
        for j in range(1, PEERS):
            moved.append(lax.ppermute(pieces[j], ("span", "ctx"), [(f, f ^ j) for f in range(spans * ctx)]))
        return moved

    def up(a, steps):
        return lax.ppermute(a, "span", [(s, (s + 2 * steps) % spans) for s in range(spans)])

    def near(a):
        return lax.ppermute(a, "ctx", other_core)

    kv, *tables = begin(spans // 2, levels, temps, ctx_list, counts, keys, values)
    own = lax.all_to_all(kv, ("span", "ctx"), 0, 0, axis_index_groups=planes, tiled=True)
    slabs = {0: own, 1: up(own, 1), last: up(own, last)}
    q = swap(cut(queries))
    others = {back: near(slab) for back, slab in slabs.items()}
    slabs, others = lax.optimization_barrier((slabs, others))
    stage = sorted(slabs)
    state = None
    for back in range(2, last):
        *state, q_all = [*attend(tables, q, state, [(slabs[b], others[b]) for b in stage], stage, False), *q][:3]
        q = [q_all]
        slabs[back] = up(slabs[back - 1], 1)
        slabs[back], state = lax.optimization_barrier((slabs[back], state))
        others[back] = near(slabs[back])
        stage = [back]
    out = attend(tables, q, state, [(slabs[b], others[b]) for b in stage], stage, True)
    return join(swap(out[:PEERS]))


def solution(mesh):
    return jax.shard_map(
        functools.partial(per_device, mesh.shape["span"], mesh.shape["ctx"]),
        mesh=mesh,
        in_specs=(
            P(("span", "ctx"), None),
            P(("span", "ctx"), None),
            P(("span", "ctx"), None),
            P(),
            P(),
            P(),
            P(),
        ),
        out_specs=P(("span", "ctx"), None),
        check_vma=False,
    )
```

```python
import functools
import math

import jax
import jax.numpy as jnp
from jax import lax
from jax.experimental import pallas as pl
from jax.experimental.pallas import tpu as pltpu
from jax.sharding import PartitionSpec as P

HQ = 24
KVH = 4
HD = 128
GROUP = HQ // KVH
WIDE = GROUP * HD
PEERS = 8
LOW = -1e30
SCALE = math.log2(math.e) / math.sqrt(HD)
SMEM = pl.BlockSpec(memory_space=pltpu.SMEM)
VMEM = pl.BlockSpec(memory_space=pltpu.VMEM)
HBM = pl.BlockSpec(memory_space=pltpu.HBM)
SMALL = pltpu.CompilerParams(vmem_limit_bytes=6 << 20)
LARGE = pltpu.CompilerParams(vmem_limit_bytes=16 << 20)


def place():
    span, tok = lax.axis_index("span"), lax.axis_index("ctx")
    return span & -2, 4 * (span & 1) + tok


def table_kernel(planes, levels_ref, temps_ref, list_ref, counts_ref, table_ref, factor_ref):
    base, number = place()
    head = number >> 1
    for side in range(2):
        level = levels_ref[base + side]
        for i in range(GROUP):
            factor_ref[side * GROUP + i] = temps_ref[level, head * GROUP + i] * SCALE

        @pl.loop(0, 2 * planes)
        def _(slab):
            ident = base + (slab & 1) - 2 * (slab >> 1)
            found = base + side == ident
            for j in range(list_ref.shape[1]):
                found = found | (list_ref[base + side, j] == ident)
            count = jnp.where(found & (ident >= 0), counts_ref[jnp.maximum(ident, 0)], 0)
            table_ref[2 * slab + side] = count


def tabulate(planes, levels, temps, ctx_list, counts):
    return pl.pallas_call(
        functools.partial(table_kernel, planes),
        out_shape=[jax.ShapeDtypeStruct((4 * planes,), jnp.int32), jax.ShapeDtypeStruct((2 * GROUP,), jnp.float32)],
        in_specs=[SMEM] * 4,
        out_specs=[SMEM] * 2,
        compiler_params=SMALL,
    )(levels, temps, ctx_list, counts)


def begin_kernel(keys_ref, values_ref, kv_ref, source, target, sems):
    loads = [pltpu.make_async_copy(ref, source.at[i], sems.at[i]) for i, ref in enumerate((keys_ref, values_ref))]
    for load in loads:
        load.start()
    for load in loads:
        load.wait()
    part = source.shape[1] // 2
    for peer in range(PEERS):
        rows = slice((peer & 1) * part, (peer & 1) * part + part)
        lanes = slice((peer >> 1) * HD, (peer >> 1) * HD + HD)
        to = slice(peer * part, (peer + 1) * part)
        target[to, :HD] = source[0, rows, lanes]
        target[to, HD:] = source[1, rows, lanes]
    store = pltpu.make_async_copy(target, kv_ref, sems.at[0])
    store.start()
    store.wait()


def begin(keys, values):
    shape = (PEERS * keys.shape[0] // 2, 2 * HD)
    return pl.pallas_call(
        begin_kernel,
        out_shape=jax.ShapeDtypeStruct(shape, jnp.bfloat16),
        in_specs=[HBM] * 2,
        out_specs=HBM,
        scratch_shapes=[
            pltpu.VMEM((2, *keys.shape), jnp.bfloat16),
            pltpu.VMEM(shape, jnp.bfloat16),
            pltpu.SemaphoreType.DMA((2,)),
        ],
        compiler_params=SMALL,
    )(keys, values)


def cut_kernel(q_ref, *pieces):
    number = place()[1]
    part = q_ref.shape[0] // 2
    for j, piece in enumerate(pieces):
        peer = number ^ j
        rows = pl.ds(pl.multiple_of((peer & 1) * part, part), part)
        lanes = pl.ds(pl.multiple_of((peer >> 1) * WIDE, HD), WIDE)
        piece[...] = q_ref[rows, lanes]


def cut(q):
    return pl.pallas_call(
        cut_kernel,
        out_shape=[jax.ShapeDtypeStruct((q.shape[0] // 2, WIDE), jnp.bfloat16)] * PEERS,
        in_specs=[VMEM],
        out_specs=[VMEM] * PEERS,
        compiler_params=SMALL,
    )(q)


def join_kernel(*refs):
    pieces, out_ref, sems = refs[:PEERS], refs[PEERS], refs[PEERS + 1]
    number = place()[1]
    part = out_ref.shape[0] // 2
    copies = []
    for j, piece in enumerate(pieces):
        peer = number ^ j
        rows = pl.ds(pl.multiple_of((peer & 1) * part, part), part)
        lanes = pl.ds(pl.multiple_of((peer >> 1) * WIDE, HD), WIDE)
        copies.append(pltpu.make_async_copy(piece, out_ref.at[rows, lanes], sems.at[j]))
        copies[-1].start()
    for copy in copies:
        copy.wait()


def join(pieces):
    return pl.pallas_call(
        join_kernel,
        out_shape=jax.ShapeDtypeStruct((2 * pieces[0].shape[0], HQ * HD), jnp.bfloat16),
        in_specs=[VMEM] * PEERS,
        out_specs=HBM,
        scratch_shapes=[pltpu.SemaphoreType.DMA((PEERS,))],
        compiler_params=SMALL,
    )(*pieces)


def attend_kernel(backs, first, final, table_ref, factor_ref, *refs):
    refs = list(refs)
    if first:
        q_pieces = [refs.pop(0) for _ in range(PEERS)]
    else:
        q_ref = refs.pop(0)
        del refs[:2]
    slabs = [(refs.pop(0), refs.pop(0)) for _ in backs]
    out_refs = [refs.pop(0) for _ in range(PEERS)] if final else None
    sums_ref, top_ref = refs.pop(0), refs.pop(0)
    number = place()[1]
    core = number & 1
    if first:
        q_ref = refs.pop(0)
        for j, piece in enumerate(q_pieces):
            q_ref[number ^ j] = piece[...]
        sums_ref[...] = jnp.zeros_like(sums_ref)
        top_ref[...] = jnp.full_like(top_ref, LOW)
    key_ref, value_ref = refs[:2]
    piece = q_ref.shape[1]
    half = slabs[0][0].shape[0] // 2
    group = GROUP // 2
    chains = [(block, g) for block in range(2) for g in range(2)]

    block_rows = 2 * piece
    index = lax.broadcasted_iota(jnp.int32, (block_rows, HD), 0)
    own_part = index < piece
    token = 2 * block_rows + index + jnp.where(own_part, core * piece, -(core * piece))
    for slab, back in zip(slabs, backs):
        for x in range(2):
            count = jnp.maximum(table_ref[4 * back + 2 * x], table_ref[4 * back + 2 * x + 1])
            at = x * half
            spare = slab[0][at : at + 16, :HD].astype(jnp.float32)[0:1]
            parts = [ref[at : at + block_rows, :] for ref in slab]
            for n in range(2, 4):
                low = at + n * piece
                parts.append(jnp.concatenate([ref[low : low + piece, :] for ref in slab], axis=0))
            for n, values in enumerate(parts):
                to = slice(n * block_rows, (n + 1) * block_rows)
                keys = values[:, :HD].astype(jnp.float32)
                values = values[:, HD:]
                ones = jnp.ones_like(values)
                if n >= 2:
                    keep = token + (n - 2) * block_rows < count
                    keys = jnp.where(keep, keys, spare)
                    values = jnp.where(keep, values.astype(jnp.float32), 0.0).astype(jnp.bfloat16)
                    ones = jnp.where(keep, 1.0, 0.0).astype(jnp.bfloat16)
                key_ref[x, :, to] = jnp.transpose(keys).astype(jnp.bfloat16)
                value_ref[x, to, :HD] = values
                value_ref[x, to, HD:] = ones

        @pl.loop(0, 4)
        def _(turn):
            x = turn >> 1
            side = turn & 1

            count = table_ref[4 * back + turn]

            def visit(width):
                keys = key_ref[x, :, :width]
                values = value_ref[x, :width, :]

                def scores(block, g):
                    rows = []
                    for i in range(group):
                        lanes = slice((g * group + i) * HD, (g * group + i + 1) * HD)
                        for t in range(2):
                            rows.append(q_ref[4 * side + 2 * block + t, :, lanes])
                    return jnp.dot(jnp.concatenate(rows, axis=0), keys, preferred_element_type=jnp.float32)

                ready = scores(*chains[0])
                for n, (block, g) in enumerate(chains):
                    s = ready
                    if n + 1 < len(chains):
                        ready = scores(*chains[n + 1])
                    step = s.shape[0] // group
                    s = jnp.concatenate(
                        [
                            s[i * step : (i + 1) * step] * factor_ref[side * GROUP + g * group + i]
                            for i in range(group)
                        ],
                        axis=0,
                    )
                    chain = 2 * block + g
                    old_top = top_ref[side, chain]
                    top = jnp.maximum(old_top, jnp.max(s, axis=1, keepdims=True))
                    weight = jnp.concatenate(
                        [jnp.exp2(s[:, at : at + HD] - top).astype(jnp.bfloat16) for at in range(0, s.shape[1], HD)],
                        axis=1,
                    )
                    sums = jnp.dot(weight, values, preferred_element_type=jnp.float32)
                    shrink = jnp.exp2(old_top - top)
                    sums_ref[side, chain] = sums + sums_ref[side, chain] * jnp.concatenate([shrink, shrink], axis=1)
                    top_ref[side, chain] = top

            most = 3 * block_rows
            pl.when((count > 0) & (count <= most))(lambda: visit(most))
            pl.when(count > most)(lambda: visit(most + block_rows))

    if final:
        done_ref = refs[2]
        for side in range(2):
            for block, g in chains:
                sums = sums_ref[side, 2 * block + g]
                result = (sums[:, :HD] / sums[:, HD:]).astype(jnp.bfloat16)
                for i in range(group):
                    lanes = slice((g * group + i) * HD, (g * group + i + 1) * HD)
                    for t in range(2):
                        at = (2 * i + t) * piece
                        done_ref[4 * side + 2 * block + t, :, lanes] = result[at : at + piece]
        for j, out_ref in enumerate(out_refs):
            out_ref[...] = done_ref[number ^ j]


def attend(tables, q, state, slabs, backs, final):
    first = state is None
    piece = q[0].shape[-2]
    tall = GROUP * piece
    tokens = slabs[0][0].shape[0]
    q_shape = (PEERS, piece, WIDE)
    out_shape = [
        jax.ShapeDtypeStruct((2, 4, tall, 2 * HD), jnp.float32),
        jax.ShapeDtypeStruct((2, 4, tall, HD), jnp.float32),
    ]
    scratch = [pltpu.VMEM((2, HD, tokens), jnp.bfloat16), pltpu.VMEM((2, tokens, 2 * HD), jnp.bfloat16)]
    if final:
        out_shape = [jax.ShapeDtypeStruct(q_shape[1:], jnp.bfloat16)] * PEERS + out_shape
        scratch.append(pltpu.VMEM(q_shape, jnp.bfloat16))
    if first:
        out_shape.append(jax.ShapeDtypeStruct(q_shape, jnp.bfloat16))
    work = len(backs) * PEERS * tall * tokens
    inputs = [*q, *(state or ()), *[a for slab in slabs for a in slab]]
    aliases = {} if first else {3: PEERS * final, 4: PEERS * final + 1}
    return pl.pallas_call(
        functools.partial(attend_kernel, backs, first, final),
        out_shape=out_shape,
        in_specs=[SMEM] * 2 + [VMEM] * len(inputs),
        out_specs=[VMEM] * len(out_shape),
        scratch_shapes=scratch,
        input_output_aliases=aliases,
        compiler_params=LARGE,
        cost_estimate=pl.CostEstimate(flops=2 * work * HD, bytes_accessed=4 * PEERS * piece * WIDE, transcendentals=work // 2),
    )(*tables, *inputs)


def per_device(spans, ctx, queries, keys, values, temps, levels, ctx_list, counts):
    planes = [list(range(p * ctx, (p + 2) * ctx)) for p in range(0, spans, 2)]
    other_core = [(t, t ^ 1) for t in range(ctx)]
    last = spans // 2 - 1

    def swap(pieces):
        moved = list(pieces)
        for j in (6, 7, 4, 2, 5, 3, 1):
            moved[j] = lax.ppermute(pieces[j], ("span", "ctx"), [(f, f ^ j) for f in range(spans * ctx)])
        return moved

    def up(a, steps):
        return lax.ppermute(a, "span", [(s, (s + 2 * steps) % spans) for s in range(spans)])

    def near(a):
        return lax.ppermute(a, "ctx", other_core)

    tables = tabulate(spans // 2, levels, temps, ctx_list, counts)
    own = lax.all_to_all(begin(keys, values), ("span", "ctx"), 0, 0, axis_index_groups=planes, tiled=True)
    own, tables, queries = lax.optimization_barrier((own, tables, queries))
    slabs = {0: own, 1: up(own, 1), last: up(own, last)}
    others = {0: near(own)}
    slabs, others, q = lax.optimization_barrier((slabs, others, swap(cut(queries))))
    others |= {back: near(slabs[back]) for back in (1, last)}
    stage = sorted(slabs)
    state = None
    for back in range(2, last):
        slabs[back] = up(slabs[back - 1], 1)
        *state, q_all = [*attend(tables, q, state, [(slabs[b], others[b]) for b in stage], stage, False), *q][:3]
        q = [q_all]
        slabs[back], state = lax.optimization_barrier((slabs[back], state))
        others[back] = near(slabs[back])
        stage = [back]
    out = attend(tables, q, state, [(slabs[b], others[b]) for b in stage], stage, True)
    return join(swap(out[:PEERS]))


def solution(mesh):
    return jax.shard_map(
        functools.partial(per_device, mesh.shape["span"], mesh.shape["ctx"]),
        mesh=mesh,
        in_specs=(
            P(("span", "ctx"), None),
            P(("span", "ctx"), None),
            P(("span", "ctx"), None),
            P(),
            P(),
            P(),
            P(),
        ),
        out_specs=P(("span", "ctx"), None),
        check_vma=False,
    )
```

```python
import functools
import math

import jax
import jax.numpy as jnp
from jax import lax
from jax.experimental import pallas as pl
from jax.experimental.pallas import tpu as pltpu
from jax.sharding import PartitionSpec as P

HQ = 24
KVH = 4
HD = 128
GROUP = HQ // KVH
WIDE = GROUP * HD
PEERS = 8
LOW = -1e30
SCALE = math.log2(math.e) / math.sqrt(HD)
SMEM = pl.BlockSpec(memory_space=pltpu.SMEM)
VMEM = pl.BlockSpec(memory_space=pltpu.VMEM)
HBM = pl.BlockSpec(memory_space=pltpu.HBM)
SMALL = pltpu.CompilerParams(vmem_limit_bytes=6 << 20)
LARGE = pltpu.CompilerParams(vmem_limit_bytes=16 << 20)


STEPS = ((0, 0), (6, 6), (7, 7), (4, 2), (2, 4), (5, 3), (3, 5), (1, 1))


def sent_to(number, step):
    even, odd = STEPS[step]
    return number ^ jnp.where(number & 1 == 0, even, odd)


def got_from(number, step):
    even, odd = STEPS[step]
    if even & 1:
        even, odd = odd, even
    return number ^ jnp.where(number & 1 == 0, even, odd)


def place():
    span, tok = lax.axis_index("span"), lax.axis_index("ctx")
    return span & -2, 4 * (span & 1) + tok


def table_kernel(planes, levels_ref, temps_ref, list_ref, counts_ref, table_ref, factor_ref):
    base, number = place()
    head = number >> 1
    for side in range(2):
        level = levels_ref[base + side]
        for i in range(GROUP):
            factor_ref[side * GROUP + i] = temps_ref[level, head * GROUP + i] * SCALE

        @pl.loop(0, 2 * planes)
        def _(slab):
            ident = base + (slab & 1) - 2 * (slab >> 1)
            found = base + side == ident
            for j in range(list_ref.shape[0]):
                found = found | (list_ref[j, base + side] == ident)
            count = jnp.where(found & (ident >= 0), counts_ref[jnp.maximum(ident, 0)], 0)
            table_ref[2 * slab + side] = count


def tabulate(planes, levels, temps, ctx_list, counts):
    return pl.pallas_call(
        functools.partial(table_kernel, planes),
        out_shape=[jax.ShapeDtypeStruct((4 * planes,), jnp.int32), jax.ShapeDtypeStruct((2 * GROUP,), jnp.float32)],
        in_specs=[SMEM] * 4,
        out_specs=[SMEM] * 2,
        compiler_params=SMALL,
    )(levels, temps, ctx_list, counts)


def begin_kernel(keys_ref, values_ref, *refs):
    pieces, (source, target, sems) = refs[:PEERS], refs[PEERS:]
    number = place()[1]
    loads = [pltpu.make_async_copy(ref, source.at[i], sems.at[i]) for i, ref in enumerate((keys_ref, values_ref))]
    for load in loads:
        load.start()
    for load in loads:
        load.wait()
    part = target.shape[1]
    stores = []
    for step, piece in enumerate(pieces):
        peer = sent_to(number, step)
        rows = pl.ds(pl.multiple_of((peer & 1) * part, part), part)
        lanes = pl.ds(pl.multiple_of((peer >> 1) * HD, HD), HD)
        target[step, :, :HD] = source[0, rows, lanes]
        target[step, :, HD:] = source[1, rows, lanes]
        stores.append(pltpu.make_async_copy(target.at[step], piece, sems.at[step]))
        stores[-1].start()
    for store in stores:
        store.wait()


def begin(keys, values):
    shape = (keys.shape[0] // 2, 2 * HD)
    return pl.pallas_call(
        begin_kernel,
        out_shape=[jax.ShapeDtypeStruct(shape, jnp.bfloat16)] * PEERS,
        in_specs=[HBM] * 2,
        out_specs=[HBM] * PEERS,
        scratch_shapes=[
            pltpu.VMEM((2, *keys.shape), jnp.bfloat16),
            pltpu.VMEM((PEERS, *shape), jnp.bfloat16),
            pltpu.SemaphoreType.DMA((PEERS,)),
        ],
    )(keys, values)


def gather_kernel(*refs):
    pieces, slab_ref = refs[:PEERS], refs[PEERS]
    number = place()[1]
    part = pieces[0].shape[0]
    for step, piece in enumerate(pieces):
        at = pl.multiple_of(got_from(number, step) * part, part)
        slab_ref[pl.ds(at, part), :] = piece[...]


def gather(pieces):
    rows, width = pieces[0].shape
    return pl.pallas_call(
        gather_kernel,
        out_shape=jax.ShapeDtypeStruct((PEERS * rows, width), jnp.bfloat16),
        in_specs=[VMEM] * PEERS,
        out_specs=VMEM,
        compiler_params=SMALL,
    )(*pieces)


def cut_kernel(q_ref, *pieces):
    number = place()[1]
    part = q_ref.shape[0] // 2
    for step, piece in enumerate(pieces):
        peer = sent_to(number, step)
        rows = pl.ds(pl.multiple_of((peer & 1) * part, part), part)
        lanes = pl.ds(pl.multiple_of((peer >> 1) * WIDE, HD), WIDE)
        piece[...] = q_ref[rows, lanes]


def cut(q):
    return pl.pallas_call(
        cut_kernel,
        out_shape=[jax.ShapeDtypeStruct((q.shape[0] // 2, WIDE), jnp.bfloat16)] * PEERS,
        in_specs=[VMEM],
        out_specs=[VMEM] * PEERS,
        compiler_params=SMALL,
    )(q)


def join_kernel(*refs):
    pieces, out_ref, sems = refs[:PEERS], refs[PEERS], refs[PEERS + 1]
    number = place()[1]
    part = out_ref.shape[0] // 2
    copies = []
    for step, piece in enumerate(pieces):
        peer = got_from(number, step)
        rows = pl.ds(pl.multiple_of((peer & 1) * part, part), part)
        lanes = pl.ds(pl.multiple_of((peer >> 1) * WIDE, HD), WIDE)
        copies.append(pltpu.make_async_copy(piece, out_ref.at[rows, lanes], sems.at[step]))
        copies[-1].start()
    for copy in copies:
        copy.wait()


def join(pieces):
    return pl.pallas_call(
        join_kernel,
        out_shape=jax.ShapeDtypeStruct((2 * pieces[0].shape[0], HQ * HD), jnp.bfloat16),
        in_specs=[VMEM] * PEERS,
        out_specs=HBM,
        scratch_shapes=[pltpu.SemaphoreType.DMA((PEERS,))],
        compiler_params=SMALL,
    )(*pieces)


def attend_kernel(backs, first, final, table_ref, factor_ref, *refs):
    refs = list(refs)
    if first:
        q_pieces = [refs.pop(0) for _ in range(PEERS)]
    else:
        q_ref = refs.pop(0)
        del refs[:2]
    slabs = [(refs.pop(0), refs.pop(0)) for _ in backs]
    out_refs = [refs.pop(0) for _ in range(PEERS)] if final else None
    sums_ref, top_ref = refs.pop(0), refs.pop(0)
    number = place()[1]
    core = number & 1
    if first:
        q_ref = refs.pop(0)
        for step, piece in enumerate(q_pieces):
            q_ref[got_from(number, step)] = piece[...]
        sums_ref[...] = jnp.zeros_like(sums_ref)
        top_ref[...] = jnp.full_like(top_ref, LOW)
    key_ref, value_ref = refs[:2]
    piece = q_ref.shape[1]
    half = slabs[0][0].shape[0] // 2
    group = GROUP // 2
    chains = [(block, g) for block in range(2) for g in range(2)]

    block_rows = 2 * piece
    index = lax.broadcasted_iota(jnp.int32, (block_rows, HD), 0)
    own_part = index < piece
    token = 2 * block_rows + index + jnp.where(own_part, core * piece, -(core * piece))
    for slab, back in zip(slabs, backs):
        for x in range(2):
            count = jnp.maximum(table_ref[4 * back + 2 * x], table_ref[4 * back + 2 * x + 1])
            at = x * half
            spare = slab[0][at : at + 16, :HD].astype(jnp.float32)[0:1]
            parts = [ref[at : at + block_rows, :] for ref in slab]
            for n in range(2, 4):
                low = at + n * piece
                parts.append(jnp.concatenate([ref[low : low + piece, :] for ref in slab], axis=0))
            for n, values in enumerate(parts):
                to = slice(n * block_rows, (n + 1) * block_rows)
                keys = values[:, :HD].astype(jnp.float32)
                values = values[:, HD:]
                ones = jnp.ones_like(values)
                if n >= 2:
                    keep = token + (n - 2) * block_rows < count
                    keys = jnp.where(keep, keys, spare)
                    values = jnp.where(keep, values.astype(jnp.float32), 0.0).astype(jnp.bfloat16)
                    ones = jnp.where(keep, 1.0, 0.0).astype(jnp.bfloat16)
                key_ref[x, :, to] = jnp.transpose(keys).astype(jnp.bfloat16)
                value_ref[x, to, :HD] = values
                value_ref[x, to, HD:] = ones

        @pl.loop(0, 4)
        def _(turn):
            x = turn >> 1
            side = turn & 1

            count = table_ref[4 * back + turn]

            def visit(width):
                keys = key_ref[x, :, :width]
                values = value_ref[x, :width, :]

                def scores(block, g):
                    rows = []
                    for i in range(group):
                        lanes = slice((g * group + i) * HD, (g * group + i + 1) * HD)
                        for t in range(2):
                            rows.append(q_ref[4 * side + 2 * block + t, :, lanes])
                    return jnp.dot(jnp.concatenate(rows, axis=0), keys, preferred_element_type=jnp.float32)

                ready = scores(*chains[0])
                for n, (block, g) in enumerate(chains):
                    s = ready
                    if n + 1 < len(chains):
                        ready = scores(*chains[n + 1])
                    step = s.shape[0] // group
                    s = jnp.concatenate(
                        [
                            s[i * step : (i + 1) * step] * factor_ref[side * GROUP + g * group + i]
                            for i in range(group)
                        ],
                        axis=0,
                    )
                    chain = 2 * block + g
                    old_top = top_ref[side, chain]
                    top = jnp.maximum(old_top, jnp.max(s, axis=1, keepdims=True))
                    weight = jnp.concatenate(
                        [jnp.exp2(s[:, at : at + HD] - top).astype(jnp.bfloat16) for at in range(0, s.shape[1], HD)],
                        axis=1,
                    )
                    sums = jnp.dot(weight, values, preferred_element_type=jnp.float32)
                    shrink = jnp.exp2(old_top - top)
                    sums_ref[side, chain] = sums + sums_ref[side, chain] * jnp.concatenate([shrink, shrink], axis=1)
                    top_ref[side, chain] = top

            most = 3 * block_rows
            pl.when((count > 0) & (count <= most))(lambda: visit(most))
            pl.when(count > most)(lambda: visit(most + block_rows))

    if final:
        done_ref = refs[2]
        for side in range(2):
            for block, g in chains:
                sums = sums_ref[side, 2 * block + g]
                result = (sums[:, :HD] / sums[:, HD:]).astype(jnp.bfloat16)
                for i in range(group):
                    lanes = slice((g * group + i) * HD, (g * group + i + 1) * HD)
                    for t in range(2):
                        at = (2 * i + t) * piece
                        done_ref[4 * side + 2 * block + t, :, lanes] = result[at : at + piece]
        for step, out_ref in enumerate(out_refs):
            out_ref[...] = done_ref[sent_to(number, step)]


def attend(tables, q, state, slabs, backs, final):
    first = state is None
    piece = q[0].shape[-2]
    tall = GROUP * piece
    tokens = slabs[0][0].shape[0]
    q_shape = (PEERS, piece, WIDE)
    out_shape = [
        jax.ShapeDtypeStruct((2, 4, tall, 2 * HD), jnp.float32),
        jax.ShapeDtypeStruct((2, 4, tall, HD), jnp.float32),
    ]
    scratch = [pltpu.VMEM((2, HD, tokens), jnp.bfloat16), pltpu.VMEM((2, tokens, 2 * HD), jnp.bfloat16)]
    if final:
        out_shape = [jax.ShapeDtypeStruct(q_shape[1:], jnp.bfloat16)] * PEERS + out_shape
        scratch.append(pltpu.VMEM(q_shape, jnp.bfloat16))
    if first:
        out_shape.append(jax.ShapeDtypeStruct(q_shape, jnp.bfloat16))
    work = len(backs) * PEERS * tall * tokens
    inputs = [*q, *(state or ()), *[a for slab in slabs for a in slab]]
    aliases = {} if first else {3: PEERS * final, 4: PEERS * final + 1}
    return pl.pallas_call(
        functools.partial(attend_kernel, backs, first, final),
        out_shape=out_shape,
        in_specs=[SMEM] * 2 + [VMEM] * len(inputs),
        out_specs=[VMEM] * len(out_shape),
        scratch_shapes=scratch,
        input_output_aliases=aliases,
        compiler_params=LARGE,
        cost_estimate=pl.CostEstimate(flops=2 * work * HD, bytes_accessed=4 * PEERS * piece * WIDE, transcendentals=work // 2),
    )(*tables, *inputs)


def per_device(spans, ctx, queries, keys, values, temps, levels, ctx_list, counts):
    other_core = [(t, t ^ 1) for t in range(ctx)]
    last = spans // 2 - 1

    def exchange(pieces):
        moved = [pieces[0]]
        for piece, step in zip(pieces[1:], STEPS[1:]):
            moved.append(lax.ppermute(piece, ("span", "ctx"), [(f, f ^ step[f % 2]) for f in range(spans * ctx)]))
        return moved

    def up(a, steps):
        return lax.ppermute(a, "span", [(s, (s + 2 * steps) % spans) for s in range(spans)])

    def near(a):
        return lax.ppermute(a, "ctx", other_core)

    own = gather(exchange(begin(keys, values)))
    slabs = {0: own, 1: up(own, 1), last: up(own, last)}
    others = {0: near(own)}
    others, queries = lax.optimization_barrier((others, queries))
    q = exchange(cut(queries))
    tables = tabulate(spans // 2, levels, temps, jnp.transpose(ctx_list), counts)
    slabs, others, q, tables = lax.optimization_barrier((slabs, others, q, tables))
    others |= {back: near(slabs[back]) for back in (1, last)}
    stage = sorted(slabs)
    state = None
    for back in range(2, last):
        slabs[back] = up(slabs[back - 1], 1)
        *state, q_all = [*attend(tables, q, state, [(slabs[b], others[b]) for b in stage], stage, False), *q][:3]
        q = [q_all]
        slabs[back], state = lax.optimization_barrier((slabs[back], state))
        others[back] = near(slabs[back])
        stage = [back]
    out = attend(tables, q, state, [(slabs[b], others[b]) for b in stage], stage, True)
    return join(exchange(out[:PEERS]))


def solution(mesh):
    return jax.shard_map(
        functools.partial(per_device, mesh.shape["span"], mesh.shape["ctx"]),
        mesh=mesh,
        in_specs=(
            P(("span", "ctx"), None),
            P(("span", "ctx"), None),
            P(("span", "ctx"), None),
            P(),
            P(),
            P(),
            P(),
        ),
        out_specs=P(("span", "ctx"), None),
        check_vma=False,
    )
```

```python
import functools
import math

import jax
import jax.numpy as jnp
from jax import lax
from jax.experimental import pallas as pl
from jax.experimental.pallas import tpu as pltpu
from jax.sharding import PartitionSpec as P

HQ = 24
KVH = 4
HD = 128
GROUP = HQ // KVH
WIDE = GROUP * HD
PEERS = 8
LOW = -1e30
SCALE = math.log2(math.e) / math.sqrt(HD)
SMEM = pl.BlockSpec(memory_space=pltpu.SMEM)
VMEM = pl.BlockSpec(memory_space=pltpu.VMEM)
HBM = pl.BlockSpec(memory_space=pltpu.HBM)
SMALL = pltpu.CompilerParams(vmem_limit_bytes=6 << 20)
LARGE = pltpu.CompilerParams(vmem_limit_bytes=16 << 20)


STEPS = ((0, 0), (6, 6), (7, 7), (4, 2), (2, 4), (5, 3), (3, 5), (1, 1))


def sent_to(number, step):
    even, odd = STEPS[step]
    return number ^ jnp.where(number & 1 == 0, even, odd)


def got_from(number, step):
    even, odd = STEPS[step]
    if even & 1:
        even, odd = odd, even
    return number ^ jnp.where(number & 1 == 0, even, odd)


def place():
    span, tok = lax.axis_index("span"), lax.axis_index("ctx")
    return span & -2, 4 * (span & 1) + tok


def table_kernel(planes, levels_ref, temps_ref, list_ref, counts_ref, table_ref, factor_ref):
    base, number = place()
    head = number >> 1
    for side in range(2):
        level = levels_ref[base + side]
        for i in range(GROUP):
            factor_ref[side * GROUP + i] = temps_ref[level, head * GROUP + i] * SCALE

        @pl.loop(0, 2 * planes)
        def _(slab):
            ident = base + (slab & 1) - 2 * (slab >> 1)
            found = base + side == ident
            for j in range(list_ref.shape[0]):
                found = found | (list_ref[j, base + side] == ident)
            count = jnp.where(found & (ident >= 0), counts_ref[jnp.maximum(ident, 0)], 0)
            table_ref[2 * slab + side] = count


def tabulate(planes, levels, temps, ctx_list, counts):
    return pl.pallas_call(
        functools.partial(table_kernel, planes),
        out_shape=[jax.ShapeDtypeStruct((4 * planes,), jnp.int32), jax.ShapeDtypeStruct((2 * GROUP,), jnp.float32)],
        in_specs=[SMEM] * 4,
        out_specs=[SMEM] * 2,
        compiler_params=SMALL,
    )(levels, temps, ctx_list, counts)


def begin_kernel(keys_ref, values_ref, *refs):
    pieces, (source, target, sems) = refs[:PEERS], refs[PEERS:]
    number = place()[1]
    loads = [pltpu.make_async_copy(ref, source.at[i], sems.at[i]) for i, ref in enumerate((keys_ref, values_ref))]
    for load in loads:
        load.start()
    for load in loads:
        load.wait()
    part = target.shape[1]
    stores = []
    for step, piece in enumerate(pieces):
        peer = sent_to(number, step)
        rows = pl.ds(pl.multiple_of((peer & 1) * part, part), part)
        lanes = pl.ds(pl.multiple_of((peer >> 1) * HD, HD), HD)
        target[step, :, :HD] = source[0, rows, lanes]
        target[step, :, HD:] = source[1, rows, lanes]
        stores.append(pltpu.make_async_copy(target.at[step], piece, sems.at[step]))
        stores[-1].start()
    for store in stores:
        store.wait()


def begin(keys, values):
    shape = (keys.shape[0] // 2, 2 * HD)
    return pl.pallas_call(
        begin_kernel,
        out_shape=[jax.ShapeDtypeStruct(shape, jnp.bfloat16)] * PEERS,
        in_specs=[HBM] * 2,
        out_specs=[HBM] * PEERS,
        scratch_shapes=[
            pltpu.VMEM((2, *keys.shape), jnp.bfloat16),
            pltpu.VMEM((PEERS, *shape), jnp.bfloat16),
            pltpu.SemaphoreType.DMA((PEERS,)),
        ],
    )(keys, values)


def gather_kernel(*refs):
    pieces, slab_ref = refs[:PEERS], refs[PEERS]
    number = place()[1]
    part = pieces[0].shape[0]
    for step, piece in enumerate(pieces):
        at = pl.multiple_of(got_from(number, step) * part, part)
        slab_ref[pl.ds(at, part), :] = piece[...]


def gather(pieces):
    rows, width = pieces[0].shape
    return pl.pallas_call(
        gather_kernel,
        out_shape=jax.ShapeDtypeStruct((PEERS * rows, width), jnp.bfloat16),
        in_specs=[VMEM] * PEERS,
        out_specs=VMEM,
        compiler_params=SMALL,
    )(*pieces)


def cut_kernel(q_ref, *pieces):
    number = place()[1]
    part = q_ref.shape[0] // 2
    for step, piece in enumerate(pieces):
        peer = sent_to(number, step)
        rows = pl.ds(pl.multiple_of((peer & 1) * part, part), part)
        lanes = pl.ds(pl.multiple_of((peer >> 1) * WIDE, HD), WIDE)
        piece[...] = q_ref[rows, lanes]


def cut(q):
    return pl.pallas_call(
        cut_kernel,
        out_shape=[jax.ShapeDtypeStruct((q.shape[0] // 2, WIDE), jnp.bfloat16)] * PEERS,
        in_specs=[VMEM],
        out_specs=[VMEM] * PEERS,
        compiler_params=SMALL,
    )(q)


def join_kernel(*refs):
    pieces, out_ref, sems = refs[:PEERS], refs[PEERS], refs[PEERS + 1]
    number = place()[1]
    part = out_ref.shape[0] // 2
    copies = []
    for step, piece in enumerate(pieces):
        peer = got_from(number, step)
        rows = pl.ds(pl.multiple_of((peer & 1) * part, part), part)
        lanes = pl.ds(pl.multiple_of((peer >> 1) * WIDE, HD), WIDE)
        copies.append(pltpu.make_async_copy(piece, out_ref.at[rows, lanes], sems.at[step]))
        copies[-1].start()
    for copy in copies:
        copy.wait()


def join(pieces):
    return pl.pallas_call(
        join_kernel,
        out_shape=jax.ShapeDtypeStruct((2 * pieces[0].shape[0], HQ * HD), jnp.bfloat16),
        in_specs=[VMEM] * PEERS,
        out_specs=HBM,
        scratch_shapes=[pltpu.SemaphoreType.DMA((PEERS,))],
        compiler_params=SMALL,
    )(*pieces)


def attend_kernel(backs, first, final, table_ref, factor_ref, *refs):
    refs = list(refs)
    if first:
        q_pieces = [refs.pop(0) for _ in range(PEERS)]
    else:
        q_ref = refs.pop(0)
        del refs[:2]
    slabs = [(refs.pop(0), refs.pop(0)) for _ in backs]
    out_refs = [refs.pop(0) for _ in range(PEERS)] if final else None
    sums_ref, top_ref = refs.pop(0), refs.pop(0)
    number = place()[1]
    core = number & 1
    if first:
        q_ref = refs.pop(0)
        for step, piece in enumerate(q_pieces):
            q_ref[got_from(number, step)] = piece[...]
        sums_ref[...] = jnp.zeros_like(sums_ref)
        top_ref[...] = jnp.full_like(top_ref, LOW)
    key_ref, value_ref = refs[:2]
    piece = q_ref.shape[1]
    half = slabs[0][0].shape[0] // 2
    group = GROUP // 2
    chains = [(block, g) for block in range(2) for g in range(2)]

    block_rows = 2 * piece
    index = lax.broadcasted_iota(jnp.int32, (block_rows, HD), 0)
    own_part = index < piece
    token = 2 * block_rows + index + jnp.where(own_part, core * piece, -(core * piece))
    for slab, back in zip(slabs, backs):
        for x in range(2):
            count = jnp.maximum(table_ref[4 * back + 2 * x], table_ref[4 * back + 2 * x + 1])
            at = x * half
            spare = slab[0][at : at + 16, :HD].astype(jnp.float32)[0:1]
            parts = [ref[at : at + block_rows, :] for ref in slab]
            for n in range(2, 4):
                low = at + n * piece
                parts.append(jnp.concatenate([ref[low : low + piece, :] for ref in slab], axis=0))
            for n, values in enumerate(parts):
                to = slice(n * block_rows, (n + 1) * block_rows)
                keys = values[:, :HD].astype(jnp.float32)
                values = values[:, HD:]
                ones = jnp.ones_like(values)
                if n >= 2:
                    keep = token + (n - 2) * block_rows < count
                    keys = jnp.where(keep, keys, spare)
                    values = jnp.where(keep, values.astype(jnp.float32), 0.0).astype(jnp.bfloat16)
                    ones = jnp.where(keep, 1.0, 0.0).astype(jnp.bfloat16)
                key_ref[x, :, to] = jnp.transpose(keys).astype(jnp.bfloat16)
                value_ref[x, to, :HD] = values
                value_ref[x, to, HD:] = ones

        @pl.loop(0, 4)
        def _(turn):
            x = turn >> 1
            side = turn & 1

            count = table_ref[4 * back + turn]

            def visit(width):
                keys = key_ref[x, :, :width]
                values = value_ref[x, :width, :]

                def scores(block, g):
                    rows = []
                    for i in range(group):
                        lanes = slice((g * group + i) * HD, (g * group + i + 1) * HD)
                        for t in range(2):
                            rows.append(q_ref[4 * side + 2 * block + t, :, lanes])
                    return jnp.dot(jnp.concatenate(rows, axis=0), keys, preferred_element_type=jnp.float32)

                ready = scores(*chains[0])
                for n, (block, g) in enumerate(chains):
                    s = ready
                    if n + 1 < len(chains):
                        ready = scores(*chains[n + 1])
                    step = s.shape[0] // group
                    s = jnp.concatenate(
                        [
                            s[i * step : (i + 1) * step] * factor_ref[side * GROUP + g * group + i]
                            for i in range(group)
                        ],
                        axis=0,
                    )
                    chain = 2 * block + g
                    old_top = top_ref[side, chain]
                    top = jnp.maximum(old_top, jnp.max(s, axis=1, keepdims=True))
                    weight = jnp.concatenate(
                        [jnp.exp2(s[:, at : at + HD] - top).astype(jnp.bfloat16) for at in range(0, s.shape[1], HD)],
                        axis=1,
                    )
                    sums = jnp.dot(weight, values, preferred_element_type=jnp.float32)
                    shrink = jnp.exp2(old_top - top)
                    sums_ref[side, chain] = sums + sums_ref[side, chain] * jnp.concatenate([shrink, shrink], axis=1)
                    top_ref[side, chain] = top

            most = 3 * block_rows
            pl.when((count > 0) & (count <= most))(lambda: visit(most))
            pl.when(count > most)(lambda: visit(most + block_rows))

    if final:
        done_ref = refs[2]
        for side in range(2):
            for block, g in chains:
                sums = sums_ref[side, 2 * block + g]
                result = (sums[:, :HD] / sums[:, HD:]).astype(jnp.bfloat16)
                for i in range(group):
                    lanes = slice((g * group + i) * HD, (g * group + i + 1) * HD)
                    for t in range(2):
                        at = (2 * i + t) * piece
                        done_ref[4 * side + 2 * block + t, :, lanes] = result[at : at + piece]
        for step, out_ref in enumerate(out_refs):
            out_ref[...] = done_ref[sent_to(number, step)]


def attend(tables, q, state, slabs, backs, final):
    first = state is None
    piece = q[0].shape[-2]
    tall = GROUP * piece
    tokens = slabs[0][0].shape[0]
    q_shape = (PEERS, piece, WIDE)
    out_shape = [
        jax.ShapeDtypeStruct((2, 4, tall, 2 * HD), jnp.float32),
        jax.ShapeDtypeStruct((2, 4, tall, HD), jnp.float32),
    ]
    scratch = [pltpu.VMEM((2, HD, tokens), jnp.bfloat16), pltpu.VMEM((2, tokens, 2 * HD), jnp.bfloat16)]
    if final:
        out_shape = [jax.ShapeDtypeStruct(q_shape[1:], jnp.bfloat16)] * PEERS + out_shape
        scratch.append(pltpu.VMEM(q_shape, jnp.bfloat16))
    if first:
        out_shape.append(jax.ShapeDtypeStruct(q_shape, jnp.bfloat16))
    work = len(backs) * PEERS * tall * tokens
    inputs = [*q, *(state or ()), *[a for slab in slabs for a in slab]]
    aliases = {} if first else {3: PEERS * final, 4: PEERS * final + 1}
    return pl.pallas_call(
        functools.partial(attend_kernel, backs, first, final),
        out_shape=out_shape,
        in_specs=[SMEM] * 2 + [VMEM] * len(inputs),
        out_specs=[VMEM] * len(out_shape),
        scratch_shapes=scratch,
        input_output_aliases=aliases,
        compiler_params=LARGE,
        cost_estimate=pl.CostEstimate(flops=2 * work * HD, bytes_accessed=4 * PEERS * piece * WIDE, transcendentals=work // 2),
    )(*tables, *inputs)


def per_device(spans, ctx, queries, keys, values, temps, levels, ctx_list, counts):
    other_core = [(t, t ^ 1) for t in range(ctx)]
    last = spans // 2 - 1

    def exchange(pieces):
        moved = [pieces[0]]
        for piece, step in zip(pieces[1:], STEPS[1:]):
            moved.append(lax.ppermute(piece, ("span", "ctx"), [(f, f ^ step[f % 2]) for f in range(spans * ctx)]))
        return moved

    def up(a, steps):
        return lax.ppermute(a, "span", [(s, (s + 2 * steps) % spans) for s in range(spans)])

    def near(a):
        return lax.ppermute(a, "ctx", other_core)

    tables = tabulate(spans // 2, levels, temps, jnp.transpose(ctx_list), counts)
    kv, tables = lax.optimization_barrier((exchange(begin(keys, values)), tables))
    own = gather(kv)
    slabs = {0: own, 1: up(own, 1), last: up(own, last)}
    others = {0: near(own)}
    others, queries = lax.optimization_barrier((others, queries))
    q = exchange(cut(queries))
    others |= {back: near(slabs[back]) for back in (1, last)}
    slabs, others, q = lax.optimization_barrier((slabs, others, q))
    stage = sorted(slabs)
    state = None
    for back in range(2, last):
        slabs[back] = up(slabs[back - 1], 1)
        *state, q_all = [*attend(tables, q, state, [(slabs[b], others[b]) for b in stage], stage, False), *q][:3]
        q = [q_all]
        slabs[back], state = lax.optimization_barrier((slabs[back], state))
        others[back] = near(slabs[back])
        stage = [back]
    out = attend(tables, q, state, [(slabs[b], others[b]) for b in stage], stage, True)
    return join(exchange(out[:PEERS]))


def solution(mesh):
    return jax.shard_map(
        functools.partial(per_device, mesh.shape["span"], mesh.shape["ctx"]),
        mesh=mesh,
        in_specs=(
            P(("span", "ctx"), None),
            P(("span", "ctx"), None),
            P(("span", "ctx"), None),
            P(),
            P(),
            P(),
            P(),
        ),
        out_specs=P(("span", "ctx"), None),
        check_vma=False,
    )
```

```python
import functools
import math

import jax
import jax.numpy as jnp
from jax import lax
from jax.experimental import pallas as pl
from jax.experimental.pallas import tpu as pltpu
from jax.sharding import PartitionSpec as P

HQ = 24
KVH = 4
HD = 128
GROUP = HQ // KVH
WIDE = GROUP * HD
PEERS = 8
LOW = -1e30
SCALE = math.log2(math.e) / math.sqrt(HD)
SMEM = pl.BlockSpec(memory_space=pltpu.SMEM)
VMEM = pl.BlockSpec(memory_space=pltpu.VMEM)
HBM = pl.BlockSpec(memory_space=pltpu.HBM)
SMALL = pltpu.CompilerParams(vmem_limit_bytes=6 << 20)
LARGE = pltpu.CompilerParams(vmem_limit_bytes=16 << 20)


STEPS = ((0, 0), (6, 6), (7, 7), (4, 2), (2, 4), (5, 3), (3, 5), (1, 1))


def sent_to(number, step):
    even, odd = STEPS[step]
    return number ^ jnp.where(number & 1 == 0, even, odd)


def got_from(number, step):
    even, odd = STEPS[step]
    if even & 1:
        even, odd = odd, even
    return number ^ jnp.where(number & 1 == 0, even, odd)


def place():
    span, tok = lax.axis_index("span"), lax.axis_index("ctx")
    return span & -2, 4 * (span & 1) + tok


def begin_kernel(planes, levels_ref, temps_ref, list_ref, counts_ref, keys_ref, values_ref, q_ref, *refs):
    pieces, (table_ref, factor_ref, source, q_source, target, sems) = refs[:PEERS], refs[PEERS:]
    loads = [pltpu.make_async_copy(ref, source.at[i], sems.at[i]) for i, ref in enumerate((keys_ref, values_ref))]
    loads.append(pltpu.make_async_copy(q_ref, q_source, sems.at[2]))
    for load in loads:
        load.start()
    base, number = place()
    head = number >> 1
    for side in range(2):
        level = levels_ref[base + side]
        for i in range(GROUP):
            factor_ref[side * GROUP + i] = temps_ref[level, head * GROUP + i] * SCALE

        @pl.loop(0, 2 * planes)
        def _(slab):
            ident = base + (slab & 1) - 2 * (slab >> 1)
            found = base + side == ident
            for j in range(list_ref.shape[0]):
                found = found | (list_ref[j, base + side] == ident)
            count = jnp.where(found & (ident >= 0), counts_ref[jnp.maximum(ident, 0)], 0)
            table_ref[2 * slab + side] = count

    for load in loads:
        load.wait()
    part = target.shape[1]
    stores = []
    for step, piece in enumerate(pieces):
        peer = sent_to(number, step)
        rows = pl.ds(pl.multiple_of((peer & 1) * part, part), part)
        lanes = pl.ds(pl.multiple_of((peer >> 1) * HD, HD), HD)
        target[step, :, :HD] = source[0, rows, lanes]
        target[step, :, HD : 2 * HD] = source[1, rows, lanes]
        target[step, :, 2 * HD :] = q_source[rows, pl.ds(pl.multiple_of((peer >> 1) * WIDE, HD), WIDE)]
        stores.append(pltpu.make_async_copy(target.at[step], piece, sems.at[step]))
        stores[-1].start()
    for store in stores:
        store.wait()


def begin(planes, levels, temps, ctx_list, counts, keys, values, queries):
    shape = (keys.shape[0] // 2, 2 * HD + WIDE)
    out = pl.pallas_call(
        functools.partial(begin_kernel, planes),
        out_shape=[jax.ShapeDtypeStruct(shape, jnp.bfloat16)] * PEERS
        + [jax.ShapeDtypeStruct((4 * planes,), jnp.int32), jax.ShapeDtypeStruct((2 * GROUP,), jnp.float32)],
        in_specs=[SMEM] * 4 + [HBM] * 3,
        out_specs=[HBM] * PEERS + [SMEM] * 2,
        scratch_shapes=[
            pltpu.VMEM((2, *keys.shape), jnp.bfloat16),
            pltpu.VMEM(queries.shape, jnp.bfloat16),
            pltpu.VMEM((PEERS, *shape), jnp.bfloat16),
            pltpu.SemaphoreType.DMA((PEERS,)),
        ],
    )(levels, temps, ctx_list, counts, keys, values, queries)
    return out[:PEERS], out[PEERS:]


def gather_kernel(*refs):
    pieces, slab_ref, q_ref = refs[:PEERS], refs[PEERS], refs[PEERS + 1]
    number = place()[1]
    part = pieces[0].shape[0]
    for step, piece in enumerate(pieces):
        peer = got_from(number, step)
        slab_ref[pl.ds(pl.multiple_of(peer * part, part), part), :] = piece[:, : 2 * HD]
        q_ref[peer] = piece[:, 2 * HD :]


def gather(pieces):
    rows = pieces[0].shape[0]
    return pl.pallas_call(
        gather_kernel,
        out_shape=[
            jax.ShapeDtypeStruct((PEERS * rows, 2 * HD), jnp.bfloat16),
            jax.ShapeDtypeStruct((PEERS, rows, WIDE), jnp.bfloat16),
        ],
        in_specs=[VMEM] * PEERS,
        out_specs=[VMEM] * 2,
        compiler_params=SMALL,
    )(*pieces)


def join_kernel(*refs):
    pieces, out_ref, sems = refs[:PEERS], refs[PEERS], refs[PEERS + 1]
    number = place()[1]
    part = out_ref.shape[0] // 2
    copies = []
    for step, piece in enumerate(pieces):
        peer = got_from(number, step)
        rows = pl.ds(pl.multiple_of((peer & 1) * part, part), part)
        lanes = pl.ds(pl.multiple_of((peer >> 1) * WIDE, HD), WIDE)
        copies.append(pltpu.make_async_copy(piece, out_ref.at[rows, lanes], sems.at[step]))
        copies[-1].start()
    for copy in copies:
        copy.wait()


def join(pieces):
    return pl.pallas_call(
        join_kernel,
        out_shape=jax.ShapeDtypeStruct((2 * pieces[0].shape[0], HQ * HD), jnp.bfloat16),
        in_specs=[VMEM] * PEERS,
        out_specs=HBM,
        scratch_shapes=[pltpu.SemaphoreType.DMA((PEERS,))],
        compiler_params=SMALL,
    )(*pieces)


def attend_kernel(backs, first, final, table_ref, factor_ref, *refs):
    refs = list(refs)
    q_ref = refs.pop(0)
    if not first:
        del refs[:2]
    slabs = [(refs.pop(0), refs.pop(0)) for _ in backs]
    out_refs = [refs.pop(0) for _ in range(PEERS)] if final else None
    sums_ref, top_ref = refs.pop(0), refs.pop(0)
    number = place()[1]
    core = number & 1
    if first:
        sums_ref[...] = jnp.zeros_like(sums_ref)
        top_ref[...] = jnp.full_like(top_ref, LOW)
    key_ref, value_ref = refs[:2]
    piece = q_ref.shape[1]
    half = slabs[0][0].shape[0] // 2
    group = GROUP // 2
    chains = [(block, g) for block in range(2) for g in range(2)]

    block_rows = 2 * piece
    index = lax.broadcasted_iota(jnp.int32, (block_rows, HD), 0)
    own_part = index < piece
    token = 2 * block_rows + index + jnp.where(own_part, core * piece, -(core * piece))
    for slab, back in zip(slabs, backs):
        for x in range(2):
            count = jnp.maximum(table_ref[4 * back + 2 * x], table_ref[4 * back + 2 * x + 1])
            at = x * half
            spare = slab[0][at : at + 16, :HD].astype(jnp.float32)[0:1]
            parts = [ref[at : at + block_rows, :] for ref in slab]
            for n in range(2, 4):
                low = at + n * piece
                parts.append(jnp.concatenate([ref[low : low + piece, :] for ref in slab], axis=0))
            for n, values in enumerate(parts):
                to = slice(n * block_rows, (n + 1) * block_rows)
                keys = values[:, :HD].astype(jnp.float32)
                values = values[:, HD:]
                ones = jnp.ones_like(values)
                if n >= 2:
                    keep = token + (n - 2) * block_rows < count
                    keys = jnp.where(keep, keys, spare)
                    values = jnp.where(keep, values.astype(jnp.float32), 0.0).astype(jnp.bfloat16)
                    ones = jnp.where(keep, 1.0, 0.0).astype(jnp.bfloat16)
                key_ref[x, :, to] = jnp.transpose(keys).astype(jnp.bfloat16)
                value_ref[x, to, :HD] = values
                value_ref[x, to, HD:] = ones

        @pl.loop(0, 4)
        def _(turn):
            x = turn >> 1
            side = turn & 1

            count = table_ref[4 * back + turn]

            def visit(width):
                keys = key_ref[x, :, :width]
                values = value_ref[x, :width, :]

                def scores(block, g):
                    rows = []
                    for i in range(group):
                        lanes = slice((g * group + i) * HD, (g * group + i + 1) * HD)
                        for t in range(2):
                            rows.append(q_ref[4 * side + 2 * block + t, :, lanes])
                    return jnp.dot(jnp.concatenate(rows, axis=0), keys, preferred_element_type=jnp.float32)

                ready = scores(*chains[0])
                for n, (block, g) in enumerate(chains):
                    s = ready
                    if n + 1 < len(chains):
                        ready = scores(*chains[n + 1])
                    step = s.shape[0] // group
                    s = jnp.concatenate(
                        [
                            s[i * step : (i + 1) * step] * factor_ref[side * GROUP + g * group + i]
                            for i in range(group)
                        ],
                        axis=0,
                    )
                    chain = 2 * block + g
                    old_top = top_ref[side, chain]
                    top = jnp.maximum(old_top, jnp.max(s, axis=1, keepdims=True))
                    weight = jnp.concatenate(
                        [jnp.exp2(s[:, at : at + HD] - top).astype(jnp.bfloat16) for at in range(0, s.shape[1], HD)],
                        axis=1,
                    )
                    sums = jnp.dot(weight, values, preferred_element_type=jnp.float32)
                    shrink = jnp.exp2(old_top - top)
                    sums_ref[side, chain] = sums + sums_ref[side, chain] * jnp.concatenate([shrink, shrink], axis=1)
                    top_ref[side, chain] = top

            most = 3 * block_rows
            pl.when((count > 0) & (count <= most))(lambda: visit(most))
            pl.when(count > most)(lambda: visit(most + block_rows))

    if final:
        done_ref = refs[2]
        for side in range(2):
            for block, g in chains:
                sums = sums_ref[side, 2 * block + g]
                result = (sums[:, :HD] / sums[:, HD:]).astype(jnp.bfloat16)
                for i in range(group):
                    lanes = slice((g * group + i) * HD, (g * group + i + 1) * HD)
                    for t in range(2):
                        at = (2 * i + t) * piece
                        done_ref[4 * side + 2 * block + t, :, lanes] = result[at : at + piece]
        for step, out_ref in enumerate(out_refs):
            out_ref[...] = done_ref[sent_to(number, step)]


def attend(tables, q, state, slabs, backs, final):
    first = state is None
    piece = q.shape[1]
    tall = GROUP * piece
    tokens = slabs[0][0].shape[0]
    out_shape = [
        jax.ShapeDtypeStruct((2, 4, tall, 2 * HD), jnp.float32),
        jax.ShapeDtypeStruct((2, 4, tall, HD), jnp.float32),
    ]
    scratch = [pltpu.VMEM((2, HD, tokens), jnp.bfloat16), pltpu.VMEM((2, tokens, 2 * HD), jnp.bfloat16)]
    if final:
        out_shape = [jax.ShapeDtypeStruct(q.shape[1:], jnp.bfloat16)] * PEERS + out_shape
        scratch.append(pltpu.VMEM(q.shape, jnp.bfloat16))
    work = len(backs) * PEERS * tall * tokens
    inputs = [q, *(state or ()), *[a for slab in slabs for a in slab]]
    aliases = {} if first else {3: PEERS * final, 4: PEERS * final + 1}
    return pl.pallas_call(
        functools.partial(attend_kernel, backs, first, final),
        out_shape=out_shape,
        in_specs=[SMEM] * 2 + [VMEM] * len(inputs),
        out_specs=[VMEM] * len(out_shape),
        scratch_shapes=scratch,
        input_output_aliases=aliases,
        compiler_params=LARGE,
        cost_estimate=pl.CostEstimate(flops=2 * work * HD, bytes_accessed=4 * q.size, transcendentals=work // 2),
    )(*tables, *inputs)


def per_device(spans, ctx, queries, keys, values, temps, levels, ctx_list, counts):
    other_core = [(t, t ^ 1) for t in range(ctx)]
    last = spans // 2 - 1

    def exchange(pieces):
        moved = [pieces[0]]
        for piece, step in zip(pieces[1:], STEPS[1:]):
            moved.append(lax.ppermute(piece, ("span", "ctx"), [(f, f ^ step[f % 2]) for f in range(spans * ctx)]))
        return moved

    def up(a, steps):
        return lax.ppermute(a, "span", [(s, (s + 2 * steps) % spans) for s in range(spans)])

    def near(a):
        return lax.ppermute(a, "ctx", other_core)

    pieces, tables = begin(spans // 2, levels, temps, jnp.transpose(ctx_list), counts, keys, values, queries)
    own, q = gather(exchange(pieces))
    slabs = {0: own, 1: up(own, 1), last: up(own, last)}
    others = {0: near(own)}
    state = attend(tables, q, None, [(own, others[0])], [0], False)
    slabs, state = lax.optimization_barrier((slabs, state))
    stage = [1, last]
    others |= {back: near(slabs[back]) for back in stage}
    for back in range(2, last):
        slabs[back] = up(slabs[back - 1], 1)
        state = attend(tables, q, state, [(slabs[b], others[b]) for b in stage], stage, False)
        slabs[back], state = lax.optimization_barrier((slabs[back], state))
        others[back] = near(slabs[back])
        stage = [back]
    out = attend(tables, q, state, [(slabs[b], others[b]) for b in stage], stage, True)
    return join(exchange(out[:PEERS]))


def solution(mesh):
    return jax.shard_map(
        functools.partial(per_device, mesh.shape["span"], mesh.shape["ctx"]),
        mesh=mesh,
        in_specs=(
            P(("span", "ctx"), None),
            P(("span", "ctx"), None),
            P(("span", "ctx"), None),
            P(),
            P(),
            P(),
            P(),
        ),
        out_specs=P(("span", "ctx"), None),
        check_vma=False,
    )
```

```python
import functools
import math

import jax
import jax.numpy as jnp
from jax import lax
from jax.experimental import pallas as pl
from jax.experimental.pallas import tpu as pltpu
from jax.sharding import PartitionSpec as P

HQ = 24
KVH = 4
HD = 128
GROUP = HQ // KVH
WIDE = GROUP * HD
PEERS = 8
LOW = -1e30
SCALE = math.log2(math.e) / math.sqrt(HD)
SMEM = pl.BlockSpec(memory_space=pltpu.SMEM)
VMEM = pl.BlockSpec(memory_space=pltpu.VMEM)
HBM = pl.BlockSpec(memory_space=pltpu.HBM)
SMALL = pltpu.CompilerParams(vmem_limit_bytes=6 << 20)
LARGE = pltpu.CompilerParams(vmem_limit_bytes=16 << 20)


STEPS = ((0, 0), (1, 1), (6, 6), (7, 7), (4, 2), (2, 4), (5, 3), (3, 5))


def sent_to(number, step):
    even, odd = STEPS[step]
    return number ^ jnp.where(number & 1 == 0, even, odd)


def got_from(number, step):
    even, odd = STEPS[step]
    if even & 1:
        even, odd = odd, even
    return number ^ jnp.where(number & 1 == 0, even, odd)


def place():
    span, tok = lax.axis_index("span"), lax.axis_index("ctx")
    return span & -2, 4 * (span & 1) + tok


def table_kernel(planes, levels_ref, temps_ref, list_ref, counts_ref, table_ref, factor_ref):
    base, number = place()
    head = number >> 1
    for side in range(2):
        level = levels_ref[base + side]
        for i in range(GROUP):
            factor_ref[side * GROUP + i] = temps_ref[level, head * GROUP + i] * SCALE

        @pl.loop(0, 2 * planes)
        def _(slab):
            ident = base + (slab & 1) - 2 * (slab >> 1)
            found = base + side == ident
            for j in range(list_ref.shape[0]):
                found = found | (list_ref[j, base + side] == ident)
            count = jnp.where(found & (ident >= 0), counts_ref[jnp.maximum(ident, 0)], 0)
            table_ref[2 * slab + side] = count


def tabulate(planes, levels, temps, ctx_list, counts):
    return pl.pallas_call(
        functools.partial(table_kernel, planes),
        out_shape=[jax.ShapeDtypeStruct((4 * planes,), jnp.int32), jax.ShapeDtypeStruct((2 * GROUP,), jnp.float32)],
        in_specs=[SMEM] * 4,
        out_specs=[SMEM] * 2,
        compiler_params=SMALL,
    )(levels, temps, ctx_list, counts)


def begin_kernel(keys_ref, values_ref, q_ref, *refs):
    pieces, (source, q_source, target, sems) = refs[:PEERS], refs[PEERS:]
    loads = [pltpu.make_async_copy(ref, source.at[i], sems.at[i]) for i, ref in enumerate((keys_ref, values_ref))]
    loads.append(pltpu.make_async_copy(q_ref, q_source, sems.at[2]))
    for load in loads:
        load.start()
    number = place()[1]
    for load in loads:
        load.wait()
    part = target.shape[1]
    stores = []
    for step in [*range(1, PEERS), 0]:
        peer = sent_to(number, step)
        rows = pl.ds(pl.multiple_of((peer & 1) * part, part), part)
        lanes = pl.ds(pl.multiple_of((peer >> 1) * HD, HD), HD)
        target[step, :, :HD] = source[0, rows, lanes]
        target[step, :, HD : 2 * HD] = source[1, rows, lanes]
        target[step, :, 2 * HD :] = q_source[rows, pl.ds(pl.multiple_of((peer >> 1) * WIDE, HD), WIDE)]
        stores.append(pltpu.make_async_copy(target.at[step], pieces[step], sems.at[step]))
        stores[-1].start()
    for store in stores:
        store.wait()


def begin(keys, values, queries):
    shape = (keys.shape[0] // 2, 2 * HD + WIDE)
    return pl.pallas_call(
        begin_kernel,
        out_shape=[jax.ShapeDtypeStruct(shape, jnp.bfloat16)] * PEERS,
        in_specs=[HBM] * 3,
        out_specs=[HBM] * PEERS,
        scratch_shapes=[
            pltpu.VMEM((2, *keys.shape), jnp.bfloat16),
            pltpu.VMEM(queries.shape, jnp.bfloat16),
            pltpu.VMEM((PEERS, *shape), jnp.bfloat16),
            pltpu.SemaphoreType.DMA((PEERS,)),
        ],
    )(keys, values, queries)


def hold_kernel(piece_ref, out_ref):
    out_ref[...] = piece_ref[...]


def hold(piece):
    return pl.pallas_call(
        hold_kernel,
        out_shape=jax.ShapeDtypeStruct(piece.shape, piece.dtype),
        in_specs=[VMEM],
        out_specs=VMEM,
        compiler_params=SMALL,
    )(piece)


def gather_kernel(*refs):
    pieces, slab_ref, q_ref = refs[:PEERS], refs[PEERS], refs[PEERS + 1]
    number = place()[1]
    part = pieces[0].shape[0]
    for step, piece in enumerate(pieces):
        peer = got_from(number, step)
        slab_ref[pl.ds(pl.multiple_of(peer * part, part), part), :] = piece[:, : 2 * HD]
        q_ref[peer] = piece[:, 2 * HD :]


def gather(pieces):
    rows = pieces[0].shape[0]
    return pl.pallas_call(
        gather_kernel,
        out_shape=[
            jax.ShapeDtypeStruct((PEERS * rows, 2 * HD), jnp.bfloat16),
            jax.ShapeDtypeStruct((PEERS, rows, WIDE), jnp.bfloat16),
        ],
        in_specs=[VMEM] * PEERS,
        out_specs=[VMEM] * 2,
        compiler_params=SMALL,
    )(*pieces)


def join_kernel(*refs):
    pieces, out_ref, sems = refs[:PEERS], refs[PEERS], refs[PEERS + 1]
    number = place()[1]
    part = out_ref.shape[0] // 2
    copies = []
    for step, piece in enumerate(pieces):
        peer = got_from(number, step)
        rows = pl.ds(pl.multiple_of((peer & 1) * part, part), part)
        lanes = pl.ds(pl.multiple_of((peer >> 1) * WIDE, HD), WIDE)
        copies.append(pltpu.make_async_copy(piece, out_ref.at[rows, lanes], sems.at[step]))
        copies[-1].start()
    for copy in copies:
        copy.wait()


def join(pieces):
    return pl.pallas_call(
        join_kernel,
        out_shape=jax.ShapeDtypeStruct((2 * pieces[0].shape[0], HQ * HD), jnp.bfloat16),
        in_specs=[VMEM] * PEERS,
        out_specs=HBM,
        scratch_shapes=[pltpu.SemaphoreType.DMA((PEERS,))],
        compiler_params=SMALL,
    )(*pieces)


def attend_kernel(backs, first, final, table_ref, factor_ref, *refs):
    refs = list(refs)
    q_ref = refs.pop(0)
    if not first:
        del refs[:2]
    slabs = [(refs.pop(0), refs.pop(0)) for _ in backs]
    out_refs = [refs.pop(0) for _ in range(PEERS)] if final else None
    sums_ref, top_ref = refs.pop(0), refs.pop(0)
    number = place()[1]
    core = number & 1
    if first:
        sums_ref[...] = jnp.zeros_like(sums_ref)
        top_ref[...] = jnp.full_like(top_ref, LOW)
    key_ref, value_ref = refs[:2]
    piece = q_ref.shape[1]
    half = slabs[0][0].shape[0] // 2
    group = GROUP // 2
    chains = [(block, g) for block in range(2) for g in range(2)]

    block_rows = 2 * piece
    index = lax.broadcasted_iota(jnp.int32, (block_rows, HD), 0)
    own_part = index < piece
    token = 2 * block_rows + index + jnp.where(own_part, core * piece, -(core * piece))
    for slab, back in zip(slabs, backs):
        for x in range(2):
            count = jnp.maximum(table_ref[4 * back + 2 * x], table_ref[4 * back + 2 * x + 1])
            at = x * half
            spare = slab[0][at : at + 16, :HD].astype(jnp.float32)[0:1]
            parts = [ref[at : at + block_rows, :] for ref in slab]
            for n in range(2, 4):
                low = at + n * piece
                parts.append(jnp.concatenate([ref[low : low + piece, :] for ref in slab], axis=0))
            for n, values in enumerate(parts):
                to = slice(n * block_rows, (n + 1) * block_rows)
                keys = values[:, :HD].astype(jnp.float32)
                values = values[:, HD:]
                ones = jnp.ones_like(values)
                if n >= 2:
                    keep = token + (n - 2) * block_rows < count
                    keys = jnp.where(keep, keys, spare)
                    values = jnp.where(keep, values.astype(jnp.float32), 0.0).astype(jnp.bfloat16)
                    ones = jnp.where(keep, 1.0, 0.0).astype(jnp.bfloat16)
                key_ref[x, :, to] = jnp.transpose(keys).astype(jnp.bfloat16)
                value_ref[x, to, :HD] = values
                value_ref[x, to, HD:] = ones

        @pl.loop(0, 4)
        def _(turn):
            x = turn >> 1
            side = turn & 1

            count = table_ref[4 * back + turn]

            def visit(width):
                keys = key_ref[x, :, :width]
                values = value_ref[x, :width, :]

                def scores(block, g):
                    rows = []
                    for i in range(group):
                        lanes = slice((g * group + i) * HD, (g * group + i + 1) * HD)
                        for t in range(2):
                            rows.append(q_ref[4 * side + 2 * block + t, :, lanes])
                    return jnp.dot(jnp.concatenate(rows, axis=0), keys, preferred_element_type=jnp.float32)

                ready = scores(*chains[0])
                for n, (block, g) in enumerate(chains):
                    s = ready
                    if n + 1 < len(chains):
                        ready = scores(*chains[n + 1])
                    step = s.shape[0] // group
                    s = jnp.concatenate(
                        [
                            s[i * step : (i + 1) * step] * factor_ref[side * GROUP + g * group + i]
                            for i in range(group)
                        ],
                        axis=0,
                    )
                    chain = 2 * block + g
                    old_top = top_ref[side, chain]
                    top = jnp.maximum(old_top, jnp.max(s, axis=1, keepdims=True))
                    weight = jnp.concatenate(
                        [jnp.exp2(s[:, at : at + HD] - top).astype(jnp.bfloat16) for at in range(0, s.shape[1], HD)],
                        axis=1,
                    )
                    sums = jnp.dot(weight, values, preferred_element_type=jnp.float32)
                    shrink = jnp.exp2(old_top - top)
                    sums_ref[side, chain] = sums + sums_ref[side, chain] * jnp.concatenate([shrink, shrink], axis=1)
                    top_ref[side, chain] = top

            most = 3 * block_rows
            pl.when((count > 0) & (count <= most))(lambda: visit(most))
            pl.when(count > most)(lambda: visit(most + block_rows))

    if final:
        done_ref = refs[2]
        for side in range(2):
            for block, g in chains:
                sums = sums_ref[side, 2 * block + g]
                result = (sums[:, :HD] / sums[:, HD:]).astype(jnp.bfloat16)
                for i in range(group):
                    lanes = slice((g * group + i) * HD, (g * group + i + 1) * HD)
                    for t in range(2):
                        at = (2 * i + t) * piece
                        done_ref[4 * side + 2 * block + t, :, lanes] = result[at : at + piece]
        for step, out_ref in enumerate(out_refs):
            out_ref[...] = done_ref[sent_to(number, step)]


def attend(tables, q, state, slabs, backs, final):
    first = state is None
    piece = q.shape[1]
    tall = GROUP * piece
    tokens = slabs[0][0].shape[0]
    out_shape = [
        jax.ShapeDtypeStruct((2, 4, tall, 2 * HD), jnp.float32),
        jax.ShapeDtypeStruct((2, 4, tall, HD), jnp.float32),
    ]
    scratch = [pltpu.VMEM((2, HD, tokens), jnp.bfloat16), pltpu.VMEM((2, tokens, 2 * HD), jnp.bfloat16)]
    if final:
        out_shape = [jax.ShapeDtypeStruct(q.shape[1:], jnp.bfloat16)] * PEERS + out_shape
        scratch.append(pltpu.VMEM(q.shape, jnp.bfloat16))
    work = len(backs) * PEERS * tall * tokens
    inputs = [q, *(state or ()), *[a for slab in slabs for a in slab]]
    aliases = {} if first else {3: PEERS * final, 4: PEERS * final + 1}
    return pl.pallas_call(
        functools.partial(attend_kernel, backs, first, final),
        out_shape=out_shape,
        in_specs=[SMEM] * 2 + [VMEM] * len(inputs),
        out_specs=[VMEM] * len(out_shape),
        scratch_shapes=scratch,
        input_output_aliases=aliases,
        compiler_params=LARGE,
        cost_estimate=pl.CostEstimate(flops=2 * work * HD, bytes_accessed=4 * q.size, transcendentals=work // 2),
    )(*tables, *inputs)


def per_device(spans, ctx, queries, keys, values, temps, levels, ctx_list, counts):
    other_core = [(t, t ^ 1) for t in range(ctx)]
    last = spans // 2 - 1

    def exchange(pieces):
        moved = [pieces[0]]
        for piece, step in zip(pieces[1:], STEPS[1:]):
            moved.append(lax.ppermute(piece, ("span", "ctx"), [(f, f ^ step[f % 2]) for f in range(spans * ctx)]))
        return moved

    def up(a, steps):
        return lax.ppermute(a, "span", [(s, (s + 2 * steps) % spans) for s in range(spans)])

    def near(a):
        return lax.ppermute(a, "ctx", other_core)

    pieces = begin(keys, values, queries)
    tables = tabulate(spans // 2, levels, temps, jnp.transpose(ctx_list), counts)
    moved, mine, tables = lax.optimization_barrier((exchange(pieces)[1:], hold(pieces[0]), tables))
    own, q = gather([mine, *moved])
    slabs = {0: own, 1: up(own, 1), last: up(own, last)}
    for back in range(2, last):
        slabs[back] = up(slabs[back - 1], 1)
    order = [1, last, *range(2, last)]
    out = attend(tables, q, None, [(own, near(own))], [0], False)
    for back in order:
        slab, state = lax.optimization_barrier((slabs[back], out))
        out = attend(tables, q, state, [(slab, near(slab))], [back], back == order[-1])
    return join(exchange(out[:PEERS]))


def solution(mesh):
    return jax.shard_map(
        functools.partial(per_device, mesh.shape["span"], mesh.shape["ctx"]),
        mesh=mesh,
        in_specs=(
            P(("span", "ctx"), None),
            P(("span", "ctx"), None),
            P(("span", "ctx"), None),
            P(),
            P(),
            P(),
            P(),
        ),
        out_specs=P(("span", "ctx"), None),
        check_vma=False,
    )
```

```python
import functools
import math

import jax
import jax.numpy as jnp
from jax import lax
from jax.experimental import pallas as pl
from jax.experimental.pallas import tpu as pltpu
from jax.sharding import PartitionSpec as P

HQ = 24
KVH = 4
HD = 128
GROUP = HQ // KVH
WIDE = GROUP * HD
PEERS = 8
LOW = -1e30
SCALE = math.log2(math.e) / math.sqrt(HD)
SMEM = pl.BlockSpec(memory_space=pltpu.SMEM)
VMEM = pl.BlockSpec(memory_space=pltpu.VMEM)
HBM = pl.BlockSpec(memory_space=pltpu.HBM)
SMALL = pltpu.CompilerParams(vmem_limit_bytes=6 << 20)
LARGE = pltpu.CompilerParams(vmem_limit_bytes=16 << 20)


STEPS = ((0, 0), (1, 1), (6, 6), (7, 7), (4, 2), (2, 4), (5, 3), (3, 5))


def sent_to(number, step):
    even, odd = STEPS[step]
    return number ^ jnp.where(number & 1 == 0, even, odd)


def got_from(number, step):
    even, odd = STEPS[step]
    if even & 1:
        even, odd = odd, even
    return number ^ jnp.where(number & 1 == 0, even, odd)


def place():
    span, tok = lax.axis_index("span"), lax.axis_index("ctx")
    return span & -2, 4 * (span & 1) + tok


def table_kernel(planes, levels_ref, temps_ref, list_ref, counts_ref, table_ref, factor_ref):
    base, number = place()
    head = number >> 1
    for side in range(2):
        level = levels_ref[base + side]
        for i in range(GROUP):
            factor_ref[side * GROUP + i] = temps_ref[level, head * GROUP + i] * SCALE

        @pl.loop(0, 2 * planes)
        def _(slab):
            ident = base + (slab & 1) - 2 * (slab >> 1)
            found = base + side == ident
            for j in range(list_ref.shape[0]):
                found = found | (list_ref[j, base + side] == ident)
            count = jnp.where(found & (ident >= 0), counts_ref[jnp.maximum(ident, 0)], 0)
            table_ref[2 * slab + side] = count


def tabulate(planes, levels, temps, ctx_list, counts):
    return pl.pallas_call(
        functools.partial(table_kernel, planes),
        out_shape=[jax.ShapeDtypeStruct((4 * planes,), jnp.int32), jax.ShapeDtypeStruct((2 * GROUP,), jnp.float32)],
        in_specs=[SMEM] * 4,
        out_specs=[SMEM] * 2,
        compiler_params=SMALL,
    )(levels, temps, ctx_list, counts)


def begin_kernel(keys_ref, values_ref, q_ref, *refs):
    pieces, (source, q_source, target, sems) = refs[:PEERS], refs[PEERS:]
    loads = [pltpu.make_async_copy(ref, source.at[i], sems.at[i]) for i, ref in enumerate((keys_ref, values_ref))]
    loads.append(pltpu.make_async_copy(q_ref, q_source, sems.at[2]))
    for load in loads:
        load.start()
    number = place()[1]
    for load in loads:
        load.wait()
    part = target.shape[1]
    stores = []
    for step in [*range(1, PEERS), 0]:
        peer = sent_to(number, step)
        rows = pl.ds(pl.multiple_of((peer & 1) * part, part), part)
        lanes = pl.ds(pl.multiple_of((peer >> 1) * HD, HD), HD)
        target[step, :, :HD] = source[0, rows, lanes]
        target[step, :, HD : 2 * HD] = source[1, rows, lanes]
        target[step, :, 2 * HD :] = q_source[rows, pl.ds(pl.multiple_of((peer >> 1) * WIDE, HD), WIDE)]
        stores.append(pltpu.make_async_copy(target.at[step], pieces[step], sems.at[step]))
        stores[-1].start()
    for store in stores:
        store.wait()


def begin(keys, values, queries):
    shape = (keys.shape[0] // 2, 2 * HD + WIDE)
    return pl.pallas_call(
        begin_kernel,
        out_shape=[jax.ShapeDtypeStruct(shape, jnp.bfloat16)] * PEERS,
        in_specs=[HBM] * 3,
        out_specs=[HBM] * PEERS,
        scratch_shapes=[
            pltpu.VMEM((2, *keys.shape), jnp.bfloat16),
            pltpu.VMEM(queries.shape, jnp.bfloat16),
            pltpu.VMEM((PEERS, *shape), jnp.bfloat16),
            pltpu.SemaphoreType.DMA((PEERS,)),
        ],
    )(keys, values, queries)


def hold_kernel(piece_ref, out_ref):
    out_ref[...] = piece_ref[...]


def hold(piece):
    return pl.pallas_call(
        hold_kernel,
        out_shape=jax.ShapeDtypeStruct(piece.shape, piece.dtype),
        in_specs=[VMEM],
        out_specs=VMEM,
        compiler_params=SMALL,
    )(piece)


def gather_kernel(*refs):
    pieces, slab_ref, q_ref = refs[:PEERS], refs[PEERS], refs[PEERS + 1]
    number = place()[1]
    part = pieces[0].shape[0]
    for step, piece in enumerate(pieces):
        peer = got_from(number, step)
        slab_ref[pl.ds(pl.multiple_of(peer * part, part), part), :] = piece[:, : 2 * HD]
        q_ref[peer] = piece[:, 2 * HD :]


def gather(pieces):
    rows = pieces[0].shape[0]
    return pl.pallas_call(
        gather_kernel,
        out_shape=[
            jax.ShapeDtypeStruct((PEERS * rows, 2 * HD), jnp.bfloat16),
            jax.ShapeDtypeStruct((PEERS, rows, WIDE), jnp.bfloat16),
        ],
        in_specs=[VMEM] * PEERS,
        out_specs=[VMEM] * 2,
        compiler_params=SMALL,
    )(*pieces)


def join_kernel(*refs):
    pieces, out_ref, sems = refs[:PEERS], refs[PEERS], refs[PEERS + 1]
    number = place()[1]
    part = out_ref.shape[0] // 2
    copies = []
    for step, piece in enumerate(pieces):
        peer = got_from(number, step)
        rows = pl.ds(pl.multiple_of((peer & 1) * part, part), part)
        lanes = pl.ds(pl.multiple_of((peer >> 1) * WIDE, HD), WIDE)
        copies.append(pltpu.make_async_copy(piece, out_ref.at[rows, lanes], sems.at[step]))
        copies[-1].start()
    for copy in copies:
        copy.wait()


def join(pieces):
    return pl.pallas_call(
        join_kernel,
        out_shape=jax.ShapeDtypeStruct((2 * pieces[0].shape[0], HQ * HD), jnp.bfloat16),
        in_specs=[VMEM] * PEERS,
        out_specs=HBM,
        scratch_shapes=[pltpu.SemaphoreType.DMA((PEERS,))],
        compiler_params=SMALL,
    )(*pieces)


def attend_kernel(backs, sides, far_side, first, final, table_ref, factor_ref, *refs):
    refs = list(refs)
    q_ref = refs.pop(0)
    if not first:
        del refs[:2]
    slabs = [[refs.pop(0) for _ in range(sides)] for _ in backs]
    out_refs = [refs.pop(0) for _ in range(PEERS)] if final else None
    sums_ref, top_ref = refs.pop(0), refs.pop(0)
    number = place()[1]
    core = (number & 1) ^ far_side
    if first:
        sums_ref[...] = jnp.zeros_like(sums_ref)
        top_ref[...] = jnp.full_like(top_ref, LOW)
    key_ref, value_ref = refs[:2]
    piece = q_ref.shape[1]
    half = slabs[0][0].shape[0] // 2
    group = GROUP // 2
    chains = [(block, g) for block in range(2) for g in range(2)]

    block_rows = 2 * piece
    index = lax.broadcasted_iota(jnp.int32, (block_rows, HD), 0)
    own_part = index < piece
    if sides == 2:
        token = 2 * block_rows + index + jnp.where(own_part, core * piece, -(core * piece))
    else:
        token = 2 * block_rows + index + jnp.where(own_part, core * piece, (core + 1) * piece)
    for slab, back in zip(slabs, backs):
        for x in range(2):
            count = jnp.maximum(table_ref[4 * back + 2 * x], table_ref[4 * back + 2 * x + 1])
            at = x * half
            spare = slab[0][at : at + 16, :HD].astype(jnp.float32)[0:1]
            parts = [ref[at : at + block_rows, :] for ref in slab]
            if sides == 2:
                for n in range(2, 4):
                    low = at + n * piece
                    parts.append(jnp.concatenate([ref[low : low + piece, :] for ref in slab], axis=0))
            else:
                parts.append(slab[0][at + block_rows : at + 2 * block_rows, :])
            for n, values in enumerate(parts):
                to = slice(n * block_rows, (n + 1) * block_rows)
                keys = values[:, :HD].astype(jnp.float32)
                values = values[:, HD:]
                ones = jnp.ones_like(values)
                if n >= sides:
                    keep = token + (n - sides) * block_rows < count
                    keys = jnp.where(keep, keys, spare)
                    values = jnp.where(keep, values.astype(jnp.float32), 0.0).astype(jnp.bfloat16)
                    ones = jnp.where(keep, 1.0, 0.0).astype(jnp.bfloat16)
                key_ref[x, :, to] = jnp.transpose(keys).astype(jnp.bfloat16)
                value_ref[x, to, :HD] = values
                value_ref[x, to, HD:] = ones

        @pl.loop(0, 4)
        def _(turn):
            x = turn >> 1
            side = turn & 1

            count = table_ref[4 * back + turn]

            def visit(width):
                keys = key_ref[x, :, :width]
                values = value_ref[x, :width, :]

                def scores(block, g):
                    rows = []
                    for i in range(group):
                        lanes = slice((g * group + i) * HD, (g * group + i + 1) * HD)
                        for t in range(2):
                            rows.append(q_ref[4 * side + 2 * block + t, :, lanes])
                    return jnp.dot(jnp.concatenate(rows, axis=0), keys, preferred_element_type=jnp.float32)

                ready = scores(*chains[0])
                for n, (block, g) in enumerate(chains):
                    s = ready
                    if n + 1 < len(chains):
                        ready = scores(*chains[n + 1])
                    step = s.shape[0] // group
                    s = jnp.concatenate(
                        [
                            s[i * step : (i + 1) * step] * factor_ref[side * GROUP + g * group + i]
                            for i in range(group)
                        ],
                        axis=0,
                    )
                    chain = 2 * block + g
                    old_top = top_ref[side, chain]
                    top = jnp.maximum(old_top, jnp.max(s, axis=1, keepdims=True))
                    weight = jnp.concatenate(
                        [jnp.exp2(s[:, at : at + HD] - top).astype(jnp.bfloat16) for at in range(0, s.shape[1], HD)],
                        axis=1,
                    )
                    sums = jnp.dot(weight, values, preferred_element_type=jnp.float32)
                    shrink = jnp.exp2(old_top - top)
                    sums_ref[side, chain] = sums + sums_ref[side, chain] * jnp.concatenate([shrink, shrink], axis=1)
                    top_ref[side, chain] = top

            most = 3 * block_rows
            if sides == 2:
                pl.when((count > 0) & (count <= most))(lambda: visit(most))
                pl.when(count > most)(lambda: visit(most + block_rows))
            else:
                pl.when(count > 0)(lambda: visit(2 * block_rows))

    if final:
        done_ref = refs[2]
        for side in range(2):
            for block, g in chains:
                sums = sums_ref[side, 2 * block + g]
                result = (sums[:, :HD] / sums[:, HD:]).astype(jnp.bfloat16)
                for i in range(group):
                    lanes = slice((g * group + i) * HD, (g * group + i + 1) * HD)
                    for t in range(2):
                        at = (2 * i + t) * piece
                        done_ref[4 * side + 2 * block + t, :, lanes] = result[at : at + piece]
        for step, out_ref in enumerate(out_refs):
            out_ref[...] = done_ref[sent_to(number, step)]


def attend(tables, q, state, slabs, backs, final, far_side=False):
    first = state is None
    piece = q.shape[1]
    tall = GROUP * piece
    tokens = slabs[0][0].shape[0] * len(slabs[0]) // 2
    out_shape = [
        jax.ShapeDtypeStruct((2, 4, tall, 2 * HD), jnp.float32),
        jax.ShapeDtypeStruct((2, 4, tall, HD), jnp.float32),
    ]
    scratch = [pltpu.VMEM((2, HD, tokens), jnp.bfloat16), pltpu.VMEM((2, tokens, 2 * HD), jnp.bfloat16)]
    if final:
        out_shape = [jax.ShapeDtypeStruct(q.shape[1:], jnp.bfloat16)] * PEERS + out_shape
        scratch.append(pltpu.VMEM(q.shape, jnp.bfloat16))
    work = len(backs) * PEERS * tall * tokens
    inputs = [q, *(state or ()), *[a for slab in slabs for a in slab]]
    aliases = {} if first else {3: PEERS * final, 4: PEERS * final + 1}
    return pl.pallas_call(
        functools.partial(attend_kernel, backs, len(slabs[0]), far_side, first, final),
        out_shape=out_shape,
        in_specs=[SMEM] * 2 + [VMEM] * len(inputs),
        out_specs=[VMEM] * len(out_shape),
        scratch_shapes=scratch,
        input_output_aliases=aliases,
        compiler_params=LARGE,
        cost_estimate=pl.CostEstimate(flops=2 * work * HD, bytes_accessed=4 * q.size, transcendentals=work // 2),
    )(*tables, *inputs)


def per_device(spans, ctx, queries, keys, values, temps, levels, ctx_list, counts):
    other_core = [(t, t ^ 1) for t in range(ctx)]
    last = spans // 2 - 1

    def exchange(pieces):
        moved = [pieces[0]]
        for piece, step in zip(pieces[1:], STEPS[1:]):
            moved.append(lax.ppermute(piece, ("span", "ctx"), [(f, f ^ step[f % 2]) for f in range(spans * ctx)]))
        return moved

    def up(a, steps):
        return lax.ppermute(a, "span", [(s, (s + 2 * steps) % spans) for s in range(spans)])

    def near(a):
        return lax.ppermute(a, "ctx", other_core)

    pieces = begin(keys, values, queries)
    tables = tabulate(spans // 2, levels, temps, jnp.transpose(ctx_list), counts)
    moved, mine, tables = lax.optimization_barrier((exchange(pieces)[1:], hold(pieces[0]), tables))
    own, q = gather([mine, *moved])
    slabs = {0: own, 1: up(own, 1), last: up(own, last)}
    state = attend(tables, q, None, [(own, near(own))], [0], False)
    slabs, state = lax.optimization_barrier((slabs, state))
    stage = [1, last]
    sides = [(slabs[b], near(slabs[b])) for b in stage]
    for back in range(2, last):
        slab = up(slabs[back - 1], 1)
        state = attend(tables, q, state, sides, stage, False)
        slabs[back], state = lax.optimization_barrier((slab, state))
        stage = [back]
        sides = [(slabs[back], near(slabs[back]))]
    mine, other = sides[0]
    state = attend(tables, q, state, [(mine,)], stage, False)
    other, state = lax.optimization_barrier((other, state))
    out = attend(tables, q, state, [(other,)], stage, True, True)
    return join(exchange(out[:PEERS]))


def solution(mesh):
    return jax.shard_map(
        functools.partial(per_device, mesh.shape["span"], mesh.shape["ctx"]),
        mesh=mesh,
        in_specs=(
            P(("span", "ctx"), None),
            P(("span", "ctx"), None),
            P(("span", "ctx"), None),
            P(),
            P(),
            P(),
            P(),
        ),
        out_specs=P(("span", "ctx"), None),
        check_vma=False,
    )
```

```python
import functools
import math

import jax
import jax.numpy as jnp
from jax import lax
from jax.experimental import pallas as pl
from jax.experimental.pallas import tpu as pltpu
from jax.sharding import PartitionSpec as P

HQ = 24
KVH = 4
HD = 128
GROUP = HQ // KVH
WIDE = GROUP * HD
PEERS = 4
LOW = -1e30
SCALE = math.log2(math.e) / math.sqrt(HD)
SMEM = pl.BlockSpec(memory_space=pltpu.SMEM)
VMEM = pl.BlockSpec(memory_space=pltpu.VMEM)
HBM = pl.BlockSpec(memory_space=pltpu.HBM)
SMALL = pltpu.CompilerParams(vmem_limit_bytes=6 << 20)
LARGE = pltpu.CompilerParams(vmem_limit_bytes=16 << 20)


STEPS = ((0, 0), (3, 3), (2, 1), (1, 2))


def place():
    span, tok = lax.axis_index("span"), lax.axis_index("ctx")
    return span & -2, 2 * (span & 1) + (tok >> 1), tok & 1


def peer_of(chip, core, step):
    even, odd = STEPS[step]
    return chip ^ jnp.where(core == 0, even, odd)


def table_kernel(planes, levels_ref, temps_ref, list_ref, counts_ref, table_ref, factor_ref):
    base, head, _ = place()
    for side in range(2):
        level = levels_ref[base + side]
        for i in range(GROUP):
            factor_ref[side * GROUP + i] = temps_ref[level, head * GROUP + i] * SCALE

        @pl.loop(0, 2 * planes)
        def _(slab):
            ident = base + (slab & 1) - 2 * (slab >> 1)
            found = base + side == ident
            for j in range(list_ref.shape[0]):
                found = found | (list_ref[j, base + side] == ident)
            count = jnp.where(found & (ident >= 0), counts_ref[jnp.maximum(ident, 0)], 0)
            table_ref[2 * slab + side] = count


def tabulate(planes, levels, temps, ctx_list, counts):
    return pl.pallas_call(
        functools.partial(table_kernel, planes),
        out_shape=[jax.ShapeDtypeStruct((4 * planes,), jnp.int32), jax.ShapeDtypeStruct((2 * GROUP,), jnp.float32)],
        in_specs=[SMEM] * 4,
        out_specs=[SMEM] * 2,
        compiler_params=SMALL,
    )(levels, temps, ctx_list, counts)


def begin_kernel(keys_ref, values_ref, q_ref, *refs):
    pieces, (source, q_source, target, sems) = refs[:PEERS], refs[PEERS:]
    loads = [pltpu.make_async_copy(ref, source.at[i], sems.at[i]) for i, ref in enumerate((keys_ref, values_ref))]
    loads.append(pltpu.make_async_copy(q_ref, q_source, sems.at[2]))
    for load in loads:
        load.start()
    _, chip, core = place()
    for load in loads:
        load.wait()
    stores = []
    for step in [*range(1, PEERS), 0]:
        peer = peer_of(chip, core, step)
        lanes = pl.ds(pl.multiple_of(peer * HD, HD), HD)
        target[step, :, :HD] = source[0, :, lanes]
        target[step, :, HD : 2 * HD] = source[1, :, lanes]
        target[step, :, 2 * HD :] = q_source[:, pl.ds(pl.multiple_of(peer * WIDE, HD), WIDE)]
        stores.append(pltpu.make_async_copy(target.at[step], pieces[step], sems.at[step]))
        stores[-1].start()
    for store in stores:
        store.wait()


def begin(keys, values, queries):
    shape = (keys.shape[0], 2 * HD + WIDE)
    return pl.pallas_call(
        begin_kernel,
        out_shape=[jax.ShapeDtypeStruct(shape, jnp.bfloat16)] * PEERS,
        in_specs=[HBM] * 3,
        out_specs=[HBM] * PEERS,
        scratch_shapes=[
            pltpu.VMEM((2, *keys.shape), jnp.bfloat16),
            pltpu.VMEM(queries.shape, jnp.bfloat16),
            pltpu.VMEM((PEERS, *shape), jnp.bfloat16),
            pltpu.SemaphoreType.DMA((PEERS,)),
        ],
    )(keys, values, queries)


def hold_kernel(piece_ref, out_ref):
    out_ref[...] = piece_ref[...]


def hold(piece):
    return pl.pallas_call(
        hold_kernel,
        out_shape=jax.ShapeDtypeStruct(piece.shape, piece.dtype),
        in_specs=[VMEM],
        out_specs=VMEM,
        compiler_params=SMALL,
    )(piece)


def gather_kernel(*refs):
    pieces, slab_ref, q_ref = refs[:PEERS], refs[PEERS], refs[PEERS + 1]
    _, chip, core = place()
    part = pieces[0].shape[0]
    for step, piece in enumerate(pieces):
        peer = peer_of(chip, core, step)
        slab_ref[pl.ds(pl.multiple_of(peer * part, part), part), :] = piece[:, : 2 * HD]
        q_ref[peer] = piece[:, 2 * HD :]


def gather(pieces):
    rows = pieces[0].shape[0]
    return pl.pallas_call(
        gather_kernel,
        out_shape=[
            jax.ShapeDtypeStruct((PEERS * rows, 2 * HD), jnp.bfloat16),
            jax.ShapeDtypeStruct((PEERS, rows, WIDE), jnp.bfloat16),
        ],
        in_specs=[VMEM] * PEERS,
        out_specs=[VMEM] * 2,
        compiler_params=SMALL,
    )(*pieces)


def join_kernel(*refs):
    pieces, out_ref, sems = refs[:PEERS], refs[PEERS], refs[PEERS + 1]
    _, chip, core = place()
    copies = []
    for step, piece in enumerate(pieces):
        lanes = pl.ds(pl.multiple_of(peer_of(chip, core, step) * WIDE, HD), WIDE)
        copies.append(pltpu.make_async_copy(piece, out_ref.at[:, lanes], sems.at[step]))
        copies[-1].start()
    for copy in copies:
        copy.wait()


def join(pieces):
    return pl.pallas_call(
        join_kernel,
        out_shape=jax.ShapeDtypeStruct((pieces[0].shape[0], HQ * HD), jnp.bfloat16),
        in_specs=[VMEM] * PEERS,
        out_specs=HBM,
        scratch_shapes=[pltpu.SemaphoreType.DMA((PEERS,))],
        compiler_params=SMALL,
    )(*pieces)


def attend_kernel(backs, sides, far_side, first, final, table_ref, factor_ref, *refs):
    refs = list(refs)
    q_ref = refs.pop(0)
    if not first:
        del refs[:2]
    slabs = [[refs.pop(0) for _ in range(sides)] for _ in backs]
    out_refs = [refs.pop(0) for _ in range(PEERS)] if final else None
    sums_ref, top_ref = refs.pop(0), refs.pop(0)
    _, chip, this_core = place()
    core = this_core ^ far_side
    if first:
        sums_ref[...] = jnp.zeros_like(sums_ref)
        top_ref[...] = jnp.full_like(top_ref, LOW)
    key_ref, value_ref = refs[:2]
    piece = q_ref.shape[1]
    half = slabs[0][0].shape[0] // 2
    group = GROUP // 2
    chains = [(block, g) for block in range(2) for g in range(2)]

    block_rows = half // 2
    index = lax.broadcasted_iota(jnp.int32, (block_rows, HD), 0)
    for slab, back in zip(slabs, backs):
        for x in range(2):
            count = jnp.maximum(table_ref[4 * back + 2 * x], table_ref[4 * back + 2 * x + 1])
            at = x * half
            spare = slab[0][at : at + 16, :HD].astype(jnp.float32)[0:1]
            for side, ref in enumerate(slab):
                owner = core ^ side
                for n in range(2):
                    values = ref[at + n * block_rows : at + (n + 1) * block_rows, :]
                    keys = values[:, :HD].astype(jnp.float32)
                    values = values[:, HD:]
                    ones = jnp.ones_like(values)
                    to = side * block_rows
                    if n:
                        keep = (2 + owner) * block_rows + index < count
                        keys = jnp.where(keep, keys, spare)
                        values = jnp.where(keep, values.astype(jnp.float32), 0.0).astype(jnp.bfloat16)
                        ones = jnp.where(keep, 1.0, 0.0).astype(jnp.bfloat16)
                        to = block_rows if sides == 1 else (2 + owner) * block_rows
                    to = pl.ds(pl.multiple_of(to, block_rows), block_rows)
                    key_ref[x, :, to] = jnp.transpose(keys).astype(jnp.bfloat16)
                    value_ref[x, to, :HD] = values
                    value_ref[x, to, HD:] = ones

        @pl.loop(0, 4)
        def _(turn):
            x = turn >> 1
            side = turn & 1

            count = table_ref[4 * back + turn]

            def visit(width):
                keys = key_ref[x, :, :width]
                values = value_ref[x, :width, :]

                def scores(block, g):
                    rows = []
                    for i in range(group):
                        lanes = slice((g * group + i) * HD, (g * group + i + 1) * HD)
                        rows.append(q_ref[2 * side + block, :, lanes])
                    return jnp.dot(jnp.concatenate(rows, axis=0), keys, preferred_element_type=jnp.float32)

                ready = scores(*chains[0])
                for n, (block, g) in enumerate(chains):
                    s = ready
                    if n + 1 < len(chains):
                        ready = scores(*chains[n + 1])
                    step = s.shape[0] // group
                    s = jnp.concatenate(
                        [
                            s[i * step : (i + 1) * step] * factor_ref[side * GROUP + g * group + i]
                            for i in range(group)
                        ],
                        axis=0,
                    )
                    chain = 2 * block + g
                    old_top = top_ref[side, chain]
                    top = jnp.maximum(old_top, jnp.max(s, axis=1, keepdims=True))
                    weight = jnp.concatenate(
                        [jnp.exp2(s[:, at : at + HD] - top).astype(jnp.bfloat16) for at in range(0, s.shape[1], HD)],
                        axis=1,
                    )
                    sums = jnp.dot(weight, values, preferred_element_type=jnp.float32)
                    shrink = jnp.exp2(old_top - top)
                    sums_ref[side, chain] = sums + sums_ref[side, chain] * jnp.concatenate([shrink, shrink], axis=1)
                    top_ref[side, chain] = top

            most = 3 * block_rows
            if sides == 2:
                pl.when((count > 0) & (count <= most))(lambda: visit(most))
                pl.when(count > most)(lambda: visit(most + block_rows))
            else:
                pl.when(count > 0)(lambda: visit(2 * block_rows))

    if final:
        done_ref = refs[2]
        for side in range(2):
            for block, g in chains:
                sums = sums_ref[side, 2 * block + g]
                result = (sums[:, :HD] / sums[:, HD:]).astype(jnp.bfloat16)
                for i in range(group):
                    lanes = slice((g * group + i) * HD, (g * group + i + 1) * HD)
                    done_ref[2 * side + block, :, lanes] = result[i * piece : (i + 1) * piece]
        for step, out_ref in enumerate(out_refs):
            out_ref[...] = done_ref[peer_of(chip, this_core, step)]


def attend(tables, q, state, slabs, backs, final, far_side=False):
    first = state is None
    piece = q.shape[1]
    tall = GROUP * piece // 2
    tokens = slabs[0][0].shape[0] * len(slabs[0]) // 2
    out_shape = [
        jax.ShapeDtypeStruct((2, 4, tall, 2 * HD), jnp.float32),
        jax.ShapeDtypeStruct((2, 4, tall, HD), jnp.float32),
    ]
    scratch = [pltpu.VMEM((2, HD, tokens), jnp.bfloat16), pltpu.VMEM((2, tokens, 2 * HD), jnp.bfloat16)]
    if final:
        out_shape = [jax.ShapeDtypeStruct(q.shape[1:], jnp.bfloat16)] * PEERS + out_shape
        scratch.append(pltpu.VMEM(q.shape, jnp.bfloat16))
    work = len(backs) * PEERS * tall * tokens
    inputs = [q, *(state or ()), *[a for slab in slabs for a in slab]]
    aliases = {} if first else {3: PEERS * final, 4: PEERS * final + 1}
    return pl.pallas_call(
        functools.partial(attend_kernel, backs, len(slabs[0]), far_side, first, final),
        out_shape=out_shape,
        in_specs=[SMEM] * 2 + [VMEM] * len(inputs),
        out_specs=[VMEM] * len(out_shape),
        scratch_shapes=scratch,
        input_output_aliases=aliases,
        compiler_params=LARGE,
        cost_estimate=pl.CostEstimate(flops=2 * work * HD, bytes_accessed=4 * q.size, transcendentals=work // 2),
    )(*tables, *inputs)


def per_device(spans, ctx, queries, keys, values, temps, levels, ctx_list, counts):
    other_core = [(t, t ^ 1) for t in range(ctx)]
    last = spans // 2 - 1

    def exchange(pieces):
        moved = [pieces[0]]
        for piece, step in zip(pieces[1:], STEPS[1:]):
            pairs = [(f, f ^ (2 * step[f % 2])) for f in range(spans * ctx)]
            moved.append(lax.ppermute(piece, ("span", "ctx"), pairs))
        return moved

    def up(a, steps):
        return lax.ppermute(a, "span", [(s, (s + 2 * steps) % spans) for s in range(spans)])

    def near(a):
        return lax.ppermute(a, "ctx", other_core)

    pieces = begin(keys, values, queries)
    tables = tabulate(spans // 2, levels, temps, jnp.transpose(ctx_list), counts)
    moved, mine, tables = lax.optimization_barrier((exchange(pieces)[1:], hold(pieces[0]), tables))
    own, q = gather([mine, *moved])
    slabs = {0: own, 1: up(own, 1), last: up(own, last)}
    state = attend(tables, q, None, [(own, near(own))], [0], False)
    slabs, state = lax.optimization_barrier((slabs, state))
    stage = [1, last]
    sides = [(slabs[b], near(slabs[b])) for b in stage]
    for back in range(2, last):
        slab = up(slabs[back - 1], 1)
        state = attend(tables, q, state, sides, stage, False)
        slabs[back], state = lax.optimization_barrier((slab, state))
        stage = [back]
        sides = [(slabs[back], near(slabs[back]))]
    mine, other = sides[0]
    state = attend(tables, q, state, [(mine,)], stage, False)
    other, state = lax.optimization_barrier((other, state))
    out = attend(tables, q, state, [(other,)], stage, True, True)
    return join(exchange(out[:PEERS]))


def solution(mesh):
    return jax.shard_map(
        functools.partial(per_device, mesh.shape["span"], mesh.shape["ctx"]),
        mesh=mesh,
        in_specs=(
            P(("span", "ctx"), None),
            P(("span", "ctx"), None),
            P(("span", "ctx"), None),
            P(),
            P(),
            P(),
            P(),
        ),
        out_specs=P(("span", "ctx"), None),
        check_vma=False,
    )
```

```python
import functools
import math

import jax
import jax.numpy as jnp
from jax import lax
from jax.experimental import pallas as pl
from jax.experimental.pallas import tpu as pltpu
from jax.sharding import PartitionSpec as P

HQ = 24
KVH = 4
HD = 128
GROUP = HQ // KVH
WIDE = GROUP * HD
PEERS = 4
LOW = -1e30
SCALE = math.log2(math.e) / math.sqrt(HD)
SMEM = pl.BlockSpec(memory_space=pltpu.SMEM)
VMEM = pl.BlockSpec(memory_space=pltpu.VMEM)
HBM = pl.BlockSpec(memory_space=pltpu.HBM)
SMALL = pltpu.CompilerParams(vmem_limit_bytes=6 << 20)
LARGE = pltpu.CompilerParams(vmem_limit_bytes=16 << 20)


STEPS = ((0, 0), (3, 3), (2, 1), (1, 2))


def place():
    span, tok = lax.axis_index("span"), lax.axis_index("ctx")
    return span & -2, 2 * (span & 1) + (tok >> 1), tok & 1


def peer_of(chip, core, step):
    even, odd = STEPS[step]
    return chip ^ jnp.where(core == 0, even, odd)


def table_kernel(planes, levels_ref, temps_ref, list_ref, counts_ref, table_ref, factor_ref):
    base, head, _ = place()
    for side in range(2):
        level = levels_ref[base + side]
        for i in range(GROUP):
            factor_ref[side * GROUP + i] = temps_ref[level, head * GROUP + i] * SCALE

        @pl.loop(0, 2 * planes)
        def _(slab):
            ident = base + (slab & 1) - 2 * (slab >> 1)
            found = base + side == ident
            for j in range(list_ref.shape[0]):
                found = found | (list_ref[j, base + side] == ident)
            count = jnp.where(found & (ident >= 0), counts_ref[jnp.maximum(ident, 0)], 0)
            table_ref[2 * slab + side] = count


def tabulate(planes, levels, temps, ctx_list, counts):
    return pl.pallas_call(
        functools.partial(table_kernel, planes),
        out_shape=[jax.ShapeDtypeStruct((4 * planes,), jnp.int32), jax.ShapeDtypeStruct((2 * GROUP,), jnp.float32)],
        in_specs=[SMEM] * 4,
        out_specs=[SMEM] * 2,
        compiler_params=SMALL,
    )(levels, temps, ctx_list, counts)


def begin_kernel(keys_ref, values_ref, q_ref, *refs):
    pieces, (source, q_source, target, sems) = refs[:PEERS], refs[PEERS:]
    loads = [pltpu.make_async_copy(ref, source.at[i], sems.at[i]) for i, ref in enumerate((keys_ref, values_ref))]
    loads.append(pltpu.make_async_copy(q_ref, q_source, sems.at[2]))
    for load in loads:
        load.start()
    _, chip, core = place()
    for load in loads:
        load.wait()
    stores = []
    for step in [*range(1, PEERS), 0]:
        peer = peer_of(chip, core, step)
        lanes = pl.ds(pl.multiple_of(peer * HD, HD), HD)
        target[step, :, :HD] = source[0, :, lanes]
        target[step, :, HD : 2 * HD] = source[1, :, lanes]
        target[step, :, 2 * HD :] = q_source[:, pl.ds(pl.multiple_of(peer * WIDE, HD), WIDE)]
        stores.append(pltpu.make_async_copy(target.at[step], pieces[step], sems.at[step]))
        stores[-1].start()
    for store in stores:
        store.wait()


def begin(keys, values, queries):
    shape = (keys.shape[0], 2 * HD + WIDE)
    return pl.pallas_call(
        begin_kernel,
        out_shape=[jax.ShapeDtypeStruct(shape, jnp.bfloat16)] * PEERS,
        in_specs=[HBM] * 3,
        out_specs=[HBM] * PEERS,
        scratch_shapes=[
            pltpu.VMEM((2, *keys.shape), jnp.bfloat16),
            pltpu.VMEM(queries.shape, jnp.bfloat16),
            pltpu.VMEM((PEERS, *shape), jnp.bfloat16),
            pltpu.SemaphoreType.DMA((PEERS,)),
        ],
    )(keys, values, queries)


def hold_kernel(piece_ref, out_ref):
    out_ref[...] = piece_ref[...]


def hold(piece):
    return pl.pallas_call(
        hold_kernel,
        out_shape=jax.ShapeDtypeStruct(piece.shape, piece.dtype),
        in_specs=[VMEM],
        out_specs=VMEM,
        compiler_params=SMALL,
    )(piece)


def gather_kernel(*refs):
    pieces, slab_ref, q_ref = refs[:PEERS], refs[PEERS], refs[PEERS + 1]
    _, chip, core = place()
    part = pieces[0].shape[0]
    for step, piece in enumerate(pieces):
        peer = peer_of(chip, core, step)
        slab_ref[pl.ds(pl.multiple_of(peer * part, part), part), :] = piece[:, : 2 * HD]
        q_ref[peer] = piece[:, 2 * HD :]


def gather(pieces):
    rows = pieces[0].shape[0]
    return pl.pallas_call(
        gather_kernel,
        out_shape=[
            jax.ShapeDtypeStruct((PEERS * rows, 2 * HD), jnp.bfloat16),
            jax.ShapeDtypeStruct((PEERS, rows, WIDE), jnp.bfloat16),
        ],
        in_specs=[VMEM] * PEERS,
        out_specs=[VMEM] * 2,
        compiler_params=SMALL,
    )(*pieces)


def join_kernel(*refs):
    pieces, out_ref, sems = refs[:PEERS], refs[PEERS], refs[PEERS + 1]
    _, chip, _ = place()
    copies = []
    for flip, piece in enumerate(pieces):
        lanes = pl.ds(pl.multiple_of((chip ^ flip) * WIDE, HD), WIDE)
        copies.append(pltpu.make_async_copy(piece, out_ref.at[:, lanes], sems.at[flip]))
        copies[-1].start()
    for copy in copies:
        copy.wait()


def join(pieces):
    return pl.pallas_call(
        join_kernel,
        out_shape=jax.ShapeDtypeStruct((pieces[0].shape[0], HQ * HD), jnp.bfloat16),
        in_specs=[VMEM] * PEERS,
        out_specs=HBM,
        scratch_shapes=[pltpu.SemaphoreType.DMA((PEERS,))],
        compiler_params=SMALL,
    )(*pieces)


def attend_kernel(backs, first, final, table_ref, factor_ref, *refs):
    refs = list(refs)
    q_ref = refs.pop(0)
    if not first:
        del refs[:2]
    slabs = [(refs.pop(0), refs.pop(0)) for _ in backs]
    out_refs = [refs.pop(0) for _ in range(2)] if final else None
    sums_ref, top_ref = refs.pop(0), refs.pop(0)
    _, chip, core = place()
    the_side = (chip >> 1) ^ (final == 1)
    if first:
        sums_ref[...] = jnp.zeros_like(sums_ref)
        top_ref[...] = jnp.full_like(top_ref, LOW)
    key_ref, value_ref = refs[:2]
    piece = q_ref.shape[1]
    half = slabs[0][0].shape[0] // 2
    group = GROUP // 2
    chains = [(block, g) for block in range(2) for g in range(2)]

    block_rows = half // 2
    index = lax.broadcasted_iota(jnp.int32, (block_rows, HD), 0)
    for slab, back in zip(slabs, backs):
        for x in range(2):
            count = jnp.maximum(table_ref[4 * back + 2 * x], table_ref[4 * back + 2 * x + 1])
            at = x * half
            spare = slab[0][at : at + 16, :HD].astype(jnp.float32)[0:1]
            for side, ref in enumerate(slab):
                owner = core ^ side
                for n in range(2):
                    values = ref[at + n * block_rows : at + (n + 1) * block_rows, :]
                    keys = values[:, :HD].astype(jnp.float32)
                    values = values[:, HD:]
                    ones = jnp.ones_like(values)
                    to = side * block_rows
                    if n:
                        keep = (2 + owner) * block_rows + index < count
                        keys = jnp.where(keep, keys, spare)
                        values = jnp.where(keep, values.astype(jnp.float32), 0.0).astype(jnp.bfloat16)
                        ones = jnp.where(keep, 1.0, 0.0).astype(jnp.bfloat16)
                        to = (2 + owner) * block_rows
                    to = pl.ds(pl.multiple_of(to, block_rows), block_rows)
                    key_ref[x, :, to] = jnp.transpose(keys).astype(jnp.bfloat16)
                    value_ref[x, to, :HD] = values
                    value_ref[x, to, HD:] = ones

        @pl.loop(0, 2 if final else 4)
        def _(turn):
            x = turn if final else turn >> 1
            side = the_side if final else turn & 1
            count = table_ref[4 * back + 2 * x + side]

            def visit(width):
                keys = key_ref[x, :, :width]
                values = value_ref[x, :width, :]

                def scores(block, g):
                    rows = []
                    for i in range(group):
                        lanes = slice((g * group + i) * HD, (g * group + i + 1) * HD)
                        rows.append(q_ref[2 * side + block, :, lanes])
                    return jnp.dot(jnp.concatenate(rows, axis=0), keys, preferred_element_type=jnp.float32)

                ready = scores(*chains[0])
                for n, (block, g) in enumerate(chains):
                    s = ready
                    if n + 1 < len(chains):
                        ready = scores(*chains[n + 1])
                    step = s.shape[0] // group
                    s = jnp.concatenate(
                        [
                            s[i * step : (i + 1) * step] * factor_ref[side * GROUP + g * group + i]
                            for i in range(group)
                        ],
                        axis=0,
                    )
                    chain = 2 * block + g
                    old_top = top_ref[side, chain]
                    top = jnp.maximum(old_top, jnp.max(s, axis=1, keepdims=True))
                    weight = jnp.concatenate(
                        [jnp.exp2(s[:, at : at + HD] - top).astype(jnp.bfloat16) for at in range(0, s.shape[1], HD)],
                        axis=1,
                    )
                    sums = jnp.dot(weight, values, preferred_element_type=jnp.float32)
                    shrink = jnp.exp2(old_top - top)
                    sums_ref[side, chain] = sums + sums_ref[side, chain] * jnp.concatenate([shrink, shrink], axis=1)
                    top_ref[side, chain] = top

            most = 3 * block_rows
            pl.when((count > 0) & (count <= most))(lambda: visit(most))
            pl.when(count > most)(lambda: visit(most + block_rows))

    if final:
        done_ref = refs[2]
        for block, g in chains:
            sums = sums_ref[the_side, 2 * block + g]
            result = (sums[:, :HD] / sums[:, HD:]).astype(jnp.bfloat16)
            for i in range(group):
                lanes = slice((g * group + i) * HD, (g * group + i + 1) * HD)
                done_ref[block, :, lanes] = result[i * piece : (i + 1) * piece]
        for flip, out_ref in enumerate(out_refs):
            out_ref[...] = done_ref[(chip & 1) ^ flip]


def attend(tables, q, state, slabs, backs, final=0):
    first = state is None
    piece = q.shape[1]
    tall = GROUP * piece // 2
    tokens = slabs[0][0].shape[0]
    out_shape = [
        jax.ShapeDtypeStruct((2, 4, tall, 2 * HD), jnp.float32),
        jax.ShapeDtypeStruct((2, 4, tall, HD), jnp.float32),
    ]
    scratch = [pltpu.VMEM((2, HD, tokens), jnp.bfloat16), pltpu.VMEM((2, tokens, 2 * HD), jnp.bfloat16)]
    if final:
        out_shape = [jax.ShapeDtypeStruct(q.shape[1:], jnp.bfloat16)] * 2 + out_shape
        scratch.append(pltpu.VMEM((2, *q.shape[1:]), jnp.bfloat16))
    work = len(backs) * PEERS * tall * tokens
    inputs = [q, *(state or ()), *[a for slab in slabs for a in slab]]
    outs = len(out_shape) - 2
    aliases = {} if first else {3: outs, 4: outs + 1}
    return pl.pallas_call(
        functools.partial(attend_kernel, backs, first, final),
        out_shape=out_shape,
        in_specs=[SMEM] * 2 + [VMEM] * len(inputs),
        out_specs=[VMEM] * len(out_shape),
        scratch_shapes=scratch,
        input_output_aliases=aliases,
        compiler_params=LARGE,
        cost_estimate=pl.CostEstimate(flops=2 * work * HD, bytes_accessed=4 * q.size, transcendentals=work // 2),
    )(*tables, *inputs)


def per_device(spans, ctx, queries, keys, values, temps, levels, ctx_list, counts):
    other_core = [(t, t ^ 1) for t in range(ctx)]
    last = spans // 2 - 1

    def flip(piece, even, odd):
        pairs = [(f, f ^ (2 * (odd if f % 2 else even))) for f in range(spans * ctx)]
        return lax.ppermute(piece, ("span", "ctx"), pairs)

    def exchange(pieces):
        return [pieces[0]] + [flip(piece, *step) for piece, step in zip(pieces[1:], STEPS[1:])]

    def up(a, steps):
        return lax.ppermute(a, "span", [(s, (s + 2 * steps) % spans) for s in range(spans)])

    def near(a):
        return lax.ppermute(a, "ctx", other_core)

    pieces = begin(keys, values, queries)
    tables = tabulate(spans // 2, levels, temps, jnp.transpose(ctx_list), counts)
    moved, mine, tables = lax.optimization_barrier((exchange(pieces)[1:], hold(pieces[0]), tables))
    own, q = gather([mine, *moved])
    slabs = {0: own, 1: up(own, 1), last: up(own, last)}
    state = attend(tables, q, None, [(own, near(own))], [0])
    slabs, state = lax.optimization_barrier((slabs, state))
    stage = [1, last]
    sides = [(slabs[b], near(slabs[b])) for b in stage]
    for back in range(2, last):
        slab = up(slabs[back - 1], 1)
        state = attend(tables, q, state, sides, stage)
        slabs[back], state = lax.optimization_barrier((slab, state))
        stage = [back]
        sides = [(slabs[back], near(slabs[back]))]
    beside, across, *state = attend(tables, q, state, sides, stage, 1)
    across = flip(across, 3, 3)
    mine, along, *_ = attend(tables, q, state, sides, stage, 2)
    across, beside, mine, along = lax.optimization_barrier((across, beside, mine, along))
    return join([mine, flip(along, 1, 1), flip(beside, 2, 2), across])


def solution(mesh):
    return jax.shard_map(
        functools.partial(per_device, mesh.shape["span"], mesh.shape["ctx"]),
        mesh=mesh,
        in_specs=(
            P(("span", "ctx"), None),
            P(("span", "ctx"), None),
            P(("span", "ctx"), None),
            P(),
            P(),
            P(),
            P(),
        ),
        out_specs=P(("span", "ctx"), None),
        check_vma=False,
    )
```

```python
import functools
import math

import jax
import jax.numpy as jnp
from jax import lax
from jax.experimental import pallas as pl
from jax.experimental.pallas import tpu as pltpu
from jax.sharding import PartitionSpec as P

HQ = 24
KVH = 4
HD = 128
GROUP = HQ // KVH
WIDE = GROUP * HD
PEERS = 4
LOW = -1e30
SCALE = math.log2(math.e) / math.sqrt(HD)
SMEM = pl.BlockSpec(memory_space=pltpu.SMEM)
VMEM = pl.BlockSpec(memory_space=pltpu.VMEM)
HBM = pl.BlockSpec(memory_space=pltpu.HBM)
SMALL = pltpu.CompilerParams(vmem_limit_bytes=6 << 20)
LARGE = pltpu.CompilerParams(vmem_limit_bytes=16 << 20)


STEPS = ((0, 0), (3, 3), (2, 1), (1, 2))


def place():
    span, tok = lax.axis_index("span"), lax.axis_index("ctx")
    return span & -2, 2 * (span & 1) + (tok >> 1), tok & 1


def peer_of(chip, core, step):
    even, odd = STEPS[step]
    return chip ^ jnp.where(core == 0, even, odd)


def table_kernel(planes, levels_ref, temps_ref, list_ref, counts_ref, table_ref, factor_ref):
    base, head, _ = place()
    for side in range(2):
        level = levels_ref[base + side]
        for i in range(GROUP):
            factor_ref[side * GROUP + i] = temps_ref[level, head * GROUP + i] * SCALE

        @pl.loop(0, 2 * planes)
        def _(slab):
            ident = base + (slab & 1) - 2 * (slab >> 1)
            found = base + side == ident
            for j in range(list_ref.shape[0]):
                found = found | (list_ref[j, base + side] == ident)
            count = jnp.where(found & (ident >= 0), counts_ref[jnp.maximum(ident, 0)], 0)
            table_ref[2 * slab + side] = count


def tabulate(planes, levels, temps, ctx_list, counts):
    return pl.pallas_call(
        functools.partial(table_kernel, planes),
        out_shape=[jax.ShapeDtypeStruct((4 * planes,), jnp.int32), jax.ShapeDtypeStruct((2 * GROUP,), jnp.float32)],
        in_specs=[SMEM] * 4,
        out_specs=[SMEM] * 2,
        compiler_params=SMALL,
    )(levels, temps, ctx_list, counts)


def begin_kernel(keys_ref, values_ref, q_ref, *refs):
    pieces, (target, sems, out_sems) = refs[:PEERS], refs[PEERS:]
    _, chip, core = place()
    steps = [*range(1, PEERS), 0]
    loads = {}
    for step in steps:
        peer = peer_of(chip, core, step)
        at = 0
        for i, ref in enumerate((keys_ref, values_ref, q_ref)):
            width = ref.shape[1] // KVH
            lanes = pl.ds(pl.multiple_of(peer * width, HD), width)
            load = pltpu.make_async_copy(ref.at[:, lanes], target.at[step, :, at : at + width], sems.at[step, i])
            load.start()
            loads[step, i] = load
            at += width
    stores = []
    for step in steps:
        for i in range(3):
            loads[step, i].wait()
        stores.append(pltpu.make_async_copy(target.at[step], pieces[step], out_sems.at[step]))
        stores[-1].start()
    for store in stores:
        store.wait()


def begin(keys, values, queries):
    shape = (keys.shape[0], 2 * HD + WIDE)
    return pl.pallas_call(
        begin_kernel,
        out_shape=[jax.ShapeDtypeStruct(shape, jnp.bfloat16)] * PEERS,
        in_specs=[HBM] * 3,
        out_specs=[HBM] * PEERS,
        scratch_shapes=[
            pltpu.VMEM((PEERS, *shape), jnp.bfloat16),
            pltpu.SemaphoreType.DMA((PEERS, 3)),
            pltpu.SemaphoreType.DMA((PEERS,)),
        ],
    )(keys, values, queries)


def hold_kernel(piece_ref, out_ref):
    out_ref[...] = piece_ref[...]


def hold(piece):
    return pl.pallas_call(
        hold_kernel,
        out_shape=jax.ShapeDtypeStruct(piece.shape, piece.dtype),
        in_specs=[VMEM],
        out_specs=VMEM,
        compiler_params=SMALL,
    )(piece)


def gather_kernel(*refs):
    pieces, slab_ref, q_ref = refs[:PEERS], refs[PEERS], refs[PEERS + 1]
    _, chip, core = place()
    part = pieces[0].shape[0]
    for step, piece in enumerate(pieces):
        peer = peer_of(chip, core, step)
        slab_ref[pl.ds(pl.multiple_of(peer * part, part), part), :] = piece[:, : 2 * HD]
        q_ref[peer] = piece[:, 2 * HD :]


def gather(pieces):
    rows = pieces[0].shape[0]
    return pl.pallas_call(
        gather_kernel,
        out_shape=[
            jax.ShapeDtypeStruct((PEERS * rows, 2 * HD), jnp.bfloat16),
            jax.ShapeDtypeStruct((PEERS, rows, WIDE), jnp.bfloat16),
        ],
        in_specs=[VMEM] * PEERS,
        out_specs=[VMEM] * 2,
        compiler_params=SMALL,
    )(*pieces)


def join_kernel(*refs):
    pieces, out_ref, sems = refs[:PEERS], refs[PEERS], refs[PEERS + 1]
    _, chip, core = place()
    copies = []
    for step, piece in enumerate(pieces):
        lanes = pl.ds(pl.multiple_of(peer_of(chip, core, step) * WIDE, HD), WIDE)
        copies.append(pltpu.make_async_copy(piece, out_ref.at[:, lanes], sems.at[step]))
        copies[-1].start()
    for copy in copies:
        copy.wait()


def join(pieces):
    return pl.pallas_call(
        join_kernel,
        out_shape=jax.ShapeDtypeStruct((pieces[0].shape[0], HQ * HD), jnp.bfloat16),
        in_specs=[VMEM] * PEERS,
        out_specs=HBM,
        scratch_shapes=[pltpu.SemaphoreType.DMA((PEERS,))],
        compiler_params=SMALL,
    )(*pieces)


def attend_kernel(backs, first, final, table_ref, factor_ref, *refs):
    refs = list(refs)
    q_ref = refs.pop(0)
    if not first:
        del refs[:2]
    slabs = [(refs.pop(0), refs.pop(0)) for _ in backs]
    out_refs = [refs.pop(0) for _ in range(PEERS)] if final else None
    sums_ref, top_ref = refs.pop(0), refs.pop(0)
    _, chip, core = place()
    if first:
        sums_ref[...] = jnp.zeros_like(sums_ref)
        top_ref[...] = jnp.full_like(top_ref, LOW)
    key_ref, value_ref = refs[:2]
    piece = q_ref.shape[1]
    half = slabs[0][0].shape[0] // 2
    group = GROUP // 2
    chains = [(block, g) for block in range(2) for g in range(2)]

    block_rows = half // 2
    index = lax.broadcasted_iota(jnp.int32, (block_rows, HD), 0)
    for slab, back in zip(slabs, backs):
        for x in range(2):
            count = jnp.maximum(table_ref[4 * back + 2 * x], table_ref[4 * back + 2 * x + 1])
            at = x * half
            spare = slab[0][at : at + 16, :HD].astype(jnp.float32)[0:1]
            for side, ref in enumerate(slab):
                owner = core ^ side
                for n in range(2):
                    values = ref[at + n * block_rows : at + (n + 1) * block_rows, :]
                    keys = values[:, :HD].astype(jnp.float32)
                    values = values[:, HD:]
                    ones = jnp.ones_like(values)
                    to = side * block_rows
                    if n:
                        keep = (2 + owner) * block_rows + index < count
                        keys = jnp.where(keep, keys, spare)
                        values = jnp.where(keep, values.astype(jnp.float32), 0.0).astype(jnp.bfloat16)
                        ones = jnp.where(keep, 1.0, 0.0).astype(jnp.bfloat16)
                        to = (2 + owner) * block_rows
                    to = pl.ds(pl.multiple_of(to, block_rows), block_rows)
                    key_ref[x, :, to] = jnp.transpose(keys).astype(jnp.bfloat16)
                    value_ref[x, to, :HD] = values
                    value_ref[x, to, HD:] = ones

        @pl.loop(0, 4)
        def _(turn):
            x = turn >> 1
            side = turn & 1
            count = table_ref[4 * back + turn]

            def visit(width):
                keys = key_ref[x, :, :width]
                values = value_ref[x, :width, :]

                def scores(block, g):
                    rows = []
                    for i in range(group):
                        lanes = slice((g * group + i) * HD, (g * group + i + 1) * HD)
                        rows.append(q_ref[2 * side + block, :, lanes])
                    return jnp.dot(jnp.concatenate(rows, axis=0), keys, preferred_element_type=jnp.float32)

                ready = scores(*chains[0])
                for n, (block, g) in enumerate(chains):
                    s = ready
                    if n + 1 < len(chains):
                        ready = scores(*chains[n + 1])
                    step = s.shape[0] // group
                    s = jnp.concatenate(
                        [
                            s[i * step : (i + 1) * step] * factor_ref[side * GROUP + g * group + i]
                            for i in range(group)
                        ],
                        axis=0,
                    )
                    chain = 2 * block + g
                    old_top = top_ref[side, chain]
                    top = jnp.maximum(old_top, jnp.max(s, axis=1, keepdims=True))
                    weight = jnp.concatenate(
                        [jnp.exp2(s[:, at : at + HD] - top).astype(jnp.bfloat16) for at in range(0, s.shape[1], HD)],
                        axis=1,
                    )
                    sums = jnp.dot(weight, values, preferred_element_type=jnp.float32)
                    shrink = jnp.exp2(old_top - top)
                    sums_ref[side, chain] = sums + sums_ref[side, chain] * jnp.concatenate([shrink, shrink], axis=1)
                    top_ref[side, chain] = top

            most = 3 * block_rows
            pl.when((count > 0) & (count <= most))(lambda: visit(most))
            pl.when(count > most)(lambda: visit(most + block_rows))

    if final:
        done_ref = refs[2]
        for side in range(2):
            for block, g in chains:
                sums = sums_ref[side, 2 * block + g]
                result = (sums[:, :HD] / sums[:, HD:]).astype(jnp.bfloat16)
                for i in range(group):
                    lanes = slice((g * group + i) * HD, (g * group + i + 1) * HD)
                    done_ref[2 * side + block, :, lanes] = result[i * piece : (i + 1) * piece]
        for step, out_ref in enumerate(out_refs):
            out_ref[...] = done_ref[peer_of(chip, core, step)]


def attend(tables, q, state, slabs, backs, final=False):
    first = state is None
    piece = q.shape[1]
    tall = GROUP * piece // 2
    tokens = slabs[0][0].shape[0]
    out_shape = [
        jax.ShapeDtypeStruct((2, 4, tall, 2 * HD), jnp.float32),
        jax.ShapeDtypeStruct((2, 4, tall, HD), jnp.float32),
    ]
    scratch = [pltpu.VMEM((2, HD, tokens), jnp.bfloat16), pltpu.VMEM((2, tokens, 2 * HD), jnp.bfloat16)]
    if final:
        out_shape = [jax.ShapeDtypeStruct(q.shape[1:], jnp.bfloat16)] * PEERS + out_shape
        scratch.append(pltpu.VMEM(q.shape, jnp.bfloat16))
    work = len(backs) * PEERS * tall * tokens
    inputs = [q, *(state or ()), *[a for slab in slabs for a in slab]]
    outs = len(out_shape) - 2
    aliases = {} if first else {3: outs, 4: outs + 1}
    return pl.pallas_call(
        functools.partial(attend_kernel, backs, first, final),
        out_shape=out_shape,
        in_specs=[SMEM] * 2 + [VMEM] * len(inputs),
        out_specs=[VMEM] * len(out_shape),
        scratch_shapes=scratch,
        input_output_aliases=aliases,
        compiler_params=LARGE,
        cost_estimate=pl.CostEstimate(flops=2 * work * HD, bytes_accessed=4 * q.size, transcendentals=work // 2),
    )(*tables, *inputs)


def per_device(spans, ctx, queries, keys, values, temps, levels, ctx_list, counts):
    other_core = [(t, t ^ 1) for t in range(ctx)]
    last = spans // 2 - 1

    def exchange(pieces):
        moved = [pieces[0]]
        for piece, step in zip(pieces[1:], STEPS[1:]):
            pairs = [(f, f ^ (2 * step[f % 2])) for f in range(spans * ctx)]
            moved.append(lax.ppermute(piece, ("span", "ctx"), pairs))
        return moved

    def up(a, steps):
        return lax.ppermute(a, "span", [(s, (s + 2 * steps) % spans) for s in range(spans)])

    def near(a):
        return lax.ppermute(a, "ctx", other_core)

    pieces = begin(keys, values, queries)
    tables = tabulate(spans // 2, levels, temps, jnp.transpose(ctx_list), counts)
    moved, mine, tables = lax.optimization_barrier((exchange(pieces)[1:], hold(pieces[0]), tables))
    own, q = gather([mine, *moved])
    slabs = {0: own, 1: up(own, 1), last: up(own, last)}
    state = attend(tables, q, None, [(own, near(own))], [0])
    slabs, state = lax.optimization_barrier((slabs, state))
    stage = [1, last]
    sides = [(slabs[b], near(slabs[b])) for b in stage]
    for back in range(2, last):
        slab = up(slabs[back - 1], 1)
        state = attend(tables, q, state, sides, stage)
        slabs[back], state = lax.optimization_barrier((slab, state))
        stage = [back]
        sides = [(slabs[back], near(slabs[back]))]
    out = attend(tables, q, state, sides, stage, True)
    return join(exchange(out[:PEERS]))


def solution(mesh):
    return jax.shard_map(
        functools.partial(per_device, mesh.shape["span"], mesh.shape["ctx"]),
        mesh=mesh,
        in_specs=(
            P(("span", "ctx"), None),
            P(("span", "ctx"), None),
            P(("span", "ctx"), None),
            P(),
            P(),
            P(),
            P(),
        ),
        out_specs=P(("span", "ctx"), None),
        check_vma=False,
    )
```

```python
import functools
import math

import jax
import jax.numpy as jnp
from jax import lax
from jax.experimental import pallas as pl
from jax.experimental.pallas import tpu as pltpu
from jax.sharding import PartitionSpec as P

HQ = 24
KVH = 4
HD = 128
GROUP = HQ // KVH
WIDE = GROUP * HD
PEERS = 4
LOW = -1e30
SCALE = math.log2(math.e) / math.sqrt(HD)
SMEM = pl.BlockSpec(memory_space=pltpu.SMEM)
VMEM = pl.BlockSpec(memory_space=pltpu.VMEM)
HBM = pl.BlockSpec(memory_space=pltpu.HBM)
SMALL = pltpu.CompilerParams(vmem_limit_bytes=6 << 20)
LARGE = pltpu.CompilerParams(vmem_limit_bytes=16 << 20)


STEPS = ((0, 0), (3, 3), (2, 1), (1, 2))


def place():
    span, tok = lax.axis_index("span"), lax.axis_index("ctx")
    return span & -2, 2 * (span & 1) + (tok >> 1), tok & 1


def peer_of(chip, core, step):
    even, odd = STEPS[step]
    return chip ^ jnp.where(core == 0, even, odd)


def table_kernel(planes, levels_ref, temps_ref, list_ref, counts_ref, table_ref, factor_ref):
    base, head, _ = place()
    for side in range(2):
        level = levels_ref[base + side]
        for i in range(GROUP):
            factor_ref[side * GROUP + i] = temps_ref[level, head * GROUP + i] * SCALE

        @pl.loop(0, 2 * planes)
        def _(slab):
            ident = base + (slab & 1) - 2 * (slab >> 1)
            found = base + side == ident
            for j in range(list_ref.shape[0]):
                found = found | (list_ref[j, base + side] == ident)
            count = jnp.where(found & (ident >= 0), counts_ref[jnp.maximum(ident, 0)], 0)
            table_ref[2 * slab + side] = count


def tabulate(planes, levels, temps, ctx_list, counts):
    return pl.pallas_call(
        functools.partial(table_kernel, planes),
        out_shape=[jax.ShapeDtypeStruct((4 * planes,), jnp.int32), jax.ShapeDtypeStruct((2 * GROUP,), jnp.float32)],
        in_specs=[SMEM] * 4,
        out_specs=[SMEM] * 2,
        compiler_params=SMALL,
    )(levels, temps, ctx_list, counts)


def begin_kernel(keys_ref, values_ref, q_ref, *refs):
    kv_pieces, q_pieces, (kv, q, sems, out_sems) = refs[:PEERS], refs[PEERS : 2 * PEERS], refs[2 * PEERS :]
    _, chip, core = place()
    steps = [*range(1, PEERS), 0]
    loads = {}
    for i, ref in enumerate((keys_ref, values_ref, q_ref)):
        width = ref.shape[1] // KVH
        for step in steps:
            lanes = pl.ds(pl.multiple_of(peer_of(chip, core, step) * width, HD), width)
            target = q.at[step] if i == 2 else kv.at[step, :, i * HD : (i + 1) * HD]
            loads[step, i] = pltpu.make_async_copy(ref.at[:, lanes], target, sems.at[step, i])
            loads[step, i].start()
    stores = []
    for n, (source, pieces) in enumerate(((kv, kv_pieces), (q, q_pieces))):
        for step in steps:
            for i in (2,) if n else (0, 1):
                loads[step, i].wait()
            stores.append(pltpu.make_async_copy(source.at[step], pieces[step], out_sems.at[step, n]))
            stores[-1].start()
    for store in stores:
        store.wait()


def begin(keys, values, queries):
    rows = keys.shape[0]
    shapes = [(rows, 2 * HD), (rows, WIDE)]
    out = pl.pallas_call(
        begin_kernel,
        out_shape=[jax.ShapeDtypeStruct(shape, jnp.bfloat16) for shape in shapes for _ in range(PEERS)],
        in_specs=[HBM] * 3,
        out_specs=[HBM] * (2 * PEERS),
        scratch_shapes=[pltpu.VMEM((PEERS, *shape), jnp.bfloat16) for shape in shapes]
        + [pltpu.SemaphoreType.DMA((PEERS, 3)), pltpu.SemaphoreType.DMA((PEERS, 2))],
    )(keys, values, queries)
    return out[:PEERS], out[PEERS:]


def hold_kernel(piece_ref, out_ref):
    out_ref[...] = piece_ref[...]


def hold(piece):
    return pl.pallas_call(
        hold_kernel,
        out_shape=jax.ShapeDtypeStruct(piece.shape, piece.dtype),
        in_specs=[VMEM],
        out_specs=VMEM,
        compiler_params=SMALL,
    )(piece)


def gather_kernel(*refs):
    pieces, out_ref = refs[:PEERS], refs[PEERS]
    _, chip, core = place()
    for step, piece in enumerate(pieces):
        out_ref[peer_of(chip, core, step)] = piece[...]


def gather(pieces):
    return pl.pallas_call(
        gather_kernel,
        out_shape=jax.ShapeDtypeStruct((PEERS, *pieces[0].shape), jnp.bfloat16),
        in_specs=[VMEM] * PEERS,
        out_specs=VMEM,
        compiler_params=SMALL,
    )(*pieces)


def join_kernel(*refs):
    pieces, out_ref, sems = refs[:PEERS], refs[PEERS], refs[PEERS + 1]
    _, chip, core = place()
    copies = []
    for step, piece in enumerate(pieces):
        lanes = pl.ds(pl.multiple_of(peer_of(chip, core, step) * WIDE, HD), WIDE)
        copies.append(pltpu.make_async_copy(piece, out_ref.at[:, lanes], sems.at[step]))
        copies[-1].start()
    for copy in copies:
        copy.wait()


def join(pieces):
    return pl.pallas_call(
        join_kernel,
        out_shape=jax.ShapeDtypeStruct((pieces[0].shape[0], HQ * HD), jnp.bfloat16),
        in_specs=[VMEM] * PEERS,
        out_specs=HBM,
        scratch_shapes=[pltpu.SemaphoreType.DMA((PEERS,))],
        compiler_params=SMALL,
    )(*pieces)


def attend_kernel(backs, first, final, table_ref, factor_ref, *refs):
    refs = list(refs)
    q_ref = refs.pop(0)
    if not first:
        del refs[:2]
    slabs = [(refs.pop(0), refs.pop(0)) for _ in backs]
    out_refs = [refs.pop(0) for _ in range(PEERS)] if final else None
    sums_ref, top_ref = refs.pop(0), refs.pop(0)
    _, chip, core = place()
    if first:
        sums_ref[...] = jnp.zeros_like(sums_ref)
        top_ref[...] = jnp.full_like(top_ref, LOW)
    key_ref, value_ref = refs[:2]
    piece = q_ref.shape[1]
    half = slabs[0][0].shape[0] // 2
    group = GROUP // 2
    chains = [(block, g) for block in range(2) for g in range(2)]

    block_rows = half // 2
    index = lax.broadcasted_iota(jnp.int32, (block_rows, HD), 0)
    for slab, back in zip(slabs, backs):
        for x in range(2):
            count = jnp.maximum(table_ref[4 * back + 2 * x], table_ref[4 * back + 2 * x + 1])
            at = x * half
            spare = slab[0][at : at + 16, :HD].astype(jnp.float32)[0:1]
            for side, ref in enumerate(slab):
                owner = core ^ side
                for n in range(2):
                    values = ref[at + n * block_rows : at + (n + 1) * block_rows, :]
                    keys = values[:, :HD].astype(jnp.float32)
                    values = values[:, HD:]
                    ones = jnp.ones_like(values)
                    to = side * block_rows
                    if n:
                        keep = (2 + owner) * block_rows + index < count
                        keys = jnp.where(keep, keys, spare)
                        values = jnp.where(keep, values.astype(jnp.float32), 0.0).astype(jnp.bfloat16)
                        ones = jnp.where(keep, 1.0, 0.0).astype(jnp.bfloat16)
                        to = (2 + owner) * block_rows
                    to = pl.ds(pl.multiple_of(to, block_rows), block_rows)
                    key_ref[x, :, to] = jnp.transpose(keys).astype(jnp.bfloat16)
                    value_ref[x, to, :HD] = values
                    value_ref[x, to, HD:] = ones

        @pl.loop(0, 4)
        def _(turn):
            x = turn >> 1
            side = turn & 1
            count = table_ref[4 * back + turn]

            def visit(width):
                keys = key_ref[x, :, :width]
                values = value_ref[x, :width, :]

                def scores(block, g):
                    rows = []
                    for i in range(group):
                        lanes = slice((g * group + i) * HD, (g * group + i + 1) * HD)
                        rows.append(q_ref[2 * side + block, :, lanes])
                    return jnp.dot(jnp.concatenate(rows, axis=0), keys, preferred_element_type=jnp.float32)

                ready = scores(*chains[0])
                for n, (block, g) in enumerate(chains):
                    s = ready
                    if n + 1 < len(chains):
                        ready = scores(*chains[n + 1])
                    step = s.shape[0] // group
                    s = jnp.concatenate(
                        [
                            s[i * step : (i + 1) * step] * factor_ref[side * GROUP + g * group + i]
                            for i in range(group)
                        ],
                        axis=0,
                    )
                    chain = 2 * block + g
                    old_top = top_ref[side, chain]
                    top = jnp.maximum(old_top, jnp.max(s, axis=1, keepdims=True))
                    weight = jnp.concatenate(
                        [jnp.exp2(s[:, at : at + HD] - top).astype(jnp.bfloat16) for at in range(0, s.shape[1], HD)],
                        axis=1,
                    )
                    sums = jnp.dot(weight, values, preferred_element_type=jnp.float32)
                    shrink = jnp.exp2(old_top - top)
                    sums_ref[side, chain] = sums + sums_ref[side, chain] * jnp.concatenate([shrink, shrink], axis=1)
                    top_ref[side, chain] = top

            most = 3 * block_rows
            pl.when((count > 0) & (count <= most))(lambda: visit(most))
            pl.when(count > most)(lambda: visit(most + block_rows))

    if final:
        done_ref = refs[2]
        for side in range(2):
            for block, g in chains:
                sums = sums_ref[side, 2 * block + g]
                result = (sums[:, :HD] / sums[:, HD:]).astype(jnp.bfloat16)
                for i in range(group):
                    lanes = slice((g * group + i) * HD, (g * group + i + 1) * HD)
                    done_ref[2 * side + block, :, lanes] = result[i * piece : (i + 1) * piece]
        for step, out_ref in enumerate(out_refs):
            out_ref[...] = done_ref[peer_of(chip, core, step)]


def attend(tables, q, state, slabs, backs, final=False):
    first = state is None
    piece = q.shape[1]
    tall = GROUP * piece // 2
    tokens = slabs[0][0].shape[0]
    out_shape = [
        jax.ShapeDtypeStruct((2, 4, tall, 2 * HD), jnp.float32),
        jax.ShapeDtypeStruct((2, 4, tall, HD), jnp.float32),
    ]
    scratch = [pltpu.VMEM((2, HD, tokens), jnp.bfloat16), pltpu.VMEM((2, tokens, 2 * HD), jnp.bfloat16)]
    if final:
        out_shape = [jax.ShapeDtypeStruct(q.shape[1:], jnp.bfloat16)] * PEERS + out_shape
        scratch.append(pltpu.VMEM(q.shape, jnp.bfloat16))
    work = len(backs) * PEERS * tall * tokens
    inputs = [q, *(state or ()), *[a for slab in slabs for a in slab]]
    outs = len(out_shape) - 2
    aliases = {} if first else {3: outs, 4: outs + 1}
    return pl.pallas_call(
        functools.partial(attend_kernel, backs, first, final),
        out_shape=out_shape,
        in_specs=[SMEM] * 2 + [VMEM] * len(inputs),
        out_specs=[VMEM] * len(out_shape),
        scratch_shapes=scratch,
        input_output_aliases=aliases,
        compiler_params=LARGE,
        cost_estimate=pl.CostEstimate(flops=2 * work * HD, bytes_accessed=4 * q.size, transcendentals=work // 2),
    )(*tables, *inputs)


def per_device(spans, ctx, queries, keys, values, temps, levels, ctx_list, counts):
    other_core = [(t, t ^ 1) for t in range(ctx)]
    last = spans // 2 - 1

    def exchange(pieces):
        moved = [pieces[0]]
        for piece, step in zip(pieces[1:], STEPS[1:]):
            pairs = [(f, f ^ (2 * step[f % 2])) for f in range(spans * ctx)]
            moved.append(lax.ppermute(piece, ("span", "ctx"), pairs))
        return moved

    def up(a, steps):
        return lax.ppermute(a, "span", [(s, (s + 2 * steps) % spans) for s in range(spans)])

    def near(a):
        return lax.ppermute(a, "ctx", other_core)

    kv_pieces, q_pieces = begin(keys, values, queries)
    moved, mine = lax.optimization_barrier((exchange(kv_pieces)[1:], hold(kv_pieces[0])))
    own = gather([mine, *moved]).reshape(-1, 2 * HD)
    slabs = {0: own, 1: up(own, 1), last: up(own, last)}
    other, q_pieces = lax.optimization_barrier((near(own), q_pieces))
    tables = tabulate(spans // 2, levels, temps, jnp.transpose(ctx_list), counts)
    slabs, moved, mine, tables = lax.optimization_barrier((slabs, exchange(q_pieces)[1:], hold(q_pieces[0]), tables))
    q = gather([mine, *moved])
    stage = [0, 1, last]
    sides = [(slabs[b], near(slabs[b]) if b else other) for b in stage]
    state = None
    for back in range(2, last):
        slab = up(slabs[back - 1], 1)
        state = attend(tables, q, state, sides, stage)
        slabs[back], state = lax.optimization_barrier((slab, state))
        stage = [back]
        sides = [(slabs[back], near(slabs[back]))]
    out = attend(tables, q, state, sides, stage, True)
    return join(exchange(out[:PEERS]))


def solution(mesh):
    return jax.shard_map(
        functools.partial(per_device, mesh.shape["span"], mesh.shape["ctx"]),
        mesh=mesh,
        in_specs=(
            P(("span", "ctx"), None),
            P(("span", "ctx"), None),
            P(("span", "ctx"), None),
            P(),
            P(),
            P(),
            P(),
        ),
        out_specs=P(("span", "ctx"), None),
        check_vma=False,
    )
```

```python
import functools
import math

import jax
import jax.numpy as jnp
from jax import lax
from jax.experimental import pallas as pl
from jax.experimental.pallas import tpu as pltpu
from jax.sharding import PartitionSpec as P

HQ = 24
KVH = 4
HD = 128
GROUP = HQ // KVH
WIDE = GROUP * HD
PEERS = 4
LOW = -1e30
SCALE = math.log2(math.e) / math.sqrt(HD)
SMEM = pl.BlockSpec(memory_space=pltpu.SMEM)
VMEM = pl.BlockSpec(memory_space=pltpu.VMEM)
HBM = pl.BlockSpec(memory_space=pltpu.HBM)
SMALL = pltpu.CompilerParams(vmem_limit_bytes=6 << 20)
LARGE = pltpu.CompilerParams(vmem_limit_bytes=16 << 20)


STEPS = ((0, 0), (3, 3), (2, 1), (1, 2))


def place():
    span, tok = lax.axis_index("span"), lax.axis_index("ctx")
    return span & -2, 2 * (span & 1) + (tok >> 1), tok & 1


def peer_of(chip, core, step):
    even, odd = STEPS[step]
    return chip ^ jnp.where(core == 0, even, odd)


def table_kernel(planes, levels_ref, temps_ref, list_ref, counts_ref, table_ref, factor_ref):
    base, head, _ = place()
    for side in range(2):
        level = levels_ref[base + side]
        for i in range(GROUP):
            factor_ref[side * GROUP + i] = temps_ref[level, head * GROUP + i] * SCALE

        @pl.loop(0, 2 * planes)
        def _(slab):
            ident = base + (slab & 1) - 2 * (slab >> 1)
            found = base + side == ident
            for j in range(list_ref.shape[0]):
                found = found | (list_ref[j, base + side] == ident)
            count = jnp.where(found & (ident >= 0), counts_ref[jnp.maximum(ident, 0)], 0)
            table_ref[2 * slab + side] = count


def tabulate(planes, levels, temps, ctx_list, counts):
    return pl.pallas_call(
        functools.partial(table_kernel, planes),
        out_shape=[jax.ShapeDtypeStruct((4 * planes,), jnp.int32), jax.ShapeDtypeStruct((2 * GROUP,), jnp.float32)],
        in_specs=[SMEM] * 4,
        out_specs=[SMEM] * 2,
        compiler_params=SMALL,
    )(levels, temps, ctx_list, counts)


def begin_kernel(keys_ref, values_ref, q_ref, *refs):
    kv_pieces, q_pieces, (kv, q, sems, out_sems) = refs[:PEERS], refs[PEERS : 2 * PEERS], refs[2 * PEERS :]
    _, chip, core = place()
    steps = [*range(1, PEERS), 0]
    loads = {}
    for i, ref in enumerate((keys_ref, values_ref, q_ref)):
        width = ref.shape[1] // KVH
        for step in steps:
            lanes = pl.ds(pl.multiple_of(peer_of(chip, core, step) * width, HD), width)
            target = q.at[step] if i == 2 else kv.at[step, :, i * HD : (i + 1) * HD]
            loads[step, i] = pltpu.make_async_copy(ref.at[:, lanes], target, sems.at[step, i])
            loads[step, i].start()
    stores = []
    for n, (source, pieces) in enumerate(((kv, kv_pieces), (q, q_pieces))):
        for step in steps:
            for i in (2,) if n else (0, 1):
                loads[step, i].wait()
            stores.append(pltpu.make_async_copy(source.at[step], pieces[step], out_sems.at[step, n]))
            stores[-1].start()
    for store in stores:
        store.wait()


def begin(keys, values, queries):
    rows = keys.shape[0]
    shapes = [(rows, 2 * HD), (rows, WIDE)]
    out = pl.pallas_call(
        begin_kernel,
        out_shape=[jax.ShapeDtypeStruct(shape, jnp.bfloat16) for shape in shapes for _ in range(PEERS)],
        in_specs=[HBM] * 3,
        out_specs=[HBM] * (2 * PEERS),
        scratch_shapes=[pltpu.VMEM((PEERS, *shape), jnp.bfloat16) for shape in shapes]
        + [pltpu.SemaphoreType.DMA((PEERS, 3)), pltpu.SemaphoreType.DMA((PEERS, 2))],
    )(keys, values, queries)
    return out[:PEERS], out[PEERS:]


def hold_kernel(piece_ref, out_ref):
    out_ref[...] = piece_ref[...]


def hold(piece):
    return pl.pallas_call(
        hold_kernel,
        out_shape=jax.ShapeDtypeStruct(piece.shape, piece.dtype),
        in_specs=[VMEM],
        out_specs=VMEM,
        compiler_params=SMALL,
    )(piece)


def gather_kernel(*refs):
    pieces, out_ref = refs[:PEERS], refs[PEERS]
    _, chip, core = place()
    for step, piece in enumerate(pieces):
        out_ref[peer_of(chip, core, step)] = piece[...]


def gather(pieces):
    return pl.pallas_call(
        gather_kernel,
        out_shape=jax.ShapeDtypeStruct((PEERS, *pieces[0].shape), jnp.bfloat16),
        in_specs=[VMEM] * PEERS,
        out_specs=VMEM,
        compiler_params=SMALL,
    )(*pieces)


def join_kernel(*refs):
    pieces, out_ref, sems = refs[:PEERS], refs[PEERS], refs[PEERS + 1]
    _, chip, core = place()
    copies = []
    for step, piece in enumerate(pieces):
        lanes = pl.ds(pl.multiple_of(peer_of(chip, core, step) * WIDE, HD), WIDE)
        copies.append(pltpu.make_async_copy(piece, out_ref.at[:, lanes], sems.at[step]))
        copies[-1].start()
    for copy in copies:
        copy.wait()


def join(pieces):
    return pl.pallas_call(
        join_kernel,
        out_shape=jax.ShapeDtypeStruct((pieces[0].shape[0], HQ * HD), jnp.bfloat16),
        in_specs=[VMEM] * PEERS,
        out_specs=HBM,
        scratch_shapes=[pltpu.SemaphoreType.DMA((PEERS,))],
        compiler_params=SMALL,
    )(*pieces)


def attend_kernel(backs, first, final, table_ref, factor_ref, *refs):
    refs = list(refs)
    q_ref = refs.pop(0)
    if not first:
        del refs[:2]
    slabs = [(refs.pop(0), refs.pop(0)) for _ in backs]
    out_refs = [refs.pop(0) for _ in range(PEERS)] if final else None
    sums_ref, top_ref = refs.pop(0), refs.pop(0)
    _, chip, core = place()
    if first:
        sums_ref[...] = jnp.zeros_like(sums_ref)
        top_ref[...] = jnp.full_like(top_ref, LOW)
    key_ref, value_ref = refs[:2]
    piece = q_ref.shape[1]
    half = slabs[0][0].shape[0] // 2
    group = GROUP // 2
    chains = [(block, g) for block in range(2) for g in range(2)]

    block_rows = half // 2
    index = lax.broadcasted_iota(jnp.int32, (block_rows, HD), 0)
    def prepare(slab, x, count):
        at = x * half
        spare = slab[0][at : at + 16, :HD].astype(jnp.float32)[0:1]
        for side, ref in enumerate(slab):
            owner = core ^ side
            for n in range(2):
                values = ref[at + n * block_rows : at + (n + 1) * block_rows, :]
                keys = values[:, :HD].astype(jnp.float32)
                values = values[:, HD:]
                ones = jnp.ones_like(values)
                to = side * block_rows
                if n:
                    keep = (2 + owner) * block_rows + index < count
                    keys = jnp.where(keep, keys, spare)
                    values = jnp.where(keep, values.astype(jnp.float32), 0.0).astype(jnp.bfloat16)
                    ones = jnp.where(keep, 1.0, 0.0).astype(jnp.bfloat16)
                    to = (2 + owner) * block_rows
                to = pl.ds(pl.multiple_of(to, block_rows), block_rows)
                key_ref[x, :, to] = jnp.transpose(keys).astype(jnp.bfloat16)
                value_ref[x, to, :HD] = values
                value_ref[x, to, HD:] = ones

    for slab, back in zip(slabs, backs):
        for x in range(2):
            count = jnp.maximum(table_ref[4 * back + 2 * x], table_ref[4 * back + 2 * x + 1])
            pl.when(count > 0)(functools.partial(prepare, slab, x, count))

        @pl.loop(0, 4)
        def _(turn):
            x = turn >> 1
            side = turn & 1
            count = table_ref[4 * back + turn]

            def visit(width):
                keys = key_ref[x, :, :width]
                values = value_ref[x, :width, :]

                def scores(block, g):
                    rows = []
                    for i in range(group):
                        lanes = slice((g * group + i) * HD, (g * group + i + 1) * HD)
                        rows.append(q_ref[2 * side + block, :, lanes])
                    return jnp.dot(jnp.concatenate(rows, axis=0), keys, preferred_element_type=jnp.float32)

                ready = scores(*chains[0])
                for n, (block, g) in enumerate(chains):
                    s = ready
                    if n + 1 < len(chains):
                        ready = scores(*chains[n + 1])
                    step = s.shape[0] // group
                    s = jnp.concatenate(
                        [
                            s[i * step : (i + 1) * step] * factor_ref[side * GROUP + g * group + i]
                            for i in range(group)
                        ],
                        axis=0,
                    )
                    chain = 2 * block + g
                    old_top = top_ref[side, chain]
                    top = jnp.maximum(old_top, jnp.max(s, axis=1, keepdims=True))
                    weight = jnp.concatenate(
                        [jnp.exp2(s[:, at : at + HD] - top).astype(jnp.bfloat16) for at in range(0, s.shape[1], HD)],
                        axis=1,
                    )
                    sums = jnp.dot(weight, values, preferred_element_type=jnp.float32)
                    shrink = jnp.exp2(old_top - top)
                    sums_ref[side, chain] = sums + sums_ref[side, chain] * jnp.concatenate([shrink, shrink], axis=1)
                    top_ref[side, chain] = top

            most = 3 * block_rows
            pl.when((count > 0) & (count <= most))(lambda: visit(most))
            pl.when(count > most)(lambda: visit(most + block_rows))

    if final:
        done_ref = refs[2]
        for side in range(2):
            for block, g in chains:
                sums = sums_ref[side, 2 * block + g]
                result = (sums[:, :HD] / sums[:, HD:]).astype(jnp.bfloat16)
                for i in range(group):
                    lanes = slice((g * group + i) * HD, (g * group + i + 1) * HD)
                    done_ref[2 * side + block, :, lanes] = result[i * piece : (i + 1) * piece]
        for step, out_ref in enumerate(out_refs):
            out_ref[...] = done_ref[peer_of(chip, core, step)]


def attend(tables, q, state, slabs, backs, final=False):
    first = state is None
    piece = q.shape[1]
    tall = GROUP * piece // 2
    tokens = slabs[0][0].shape[0]
    out_shape = [
        jax.ShapeDtypeStruct((2, 4, tall, 2 * HD), jnp.float32),
        jax.ShapeDtypeStruct((2, 4, tall, HD), jnp.float32),
    ]
    scratch = [pltpu.VMEM((2, HD, tokens), jnp.bfloat16), pltpu.VMEM((2, tokens, 2 * HD), jnp.bfloat16)]
    if final:
        out_shape = [jax.ShapeDtypeStruct(q.shape[1:], jnp.bfloat16)] * PEERS + out_shape
        scratch.append(pltpu.VMEM(q.shape, jnp.bfloat16))
    work = len(backs) * PEERS * tall * tokens
    inputs = [q, *(state or ()), *[a for slab in slabs for a in slab]]
    outs = len(out_shape) - 2
    aliases = {} if first else {3: outs, 4: outs + 1}
    return pl.pallas_call(
        functools.partial(attend_kernel, backs, first, final),
        out_shape=out_shape,
        in_specs=[SMEM] * 2 + [VMEM] * len(inputs),
        out_specs=[VMEM] * len(out_shape),
        scratch_shapes=scratch,
        input_output_aliases=aliases,
        compiler_params=LARGE,
        cost_estimate=pl.CostEstimate(flops=2 * work * HD, bytes_accessed=4 * q.size, transcendentals=work // 2),
    )(*tables, *inputs)


def per_device(spans, ctx, queries, keys, values, temps, levels, ctx_list, counts):
    other_core = [(t, t ^ 1) for t in range(ctx)]
    last = spans // 2 - 1

    def exchange(pieces):
        moved = [pieces[0]]
        for piece, step in zip(pieces[1:], STEPS[1:]):
            pairs = [(f, f ^ (2 * step[f % 2])) for f in range(spans * ctx)]
            moved.append(lax.ppermute(piece, ("span", "ctx"), pairs))
        return moved

    def up(a, steps):
        return lax.ppermute(a, "span", [(s, (s + 2 * steps) % spans) for s in range(spans)])

    def near(a):
        return lax.ppermute(a, "ctx", other_core)

    kv_pieces, q_pieces = begin(keys, values, queries)
    moved, mine = lax.optimization_barrier((exchange(kv_pieces)[1:], hold(kv_pieces[0])))
    own = gather([mine, *moved]).reshape(-1, 2 * HD)
    slabs = {0: own, 1: up(own, 1), last: up(own, last)}
    other, q_pieces = lax.optimization_barrier((near(own), q_pieces))
    tables = tabulate(spans // 2, levels, temps, jnp.transpose(ctx_list), counts)
    slabs, moved, mine, tables = lax.optimization_barrier((slabs, exchange(q_pieces)[1:], hold(q_pieces[0]), tables))
    q = gather([mine, *moved])
    stage = [0, 1]
    sides = [(own, other), (slabs[1], near(slabs[1]))]
    farthest = [(slabs[last], near(slabs[last]))]
    state = None
    for back in range(2, last):
        slab = up(slabs[back - 1], 1)
        state = attend(tables, q, state, sides, stage)
        slabs[back], state = lax.optimization_barrier((slab, state))
        other = near(slabs[back])
        if back == 2:
            state = attend(tables, q, state, farthest, [last])
            other, state = lax.optimization_barrier((other, state))
        stage = [back]
        sides = [(slabs[back], other)]
    out = attend(tables, q, state, sides, stage, True)
    return join(exchange(out[:PEERS]))


def solution(mesh):
    return jax.shard_map(
        functools.partial(per_device, mesh.shape["span"], mesh.shape["ctx"]),
        mesh=mesh,
        in_specs=(
            P(("span", "ctx"), None),
            P(("span", "ctx"), None),
            P(("span", "ctx"), None),
            P(),
            P(),
            P(),
            P(),
        ),
        out_specs=P(("span", "ctx"), None),
        check_vma=False,
    )
```

```python
import functools
import math

import jax
import jax.numpy as jnp
from jax import lax
from jax.experimental import pallas as pl
from jax.experimental.pallas import tpu as pltpu
from jax.sharding import PartitionSpec as P

HQ = 24
KVH = 4
HD = 128
GROUP = HQ // KVH
WIDE = GROUP * HD
PEERS = 4
LOW = -1e30
SCALE = math.log2(math.e) / math.sqrt(HD)
SMEM = pl.BlockSpec(memory_space=pltpu.SMEM)
VMEM = pl.BlockSpec(memory_space=pltpu.VMEM)
HBM = pl.BlockSpec(memory_space=pltpu.HBM)
SMALL = pltpu.CompilerParams(vmem_limit_bytes=6 << 20)
LARGE = pltpu.CompilerParams(vmem_limit_bytes=16 << 20)


STEPS = ((0, 0), (3, 1), (1, 2), (2, 3))


def place():
    span, tok = lax.axis_index("span"), lax.axis_index("ctx")
    return span & -2, 2 * (span & 1) + (tok >> 1), tok & 1


def peer_of(chip, core, step):
    even, odd = STEPS[step]
    return chip ^ jnp.where(core == 0, even, odd)


def table_kernel(planes, levels_ref, temps_ref, list_ref, counts_ref, table_ref, factor_ref):
    base, head, _ = place()
    for side in range(2):
        level = levels_ref[base + side]
        for i in range(GROUP):
            factor_ref[side * GROUP + i] = temps_ref[level, head * GROUP + i] * SCALE

        @pl.loop(0, 2 * planes)
        def _(slab):
            ident = base + (slab & 1) - 2 * (slab >> 1)
            found = base + side == ident
            for j in range(list_ref.shape[0]):
                found = found | (list_ref[j, base + side] == ident)
            count = jnp.where(found & (ident >= 0), counts_ref[jnp.maximum(ident, 0)], 0)
            table_ref[2 * slab + side] = count


def tabulate(planes, levels, temps, ctx_list, counts):
    return pl.pallas_call(
        functools.partial(table_kernel, planes),
        out_shape=[jax.ShapeDtypeStruct((4 * planes,), jnp.int32), jax.ShapeDtypeStruct((2 * GROUP,), jnp.float32)],
        in_specs=[SMEM] * 4,
        out_specs=[SMEM] * 2,
        compiler_params=SMALL,
    )(levels, temps, ctx_list, counts)


def begin_kernel(keys_ref, values_ref, q_ref, *refs):
    kv_pieces, q_pieces, (kv, q, sems, out_sems) = refs[:PEERS], refs[PEERS : 2 * PEERS], refs[2 * PEERS :]
    _, chip, core = place()
    steps = [*range(1, PEERS), 0]
    loads = {}
    for i, ref in enumerate((keys_ref, values_ref, q_ref)):
        width = ref.shape[1] // KVH
        for step in steps:
            lanes = pl.ds(pl.multiple_of(peer_of(chip, core, step) * width, HD), width)
            target = q.at[step] if i == 2 else kv.at[step, :, i * HD : (i + 1) * HD]
            loads[step, i] = pltpu.make_async_copy(ref.at[:, lanes], target, sems.at[step, i])
            loads[step, i].start()
    stores = []
    for n, (source, pieces) in enumerate(((kv, kv_pieces), (q, q_pieces))):
        for step in steps:
            for i in (2,) if n else (0, 1):
                loads[step, i].wait()
            stores.append(pltpu.make_async_copy(source.at[step], pieces[step], out_sems.at[step, n]))
            stores[-1].start()
    for store in stores:
        store.wait()


def begin(keys, values, queries):
    rows = keys.shape[0]
    shapes = [(rows, 2 * HD), (rows, WIDE)]
    out = pl.pallas_call(
        begin_kernel,
        out_shape=[jax.ShapeDtypeStruct(shape, jnp.bfloat16) for shape in shapes for _ in range(PEERS)],
        in_specs=[HBM] * 3,
        out_specs=[HBM] * (2 * PEERS),
        scratch_shapes=[pltpu.VMEM((PEERS, *shape), jnp.bfloat16) for shape in shapes]
        + [pltpu.SemaphoreType.DMA((PEERS, 3)), pltpu.SemaphoreType.DMA((PEERS, 2))],
    )(keys, values, queries)
    return out[:PEERS], out[PEERS:]


def hold_kernel(piece_ref, out_ref):
    out_ref[...] = piece_ref[...]


def hold(piece):
    return pl.pallas_call(
        hold_kernel,
        out_shape=jax.ShapeDtypeStruct(piece.shape, piece.dtype),
        in_specs=[VMEM],
        out_specs=VMEM,
        compiler_params=SMALL,
    )(piece)


def gather_kernel(*refs):
    pieces, out_ref = refs[:PEERS], refs[PEERS]
    _, chip, core = place()
    for step, piece in enumerate(pieces):
        out_ref[peer_of(chip, core, step)] = piece[...]


def gather(pieces):
    return pl.pallas_call(
        gather_kernel,
        out_shape=jax.ShapeDtypeStruct((PEERS, *pieces[0].shape), jnp.bfloat16),
        in_specs=[VMEM] * PEERS,
        out_specs=VMEM,
        compiler_params=SMALL,
    )(*pieces)


def join_kernel(*refs):
    pieces, out_ref, sems = refs[:PEERS], refs[PEERS], refs[PEERS + 1]
    _, chip, core = place()
    copies = []
    for step, piece in enumerate(pieces):
        lanes = pl.ds(pl.multiple_of(peer_of(chip, core, step) * WIDE, HD), WIDE)
        copies.append(pltpu.make_async_copy(piece, out_ref.at[:, lanes], sems.at[step]))
        copies[-1].start()
    for copy in copies:
        copy.wait()


def join(pieces):
    return pl.pallas_call(
        join_kernel,
        out_shape=jax.ShapeDtypeStruct((pieces[0].shape[0], HQ * HD), jnp.bfloat16),
        in_specs=[VMEM] * PEERS,
        out_specs=HBM,
        scratch_shapes=[pltpu.SemaphoreType.DMA((PEERS,))],
        compiler_params=SMALL,
    )(*pieces)


def attend_kernel(backs, first, final, table_ref, factor_ref, *refs):
    refs = list(refs)
    q_ref = refs.pop(0)
    if not first:
        del refs[:2]
    slabs = [(refs.pop(0), refs.pop(0)) for _ in backs]
    out_refs = [refs.pop(0) for _ in range(PEERS)] if final else None
    sums_ref, top_ref = refs.pop(0), refs.pop(0)
    _, chip, core = place()
    if first:
        sums_ref[...] = jnp.zeros_like(sums_ref)
        top_ref[...] = jnp.full_like(top_ref, LOW)
    key_ref, value_ref = refs[:2]
    piece = q_ref.shape[1]
    half = slabs[0][0].shape[0] // 2
    group = GROUP // 2
    chains = [(block, g) for block in range(2) for g in range(2)]

    block_rows = half // 2
    index = lax.broadcasted_iota(jnp.int32, (block_rows, HD), 0)
    for slab, back in zip(slabs, backs):
        for x in range(2):
            count = jnp.maximum(table_ref[4 * back + 2 * x], table_ref[4 * back + 2 * x + 1])
            at = x * half
            spare = slab[0][at : at + 16, :HD].astype(jnp.float32)[0:1]
            for side, ref in enumerate(slab):
                owner = core ^ side
                for n in range(2):
                    values = ref[at + n * block_rows : at + (n + 1) * block_rows, :]
                    keys = values[:, :HD].astype(jnp.float32)
                    values = values[:, HD:]
                    ones = jnp.ones_like(values)
                    to = side * block_rows
                    if n:
                        keep = (2 + owner) * block_rows + index < count
                        keys = jnp.where(keep, keys, spare)
                        values = jnp.where(keep, values.astype(jnp.float32), 0.0).astype(jnp.bfloat16)
                        ones = jnp.where(keep, 1.0, 0.0).astype(jnp.bfloat16)
                        to = (2 + owner) * block_rows
                    to = pl.ds(pl.multiple_of(to, block_rows), block_rows)
                    key_ref[x, :, to] = jnp.transpose(keys).astype(jnp.bfloat16)
                    value_ref[x, to, :HD] = values
                    value_ref[x, to, HD:] = ones

        @pl.loop(0, 4)
        def _(turn):
            x = turn >> 1
            side = turn & 1
            count = table_ref[4 * back + turn]

            def visit(width):
                keys = key_ref[x, :, :width]
                values = value_ref[x, :width, :]

                def scores(block, g):
                    rows = []
                    for i in range(group):
                        lanes = slice((g * group + i) * HD, (g * group + i + 1) * HD)
                        rows.append(q_ref[2 * side + block, :, lanes])
                    return jnp.dot(jnp.concatenate(rows, axis=0), keys, preferred_element_type=jnp.float32)

                ready = scores(*chains[0])
                for n, (block, g) in enumerate(chains):
                    s = ready
                    if n + 1 < len(chains):
                        ready = scores(*chains[n + 1])
                    step = s.shape[0] // group
                    s = jnp.concatenate(
                        [
                            s[i * step : (i + 1) * step] * factor_ref[side * GROUP + g * group + i]
                            for i in range(group)
                        ],
                        axis=0,
                    )
                    chain = 2 * block + g
                    old_top = top_ref[side, chain]
                    top = jnp.maximum(old_top, jnp.max(s, axis=1, keepdims=True))
                    weight = jnp.concatenate(
                        [jnp.exp2(s[:, at : at + HD] - top).astype(jnp.bfloat16) for at in range(0, s.shape[1], HD)],
                        axis=1,
                    )
                    sums = jnp.dot(weight, values, preferred_element_type=jnp.float32)
                    shrink = jnp.exp2(old_top - top)
                    sums_ref[side, chain] = sums + sums_ref[side, chain] * jnp.concatenate([shrink, shrink], axis=1)
                    top_ref[side, chain] = top

            most = 3 * block_rows
            pl.when((count > 0) & (count <= most))(lambda: visit(most))
            pl.when(count > most)(lambda: visit(most + block_rows))

    if final:
        done_ref = refs[2]
        for side in range(2):
            for block, g in chains:
                sums = sums_ref[side, 2 * block + g]
                result = (sums[:, :HD] / sums[:, HD:]).astype(jnp.bfloat16)
                for i in range(group):
                    lanes = slice((g * group + i) * HD, (g * group + i + 1) * HD)
                    done_ref[2 * side + block, :, lanes] = result[i * piece : (i + 1) * piece]
        for step, out_ref in enumerate(out_refs):
            out_ref[...] = done_ref[peer_of(chip, core, step)]


def attend(tables, q, state, slabs, backs, final=False):
    first = state is None
    piece = q.shape[1]
    tall = GROUP * piece // 2
    tokens = slabs[0][0].shape[0]
    out_shape = [
        jax.ShapeDtypeStruct((2, 4, tall, 2 * HD), jnp.float32),
        jax.ShapeDtypeStruct((2, 4, tall, HD), jnp.float32),
    ]
    scratch = [pltpu.VMEM((2, HD, tokens), jnp.bfloat16), pltpu.VMEM((2, tokens, 2 * HD), jnp.bfloat16)]
    if final:
        out_shape = [jax.ShapeDtypeStruct(q.shape[1:], jnp.bfloat16)] * PEERS + out_shape
        scratch.append(pltpu.VMEM(q.shape, jnp.bfloat16))
    work = len(backs) * PEERS * tall * tokens
    inputs = [q, *(state or ()), *[a for slab in slabs for a in slab]]
    outs = len(out_shape) - 2
    aliases = {} if first else {3: outs, 4: outs + 1}
    return pl.pallas_call(
        functools.partial(attend_kernel, backs, first, final),
        out_shape=out_shape,
        in_specs=[SMEM] * 2 + [VMEM] * len(inputs),
        out_specs=[VMEM] * len(out_shape),
        scratch_shapes=scratch,
        input_output_aliases=aliases,
        compiler_params=LARGE,
        cost_estimate=pl.CostEstimate(flops=2 * work * HD, bytes_accessed=4 * q.size, transcendentals=work // 2),
    )(*tables, *inputs)


def per_device(spans, ctx, queries, keys, values, temps, levels, ctx_list, counts):
    other_core = [(t, t ^ 1) for t in range(ctx)]
    last = spans // 2 - 1

    def exchange(pieces):
        moved = [pieces[0]]
        for piece, step in zip(pieces[1:], STEPS[1:]):
            pairs = [(f, f ^ (2 * step[f % 2])) for f in range(spans * ctx)]
            moved.append(lax.ppermute(piece, ("span", "ctx"), pairs))
        return moved

    def up(a, steps):
        return lax.ppermute(a, "span", [(s, (s + 2 * steps) % spans) for s in range(spans)])

    def near(a):
        return lax.ppermute(a, "ctx", other_core)

    kv_pieces, q_pieces = begin(keys, values, queries)
    moved, mine = lax.optimization_barrier((exchange(kv_pieces)[1:], hold(kv_pieces[0])))
    own = gather([mine, *moved]).reshape(-1, 2 * HD)
    slabs = {0: own, 1: up(own, 1), last: up(own, last)}
    other, q_pieces = lax.optimization_barrier((near(own), q_pieces))
    tables = tabulate(spans // 2, levels, temps, jnp.transpose(ctx_list), counts)
    slabs, moved, mine, tables = lax.optimization_barrier((slabs, exchange(q_pieces)[1:], hold(q_pieces[0]), tables))
    q = gather([mine, *moved])
    stage = [0, 1, last]
    sides = [(slabs[b], near(slabs[b]) if b else other) for b in stage]
    state = None
    for back in range(2, last):
        slab = up(slabs[back - 1], 1)
        state = attend(tables, q, state, sides, stage)
        slabs[back], state = lax.optimization_barrier((slab, state))
        stage = [back]
        sides = [(slabs[back], near(slabs[back]))]
    out = attend(tables, q, state, sides, stage, True)
    return join(exchange(out[:PEERS]))


def solution(mesh):
    return jax.shard_map(
        functools.partial(per_device, mesh.shape["span"], mesh.shape["ctx"]),
        mesh=mesh,
        in_specs=(
            P(("span", "ctx"), None),
            P(("span", "ctx"), None),
            P(("span", "ctx"), None),
            P(),
            P(),
            P(),
            P(),
        ),
        out_specs=P(("span", "ctx"), None),
        check_vma=False,
    )
```
